512 devices in a mesh: cut: 32 (over z, y_lo), depth: 16 (over x, y_hi, core).
Axes of the slice: x: 4, y: 4 (y_hi: 2, y_lo: 2; y = y_hi * 2 + y_lo), z: 16, core: 2. Of those that a mesh axis runs over, the one named last changes fastest.
Arguments:
- positions: float32 [2, 64, 128, 128], P(None, 'cut', 'depth'), may hold values from 0 to 128, as said below
- velocity: float32 [2, 64, 128, 128], P(None, 'cut', 'depth'), may hold values from -3 to 3
- density: float32 [64, 128, 128], P('cut', 'depth'), may hold values from 0.9 to 1.1
- counts: int32 [64, 128], P('cut', 'depth'), may hold values from 16 to 128, as said below
- contact_mask: int32 [64, 128], P('cut', 'depth'), may hold values 0 or 1
- destination: int32 [32], replicated, may hold values from 0 to 31, each once
- tool: float32 [2], replicated, may hold values from -0.5 to 0.5
Outputs:
- particles: float32 [5, 64, 128, 128], P(None, 'cut', 'depth')
- tool_state: float32 [2], replicated
The draws below stay inside these ranges and needn't reach their ends.
Inputs may be any that keep to these rules, and one draw needn't show every extreme that they name: `counts`: cell (0, 0) holds 128 live particles. `positions`: each particle lies inside its own cell: coordinates of cell (i, j) lie in [i, i+1) x [j, j+1).
All inputs are finite; a program needn't handle non-finite values. No bound on the sum of `contact_mask` on one device may be relied on, other than what follows from the above.
Results may differ from the reference program's by a relative error of at most 0.0003.
Values sent between devices are 32-bit elements; how exact they have to be, the bound alone decides.
No kernel may reach another device: no remote copies, remote signals or barrier semaphores. Data moves between devices by JAX's collectives and lax.ppermute only.
A program may use at most 64 MiB of HBM per device.

```python
import jax
import jax.numpy as jnp
from jax import lax

CX = 2
P_SIZE = 128
STEPS = 4
NX = 64
NY = 128
N_CUT = 32


def draw_positions(key, part):
    key = jax.random.fold_in(key, 11)
    frac = jax.random.uniform(key, (2, NX, NY, P_SIZE), jnp.float32, 0.0, 0.999)
    col = jnp.broadcast_to(jnp.arange(NX).astype(jnp.float32)[:, None, None], (NX, NY, P_SIZE))
    row = jnp.broadcast_to(jnp.arange(NY).astype(jnp.float32)[None, :, None], (NX, NY, P_SIZE))
    return jnp.stack([col, row]) + frac


def draw_counts(key, part):
    key = jax.random.fold_in(key, 23)
    filled = jax.random.randint(key, (NX, NY), P_SIZE // 8, P_SIZE + 1)
    return filled.at[0, 0].set(P_SIZE).astype(jnp.int32)


def plant(entries, stream_key, low, high):
    spot = [jax.random.randint(jax.random.fold_in(stream_key, axis), (), 0, length) for axis, length in enumerate(entries.shape)]
    longest = entries.shape.index(max(entries.shape))
    beside = spot[:longest] + [(spot[longest] + 1) % entries.shape[longest]] + spot[longest + 1:]
    return entries.at[tuple(spot)].set(low).at[tuple(beside)].set(high)


def levels(stream_key, dims, shards, low, high):
    def one(axis_at, blocks):
        draws = jax.random.uniform(jax.random.fold_in(jax.random.fold_in(stream_key, 6), axis_at), (blocks,), jnp.float32, low / len(shards), high / len(shards))
        return jnp.repeat(jnp.exp(draws), dims[axis_at] // blocks).reshape((-1,) + (1,) * (len(dims) - axis_at - 1))

    loudness = one(*shards[0])
    for cut in shards[1:]:
        loudness = loudness * one(*cut)
    return loudness


def normal_values(rng, dims, scale, most, cuts=(), held_as=jnp.bfloat16):
    gain = levels(rng, dims, cuts, -0.22, 0.18) if cuts else 1.0
    array = jax.random.normal(rng, dims, jnp.float32) * scale * gain
    return jnp.minimum(jnp.maximum(array, -most), most).astype(held_as)


def setup_inputs(seed: int = 0) -> dict:
    key_of = jax.random.split(jax.random.key(seed), 8)
    return {
        "positions": draw_positions(jax.random.fold_in(key_of[7], 71), 0),
        "velocity": normal_values(key_of[1], (2, NX, NY, P_SIZE), 0.5, 3.0, ((1, 32), (2, 16)), jnp.float32),
        "density": jnp.clip(0.9 + 0.20000005 * jax.random.uniform(key_of[2], (NX, NY, P_SIZE), jnp.float32) ** levels(key_of[2], (NX, NY, P_SIZE), ((0, 32), (1, 16)), -0.2, 0.2), 0.9, 1.1),
        "counts": draw_counts(jax.random.fold_in(key_of[7], 71), 0),
        "contact_mask": plant((jax.random.randint(key_of[4], (NX, NY), 0, 3) < 1).astype(jnp.int32), jax.random.fold_in(key_of[4], 1), 0, 1),
        "destination": jax.random.permutation(key_of[5], N_CUT).astype(jnp.int32),
        "tool": jnp.clip(jax.random.uniform(key_of[6], (2,), jnp.float32, -0.5, 0.5), -0.5, 0.5),
    }


MASS = 0.02
SOUND = 20.0
VISCOSITY = 2.0
STIFF = 50.0
DT = 0.05


def cell_rates(ext):
    rows = ext.shape[1] - 2
    cols = ext.shape[2] - 2
    mid = ext[:, 1:rows + 1, 1:cols + 1]
    xi = mid[0][..., :, None]
    yi = mid[1][..., :, None]
    ui = mid[2][..., :, None]
    vi = mid[3][..., :, None]
    rho_i = jnp.where(mid[5] > 0, mid[4], 1.0)[..., :, None]
    press_i = SOUND * (rho_i - 1.0) / (rho_i * rho_i)
    acc_x = jnp.zeros(mid[0].shape, ext.dtype)
    acc_y = jnp.zeros(mid[0].shape, ext.dtype)
    drho = jnp.zeros(mid[0].shape, ext.dtype)
    for a in range(3):
        for b in range(3):
            nbr = ext[:, a:a + rows, b:b + cols]
            dx = xi - nbr[0][..., None, :]
            dy = yi - nbr[1][..., None, :]
            q = jnp.maximum(0.0, 1.0 - dx * dx - dy * dy)
            live_j = nbr[5][..., None, :]
            rho_j = jnp.where(nbr[5] > 0, nbr[4], 1.0)[..., None, :]
            press_j = SOUND * (rho_j - 1.0) / (rho_j * rho_j)
            grad = -6.0 * q * q * live_j
            coef = MASS * (press_i + press_j) * grad
            du = ui - nbr[2][..., None, :]
            dv = vi - nbr[3][..., None, :]
            visc = VISCOSITY * MASS * q * q * q * live_j / rho_j
            acc_x = acc_x + jnp.sum(-coef * dx - visc * du, -1)
            acc_y = acc_y + jnp.sum(-coef * dy - visc * dv, -1)
            drho = drho + jnp.sum(MASS * grad * (du * dx + dv * dy), -1)
    return jnp.stack([acc_x, acc_y, drho])


def contact(region, offset, first_col):
    cells = first_col + jnp.arange(region.shape[1]).astype(region.dtype)
    local = region[0] - cells[:, None, None]
    return region[6] * region[5] * jnp.maximum(0.0, local + offset - 0.5)


def update(region, rates, pen):
    live = region[5]
    u = region[2] + DT * live * (rates[0] - STIFF * pen)
    v = region[3] + DT * live * rates[1]
    x = region[0] + DT * live * u
    y = region[1] + DT * live * v
    rho = region[4] + DT * live * rates[2]
    return jnp.stack([x, y, u, v, rho, live, region[6]])


def tool_step(tool, force, slots):
    speed = tool[1] + DT * (1.0 - force / slots)
    return jnp.stack([tool[0] + DT * speed, speed])


def reference(positions, velocity, density, counts, contact_mask, destination, tool):
    dtype = positions.dtype
    slot = jnp.arange(P_SIZE).astype(jnp.int32)
    live = (slot[None, None, :] < counts[:, :, None]).astype(dtype)
    touch = jnp.broadcast_to(contact_mask[:, :, None].astype(dtype), live.shape)
    state = jnp.concatenate([positions, velocity, density[None], live[None], touch[None]], 0)
    slots = NX * NY * P_SIZE * 1.0
    for step in range(STEPS):
        ext = jnp.pad(state, ((0, 0), (1, 1), (1, 1), (0, 0)))

        def one_row(index):
            return cell_rates(lax.dynamic_slice_in_dim(ext, index, 3, 1))[:, 0]

        rates = jnp.moveaxis(lax.map(one_row, jnp.arange(NX).astype(jnp.int32)), 0, 1)
        pen = contact(state, tool[0], 0.0)
        force = jnp.sum(STIFF * pen)
        state = update(state, rates, pen)
        tool = tool_step(tool, force, slots)
    blocks = state[:5].reshape(5, N_CUT, CX, NY, P_SIZE)
    moved = jnp.zeros_like(blocks).at[:, destination].set(blocks)
    return moved.reshape(5, NX, NY, P_SIZE), tool
```

```python
import functools

import jax
import jax.numpy as jnp
from jax import lax
from jax.experimental import pallas as pl
from jax.experimental.pallas import tpu as pltpu
from jax.sharding import PartitionSpec as P

STEPS = 4
MASS = 0.02
SOUND = 20.0
VISCOSITY = 2.0
STIFF = 50.0
DT = 0.05

F32 = jnp.float32
BF16 = jnp.bfloat16
PARAMS = pltpu.CompilerParams(vmem_limit_bytes=40 * 1024 * 1024)
VMEM = pl.BlockSpec(memory_space=pltpu.VMEM)
SMEM = pl.BlockSpec(memory_space=pltpu.SMEM)


def shape(*dims):
    return jax.ShapeDtypeStruct(dims, F32)


def pressure(rho, live):
    s = jnp.where(live > 0, rho, 1.0)
    inv = 1.0 / s
    return SOUND * (s - 1.0) * inv * inv, inv


def rates_kernel(origin, own, left, right, top, bottom, out, ext, feat, xcol, ycol, acc):
    cols, rows, slots = own.shape[1:]
    wide, tall = cols + 2, rows + 2
    x0, y0 = origin[0], origin[1]
    for f in range(6):
        ext[f, 0, 1 : rows + 1] = left[f]
        ext[f, wide - 1, 1 : rows + 1] = right[f]
        for c in range(cols):
            ext[f, c + 1, 1 : rows + 1] = own[f, c]
        for c in range(wide):
            ext[f, c, 0:1] = top[f, c : c + 1]
            ext[f, c, tall - 1 : tall] = bottom[f, c : c + 1]
    for c in range(wide):
        x, y = ext[0, c] - x0, ext[1, c] - y0
        u, v, live = ext[2, c], ext[3, c], ext[5, c]
        press, inv = pressure(ext[4, c], live)
        lp, li = live * press, live * inv
        parts = [live, live * x, live * y, lp, lp * x, lp * y, live * u, live * v, live * (u * x + v * y), li, li * u, li * v]
        for k, part in enumerate(parts):
            high = part.astype(BF16).astype(F32)
            feat[c, :, k, :] = high
            feat[c, :, 16 + k, :] = part - high
        for k in (12, 13, 14, 15, 28, 29, 30, 31):
            feat[c, :, k, :] = jnp.zeros((tall, slots), F32)

    def spread(i, carry):
        c = lax.div(i, tall)
        r = i - c * tall
        xcol[c, r] = jnp.broadcast_to(ext[0, c, pl.ds(r, 1), :], (slots, slots)).T
        ycol[c, r] = jnp.broadcast_to(ext[1, c, pl.ds(r, 1), :], (slots, slots)).T
        return carry

    lax.fori_loop(0, wide * tall, spread, 0, unroll=4)

    def one_cell(i, carry):
        c = lax.div(i, rows)
        r = i - c * rows
        xi = jnp.broadcast_to(ext[0, c + 1, pl.ds(r + 1, 1), :], (slots, slots))
        yi = jnp.broadcast_to(ext[1, c + 1, pl.ds(r + 1, 1), :], (slots, slots))

        def weights(a, b):
            dx = xi - xcol[c + a, r + b]
            dy = yi - ycol[c + a, r + b]
            q = jnp.maximum(0.0, 1.0 - dx * dx - dy * dy)
            q2 = q * q
            return jnp.concatenate([q2, q2 * q], axis=1).astype(BF16)

        around = [(a, b) for a in range(3) for b in range(3)]
        total = None
        for n in range(0, 9, 2):
            pair = around[n : n + 2]
            w = jnp.concatenate([weights(a, b) for a, b in pair], axis=0)
            f = jnp.concatenate([feat[c + a, r + b] for a, b in pair], axis=1).astype(BF16)
            found = jnp.dot(f, w, preferred_element_type=F32)
            total = found if total is None else total + found
        acc[i] = total
        return carry

    lax.fori_loop(0, cols * rows, one_cell, 0, unroll=2)

    for c in range(cols):

        def summed(k):
            lanes = slice(0, slots) if k < 9 else slice(slots, 2 * slots)
            return acc[rows * c : rows * (c + 1), k, lanes] + acc[rows * c : rows * (c + 1), 16 + k, lanes]

        x, y = own[0, c] - x0, own[1, c] - y0
        u, v = own[2, c], own[3, c]
        press, _ = pressure(own[4, c], own[5, c])
        a0, ax, ay, ap, apx, apy, au, av, aw, b0, bu, bv = [summed(k) for k in range(12)]
        sx, sy = x * a0 - ax, y * a0 - ay
        out[0, c] = (6.0 * MASS) * (press * sx + x * ap - apx) - (VISCOSITY * MASS) * (u * b0 - bu)
        out[1, c] = (6.0 * MASS) * (press * sy + y * ap - apy) - (VISCOSITY * MASS) * (v * b0 - bv)
        out[2, c] = (-6.0 * MASS) * (u * sx + v * sy - x * au - y * av + aw)


def rates(origin, own, left, right, top, bottom):
    cols, rows, slots = own.shape[1:]
    wide, tall = cols + 2, rows + 2
    return pl.pallas_call(
        rates_kernel,
        out_shape=shape(3, cols, rows, slots),
        in_specs=[SMEM] + [VMEM] * 5,
        out_specs=VMEM,
        scratch_shapes=[
            pltpu.VMEM((6, wide, tall, slots), F32),
            pltpu.VMEM((wide, tall, 32, slots), F32),
            pltpu.VMEM((wide, tall, slots, slots), F32),
            pltpu.VMEM((wide, tall, slots, slots), F32),
            pltpu.VMEM((cols * rows, 32, 2 * slots), F32),
        ],
        compiler_params=PARAMS,
    )(origin, own, left, right, top, bottom)


def rims_kernel(before, own, after, first_rim, last_rim):
    cols, rows = own.shape[1:3]
    for f in range(6):
        for rim, r in ((first_rim, 0), (last_rim, rows - 1)):
            rim[f, 0:1] = before[f, r : r + 1]
            for c in range(cols):
                rim[f, c + 1 : c + 2] = own[f, c, r : r + 1]
            rim[f, cols + 1 : cols + 2] = after[f, r : r + 1]


def rims(before, own, after):
    cols, _, slots = own.shape[1:]
    return pl.pallas_call(
        rims_kernel,
        out_shape=[shape(6, cols + 2, slots)] * 2,
        in_specs=[VMEM] * 3,
        out_specs=[VMEM] * 2,
        compiler_params=PARAMS,
    )(before, own, after)


def penalties(x, touch, live, offset, first, c):
    return touch * live * jnp.maximum(0.0, x - (first + c) + offset - 0.5)


def send_force(x, touch, live, offset, first, force):
    cols = len(x)
    total = sum(STIFF * penalties(x[c], touch[c], live[c], offset, first, c) for c in range(cols))
    total = jnp.sum(jnp.sum(total, axis=0, keepdims=True), axis=1, keepdims=True)
    force[...] = jnp.broadcast_to(total[None], force.shape)


def start_kernel(origin, positions, velocity, density, marks, tool, own, left, right, force):
    cols = positions.shape[1]
    first = origin[2]
    fields = [positions[0], positions[1], velocity[0], velocity[1], density[...], marks[0]]
    for f, field in enumerate(fields):
        own[f] = field
        left[f] = field[0]
        right[f] = field[cols - 1]
    each = range(cols)
    send_force([positions[0, c] for c in each], [marks[1, c] for c in each], [marks[0, c] for c in each], tool[0:1], first, force)


def start(origin, positions, velocity, density, marks, tool, ncut):
    cols, rows, slots = density.shape
    return pl.pallas_call(
        start_kernel,
        out_shape=[shape(6, cols, rows, slots), shape(6, rows, slots), shape(6, rows, slots), shape(ncut, 1, slots)],
        in_specs=[SMEM] + [VMEM] * 5,
        out_specs=[VMEM] * 4,
        compiler_params=PARAMS,
    )(origin, positions, velocity, density, marks, tool)


def advance(total, tool, scale):
    force = jnp.sum(total[...], axis=0)
    speed = tool[1:2] + DT * (1.0 - force * scale)
    return tool[0:1] + DT * speed, speed


def moved_state(origin, own, found, marks, offset):
    cols = own.shape[1]
    first = origin[2]
    new = []
    for c in range(cols):
        live = own[5, c]
        pen = penalties(own[0, c], marks[1, c], live, offset, first, c)
        u = own[2, c] + DT * live * (found[0, c] - STIFF * pen)
        v = own[3, c] + DT * live * found[1, c]
        x = own[0, c] + DT * live * u
        y = own[1, c] + DT * live * v
        rho = own[4, c] + DT * live * found[2, c]
        new.append([x, y, u, v, rho, live])
    return new


def update_kernel(scale, origin, own, found, marks, total, tool, new_own, left, right, force, new_tool):
    cols = own.shape[1]
    new = moved_state(origin, own, found, marks, tool[0:1])
    for f in range(6):
        for c in range(cols):
            new_own[f, c] = new[c][f]
        left[f] = new[0][f]
        right[f] = new[cols - 1][f]
    offset, speed = advance(total, tool, scale)
    new_tool[0:1] = offset
    new_tool[1:2] = speed
    each = range(cols)
    send_force([new[c][0] for c in each], [marks[1, c] for c in each], [new[c][5] for c in each], offset, origin[2], force)


def update(origin, own, found, marks, total, tool, ncut, scale):
    cols, rows, slots = own.shape[1:]
    return pl.pallas_call(
        functools.partial(update_kernel, scale),
        out_shape=[
            shape(6, cols, rows, slots),
            shape(6, rows, slots),
            shape(6, rows, slots),
            shape(ncut, 1, slots),
            shape(2, slots),
        ],
        in_specs=[SMEM] + [VMEM] * 5,
        out_specs=[VMEM] * 5,
        compiler_params=PARAMS,
    )(origin, own, found, marks, total, tool)


def last_kernel(near, origin, place, own, found, marks, tool, sent):
    cols = own.shape[1]
    new = moved_state(origin, own, found, marks, tool[0:1])
    target = lax.rem(place[0], near)
    for k in range(near):
        for f in range(5):
            for c in range(cols):
                sent[k, f, c] = jnp.where(target == k, new[c][f], 0.0)


def last(origin, place, own, found, marks, tool, near):
    cols, rows, slots = own.shape[1:]
    return pl.pallas_call(
        functools.partial(last_kernel, near),
        out_shape=shape(near, 5, cols, rows, slots),
        in_specs=[SMEM, SMEM] + [VMEM] * 4,
        out_specs=VMEM,
        compiler_params=PARAMS,
    )(origin, place, own, found, marks, tool)


def sort_kernel(near, far, place, got, sent):
    sent[...] = jnp.zeros(sent.shape, F32)
    mine = place[1]
    for k in range(near):
        target = place[2 + k]
        wanted = lax.rem(target, near) == mine

        @pl.when(wanted)
        def _():
            sent[lax.div(target, near)] = got[k]


def sort(place, got, near, far):
    return pl.pallas_call(
        functools.partial(sort_kernel, near, far),
        out_shape=shape(far, *got.shape[1:]),
        in_specs=[SMEM, VMEM],
        out_specs=VMEM,
        compiler_params=PARAMS,
    )(place, got)


def take_kernel(place, got, out):
    out[...] = got[place[0]]


def take(place, got):
    return pl.pallas_call(
        take_kernel,
        out_shape=shape(*got.shape[1:]),
        in_specs=[SMEM, VMEM],
        out_specs=VMEM,
        compiler_params=PARAMS,
    )(place, got)


def exchange(up, down, axis):
    size = lax.axis_size(axis)
    forth = [(i, i + 1) for i in range(size - 1)]
    back = [(i + 1, i) for i in range(size - 1)]
    return lax.ppermute(up, axis, forth), lax.ppermute(down, axis, back)


def body(positions, velocity, density, counts, contact_mask, destination, tool):
    cols, rows, slots = density.shape
    ncut, ndepth = lax.axis_size("cut"), lax.axis_size("depth")
    here, depth = lax.axis_index("cut"), lax.axis_index("depth")
    scale = 1.0 / (ncut * cols * ndepth * rows * slots)
    first_col = (here * cols).astype(F32)
    first_row = (depth * rows).astype(F32)
    origin = jnp.stack([first_col + 0.5 * cols, first_row + 0.5 * rows, first_col])
    live = (jnp.arange(slots)[None, None, :] < counts[:, :, None]).astype(F32)
    touch = jnp.broadcast_to(contact_mask[:, :, None].astype(F32), live.shape)
    marks = jnp.stack([live, touch])
    tool = jnp.broadcast_to(tool[:, None], (2, slots))

    near = 8 if ncut % 8 == 0 else 1
    far = ncut // near
    group, digit = here // near, here % near
    from_group = lax.dynamic_slice_in_dim(destination, group * near, near)
    place = jnp.concatenate([destination[here][None], digit[None], from_group])
    source = jnp.sum(jnp.where(destination == here, jnp.arange(ncut), 0))
    source = (source // near)[None]

    own, left, right, force = start(origin, positions, velocity, density, marks, tool, ncut)
    for step in range(STEPS):
        before, after = exchange(right, left, "cut")
        got = lax.all_to_all(force, "cut", 0, 0, tiled=True)
        first_rim, last_rim = rims(before, own, after)
        top, bottom = exchange(last_rim, first_rim, "depth")
        got = jnp.broadcast_to(jnp.sum(got, axis=0, keepdims=True), (ndepth, 1, slots))
        total = lax.all_to_all(got, "depth", 0, 0, tiled=True)
        found = rates(origin, own, before, after, top, bottom)
        if step < STEPS - 1:
            own, left, right, force, tool = update(origin, own, found, marks, total, tool, ncut, scale)
        else:
            sent = last(origin, place, own, found, marks, tool, near)
            force = jnp.sum(total[:, 0, 0])
            speed = tool[1, 0] + DT * (1.0 - force * scale)
            tool = jnp.stack([tool[0, 0] + DT * speed, speed])
    close = [[g * near + k for k in range(near)] for g in range(far)]
    apart = [[g * near + k for g in range(far)] for k in range(near)]
    got = lax.all_to_all(sent, "cut", 0, 0, tiled=True, axis_index_groups=close)
    sent = sort(place, got, near, far)
    got = lax.all_to_all(sent, "cut", 0, 0, tiled=True, axis_index_groups=apart)
    return take(source, got), tool


def solution(mesh):
    return jax.shard_map(
        body,
        mesh=mesh,
        in_specs=(
            P(None, "cut", "depth", None),
            P(None, "cut", "depth", None),
            P("cut", "depth", None),
            P("cut", "depth"),
            P("cut", "depth"),
            P(),
            P(),
        ),
        out_specs=(P(None, "cut", "depth", None), P()),
        check_vma=False,
    )
```

```python
import functools

import jax
import jax.numpy as jnp
from jax import lax
from jax.experimental import pallas as pl
from jax.experimental.pallas import tpu as pltpu
from jax.sharding import PartitionSpec as P

STEPS = 4
MASS = 0.02
SOUND = 20.0
VISCOSITY = 2.0
STIFF = 50.0
DT = 0.05

FAR = 1.0e6

F32 = jnp.float32
BF16 = jnp.bfloat16
PARAMS = pltpu.CompilerParams(vmem_limit_bytes=40 * 1024 * 1024)
VMEM = pl.BlockSpec(memory_space=pltpu.VMEM)
SMEM = pl.BlockSpec(memory_space=pltpu.SMEM)


def shape(*dims):
    return jax.ShapeDtypeStruct(dims, F32)


def call(kernel, outs, scalars, arrays, scratch=(), estimate=0):
    return pl.pallas_call(
        kernel,
        out_shape=outs,
        in_specs=[SMEM] * len(scalars) + [VMEM] * len(arrays),
        out_specs=[VMEM] * len(outs) if isinstance(outs, list) else VMEM,
        scratch_shapes=scratch,
        compiler_params=PARAMS,
        cost_estimate=pl.CostEstimate(flops=estimate, bytes_accessed=1 << 20, transcendentals=0) if estimate else None,
    )(*scalars, *arrays)


def pressure(s):
    inv = 1.0 / s
    return SOUND * (s - 1.0) * inv * inv, inv


def penalties(x, touch, live, offset, column):
    return touch * live * jnp.maximum(0.0, x - column + offset - 0.5)


def own_force(new, marks, offset, first):
    total = 0.0
    for c, fields in enumerate(new):
        total = total + STIFF * penalties(fields[0], marks[1, c], marks[0, c], offset, first + c)
    total = jnp.sum(total, axis=0, keepdims=True)
    return jnp.broadcast_to(jnp.sum(total, axis=1, keepdims=True), total.shape)


def visible(fields, live):
    alive = live > 0
    x, y, u, v, rho = fields
    return [jnp.where(alive, x, FAR), y, u, v, jnp.where(alive, rho, 1.0)]


def fill_depth(place, new, marks, force, sent):
    depth, ndepth = place[1], sent.shape[0]
    cols, rows = marks.shape[1:3]
    sent[...] = jnp.zeros(sent.shape, F32)
    sent[:, 5 * cols : 5 * cols + 1, :] = jnp.broadcast_to(force[None], (ndepth, 1, force.shape[1]))
    seen = [visible(new[c], marks[0, c]) for c in range(cols)]

    @pl.when(depth > 0)
    def _():
        for c in range(cols):
            for f in range(5):
                sent[depth - 1, f * cols + c : f * cols + c + 1] = seen[c][f][0:1]

    @pl.when(depth < ndepth - 1)
    def _():
        for c in range(cols):
            for f in range(5):
                sent[depth + 1, f * cols + c : f * cols + c + 1] = seen[c][f][rows - 1 : rows]


def start_kernel(place, origin, positions, velocity, density, marks, tool, sent):
    cols = positions.shape[1]
    new = [[positions[0, c], positions[1, c], velocity[0, c], velocity[1, c], density[c]] for c in range(cols)]
    fill_depth(place, new, marks, own_force(new, marks, tool[0:1], origin[2]), sent)


def extend_kernel(place, own, marks, got, left, right, force):
    depth, ndepth = place[1], got.shape[0]
    cols, rows = own.shape[1:3]
    above = got[jnp.maximum(depth - 1, 0)]
    below = got[jnp.minimum(depth + 1, ndepth - 1)]
    blank = [FAR, 0.0, 0.0, 0.0, 1.0]
    for c, column in ((0, left), (cols - 1, right)):
        seen = visible([own[f, c] for f in range(5)], marks[0, c])
        for f in range(5):
            k = f * cols + c
            column[f, 0:1] = jnp.where(depth > 0, above[k : k + 1], blank[f])
            column[f, 1 : rows + 1] = seen[f]
            column[f, rows + 1 : rows + 2] = jnp.where(depth < ndepth - 1, below[k : k + 1], blank[f])
    total = jnp.sum(got[:, 5 * cols : 5 * cols + 1, :], axis=0)
    force[...] = jnp.broadcast_to(total[None], force.shape)


def rates_kernel(place, origin, before, left, right, after, out, feat, acc2, acc3):
    ncut = place[2]
    tall, slots = left.shape[1:]
    rows = tall - 2
    x0, y0 = origin[0], origin[1]
    columns = []
    for c, ref in enumerate((before, left, right, after)):
        x, y, u, v, s = [ref[f] for f in range(5)]
        if c in (0, 3):
            outside = place[0] == (0 if c == 0 else ncut - 1)
            x = jnp.where(outside, FAR, x)
            s = jnp.where(outside, 1.0, s)
        columns.append((x, y))
        lx, ly = x - x0, y - y0
        press, inv = pressure(s)
        parts = [jnp.ones_like(x), lx, ly, press, press * lx, press * ly, u, v, u * lx + v * ly, inv, inv * u, inv * v]
        for k in range(16):
            high = parts[k].astype(BF16).astype(F32) if k < 12 else jnp.zeros_like(x)
            feat[pl.ds(c * tall * 32 + k, tall, stride=32), :] = high
            feat[pl.ds(c * tall * 32 + 16 + k, tall, stride=32), :] = parts[k] - high if k < 12 else high
    around = [(a, b) for a in range(3) for b in range(3)]
    for i in range(2 * rows):
        c, r = divmod(i, rows)
        xi, yi = [jnp.broadcast_to(f[r + 1 : r + 2], (slots, slots)).T for f in columns[c + 1]]

        def weights(a, b):
            dx = (xi - columns[c + a][0][r + b : r + b + 1]).astype(BF16)
            dy = (yi - columns[c + a][1][r + b : r + b + 1]).astype(BF16)
            q = jnp.maximum(BF16(0.0), BF16(1.0) - dx * dx - dy * dy)
            q2 = q * q
            return jnp.concatenate([q2, q2 * q], axis=0)

        total = None
        for n in range(0, 9, 2):
            pair = around[n : n + 2]
            w = jnp.concatenate([weights(a, b) for a, b in pair], axis=1)
            f = jnp.concatenate([feat[pl.ds(((c + a) * tall + r + b) * 32, 32), :] for a, b in pair], axis=1).astype(BF16)
            found = lax.dot_general(f, w, (((1,), (1,)), ((), ())), preferred_element_type=F32)
            total = found if total is None else total + found
        acc2[i * 32 : (i + 1) * 32] = total[:, :slots]
        acc3[i * 32 : (i + 1) * 32] = total[:, slots:]

    for c, ref in enumerate((left, right)):

        def summed(k):
            acc = acc2 if k < 9 else acc3
            return sum(acc[pl.ds(c * rows * 32 + k + low, rows, stride=32), :] for low in (0, 16))

        x, y, u, v, s = [ref[f, 1 : rows + 1] for f in range(5)]
        x, y = x - x0, y - y0
        press, _ = pressure(s)
        a0, ax, ay, ap, apx, apy, au, av, aw, b0, bu, bv = [summed(k) for k in range(12)]
        sx, sy = x * a0 - ax, y * a0 - ay
        out[0, c] = (6.0 * MASS) * (press * sx + x * ap - apx) - (VISCOSITY * MASS) * (u * b0 - bu)
        out[1, c] = (6.0 * MASS) * (press * sy + y * ap - apy) - (VISCOSITY * MASS) * (v * b0 - bv)
        out[2, c] = (-6.0 * MASS) * (u * sx + v * sy - x * au - y * av + aw)


def moved_state(own, found, marks, offset, first):
    new = []
    for c in range(own.shape[1]):
        live = marks[0, c]
        pen = penalties(own[0, c], marks[1, c], live, offset, first + c)
        u = own[2, c] + DT * live * (found[0, c] - STIFF * pen)
        v = own[3, c] + DT * live * found[1, c]
        x = own[0, c] + DT * live * u
        y = own[1, c] + DT * live * v
        rho = own[4, c] + DT * live * found[2, c]
        new.append([x, y, u, v, rho])
    return new


def tool_step(tool, force, scale):
    speed = tool[1:2] + DT * (1.0 - force * scale)
    return tool[0:1] + DT * speed, speed


def update_kernel(scale, place, origin, own, found, marks, total, tool, new_own, new_tool, sent):
    new = moved_state(own, found, marks, tool[0:1], origin[2])
    for c, fields in enumerate(new):
        for f in range(5):
            new_own[f, c] = fields[f]
    offset, speed = tool_step(tool, jnp.sum(total[...], axis=0), scale)
    new_tool[0:1] = offset
    new_tool[1:2] = speed
    fill_depth(place, new, marks, own_force(new, marks, offset, origin[2]), sent)


def last_kernel(near, place, destination, origin, own, found, marks, tool, force, sent):
    cols, rows, slots = own.shape[1:]
    size = 5 * cols * rows
    new = moved_state(own, found, marks, tool[0:1], origin[2])
    sent[...] = jnp.zeros(sent.shape, F32)
    sent[:, size:, :] = jnp.broadcast_to(force[0:1], (near, sent.shape[1] - size, slots))
    digit = lax.rem(destination[place[0]], near)
    for f in range(5):
        for c in range(cols):
            at = (f * cols + c) * rows
            sent[digit, at : at + rows] = new[c][f]


def sort_kernel(near, size, place, destination, got, sent):
    far, most, slots = sent.shape
    group, digit = lax.div(place[0], near), lax.rem(place[0], near)
    sent[...] = jnp.zeros(sent.shape, F32)
    total = jnp.sum(got[:, size : size + 1, :], axis=0, keepdims=True)
    sent[:, size:, :] = jnp.broadcast_to(total, (far, most - size, slots))
    for k in range(near):
        target = destination[group * near + k]

        @pl.when(lax.rem(target, near) == digit)
        def _():
            sent[lax.div(target, near), 0:size] = got[k, 0:size]


def take_kernel(near, scale, place, destination, got, tool, out, new_tool):
    cols, rows, slots = out.shape[1:]
    size = 5 * cols * rows
    source = 0
    for k in range(got.shape[0] * near):
        source = jnp.where(destination[k] == place[0], k // near, source)
    for f in range(5):
        for c in range(cols):
            at = (f * cols + c) * rows
            out[f, c] = got[source, at : at + rows]
    offset, speed = tool_step(tool, jnp.sum(got[:, size : size + 1, :], axis=0), scale)
    new_tool[0:1] = offset
    new_tool[1:2] = speed


def body(positions, velocity, density, counts, contact_mask, destination, tool):
    cols, rows, slots = density.shape
    ncut, ndepth = lax.axis_size("cut"), lax.axis_size("depth")
    here, depth = lax.axis_index("cut"), lax.axis_index("depth")
    scale = 1.0 / (ncut * cols * ndepth * rows * slots)
    place = jnp.stack([here, depth, jnp.int32(ncut)]).astype(jnp.int32)
    first_col = (here * cols).astype(F32)
    first_row = (depth * rows).astype(F32)
    origin = jnp.stack([first_col + 0.5 * cols, first_row + 0.5 * rows, first_col])
    live = (jnp.arange(slots)[None, None, :] < counts[:, :, None]).astype(F32)
    touch = jnp.broadcast_to(contact_mask[:, :, None].astype(F32), live.shape)
    marks = jnp.stack([live, touch])
    tool = jnp.broadcast_to(tool[:, None], (2, slots))
    own = jnp.concatenate([positions, velocity, density[None]], axis=0)
    near = 8 if ncut % 8 == 0 else 1
    far = ncut // near
    size = 5 * cols * rows
    tall = rows + 2
    message = shape(ndepth, 16, slots)
    forth = [(i, i + 1) for i in range(ncut - 1)]
    back = [(i + 1, i) for i in range(ncut - 1)]

    sent = call(start_kernel, message, (place, origin), (positions, velocity, density, marks, tool))
    for step in range(STEPS):
        got = lax.all_to_all(sent, "depth", 0, 0, tiled=True)
        outs = [shape(5, tall, slots), shape(5, tall, slots), shape(ncut, 1, slots)]
        left, right, force = call(extend_kernel, outs, (place,), (own, marks, got))
        before = lax.ppermute(right, "cut", forth)
        after = lax.ppermute(left, "cut", back)
        if step < STEPS - 1:
            total = lax.all_to_all(force, "cut", 0, 0, tiled=True)
        scratch = [pltpu.VMEM((4 * tall * 32, slots), F32)] + [pltpu.VMEM((cols * rows * 32, slots), F32)] * 2
        found = call(rates_kernel, shape(3, cols, rows, slots), (place, origin), (before, left, right, after), scratch, 1 << 27)
        if step < STEPS - 1:
            outs = [shape(5, cols, rows, slots), shape(2, slots), message]
            kernel = functools.partial(update_kernel, scale)
            own, tool, sent = call(kernel, outs, (place, origin), (own, found, marks, total, tool))
    kernel = functools.partial(last_kernel, near)
    sent = call(kernel, shape(near, size + 8, slots), (place, destination, origin), (own, found, marks, tool, force[:, 0]))
    close = [[g * near + k for k in range(near)] for g in range(far)]
    apart = [[g * near + k for g in range(far)] for k in range(near)]
    got = lax.all_to_all(sent, "cut", 0, 0, tiled=True, axis_index_groups=close)
    sent = call(functools.partial(sort_kernel, near, size), shape(far, size + 8, slots), (place, destination), (got,))
    got = lax.all_to_all(sent, "cut", 0, 0, tiled=True, axis_index_groups=apart)
    outs = [shape(5, cols, rows, slots), shape(2, slots)]
    moved, tool = call(functools.partial(take_kernel, near, scale), outs, (place, destination), (got, tool))
    return moved, tool[:, 0]


def solution(mesh):
    return jax.shard_map(
        body,
        mesh=mesh,
        in_specs=(
            P(None, "cut", "depth", None),
            P(None, "cut", "depth", None),
            P("cut", "depth", None),
            P("cut", "depth"),
            P("cut", "depth"),
            P(),
            P(),
        ),
        out_specs=(P(None, "cut", "depth", None), P()),
        check_vma=False,
    )
```

```python
import functools

import jax
import jax.numpy as jnp
from jax import lax
from jax.experimental import pallas as pl
from jax.experimental.pallas import tpu as pltpu
from jax.sharding import PartitionSpec as P

STEPS = 4
MASS = 0.02
SOUND = 20.0
VISCOSITY = 2.0
STIFF = 50.0
DT = 0.05

FAR = 1.0e6

COST = 20_000_000_000

F32 = jnp.float32
BF16 = jnp.bfloat16
PARAMS = pltpu.CompilerParams(vmem_limit_bytes=40 * 1024 * 1024)
VMEM = pl.BlockSpec(memory_space=pltpu.VMEM)
SMEM = pl.BlockSpec(memory_space=pltpu.SMEM)


def shape(*dims):
    return jax.ShapeDtypeStruct(dims, F32)


def call(kernel, outs, scalars, arrays, scratch=(), estimate=0):
    return pl.pallas_call(
        kernel,
        out_shape=outs,
        in_specs=[SMEM] * len(scalars) + [VMEM] * len(arrays),
        out_specs=[VMEM] * len(outs) if isinstance(outs, list) else VMEM,
        scratch_shapes=scratch,
        compiler_params=PARAMS,
        cost_estimate=pl.CostEstimate(flops=estimate, bytes_accessed=1 << 20, transcendentals=0) if estimate else None,
    )(*scalars, *arrays)


def pressure(s):
    inv = 1.0 / s
    return SOUND * (s - 1.0) * inv * inv, inv


def penalties(x, touch, live, offset, column):
    return touch * live * jnp.maximum(0.0, x - column + offset - 0.5)


def own_force(new, marks, offset, first):
    total = 0.0
    for c, fields in enumerate(new):
        total = total + STIFF * penalties(fields[0], marks[1, c], marks[0, c], offset, first + c)
    total = jnp.sum(total, axis=0, keepdims=True)
    return jnp.broadcast_to(jnp.sum(total, axis=1, keepdims=True), total.shape)


def visible(fields, live):
    alive = live > 0
    x, y, u, v, rho = fields
    return [jnp.where(alive, x, FAR), y, u, v, jnp.where(alive, rho, 1.0)]


def fill_depth(place, new, marks, force, sent):
    depth, ndepth = place[1], sent.shape[0]
    cols, rows = marks.shape[1:3]
    sent[...] = jnp.zeros(sent.shape, F32)
    sent[:, 5 * cols : 5 * cols + 1, :] = jnp.broadcast_to(force[None], (ndepth, 1, force.shape[1]))
    seen = [visible(new[c], marks[0, c]) for c in range(cols)]

    @pl.when(depth > 0)
    def _():
        for c in range(cols):
            for f in range(5):
                sent[depth - 1, f * cols + c : f * cols + c + 1] = seen[c][f][0:1]

    @pl.when(depth < ndepth - 1)
    def _():
        for c in range(cols):
            for f in range(5):
                sent[depth + 1, f * cols + c : f * cols + c + 1] = seen[c][f][rows - 1 : rows]


def origin(place, cols, rows):
    first = (place[0] * cols).astype(F32)
    return first + 0.5 * cols, (place[1] * rows).astype(F32) + 0.5 * rows, first


def start_kernel(place, counts, contact, first_tool, positions, velocity, density, own, marks, tool, sent):
    cols, rows, slots = density.shape
    row = lax.broadcasted_iota(jnp.int32, (rows, slots), 0)
    slot = lax.broadcasted_iota(jnp.int32, (rows, slots), 1)
    new = []
    for c in range(cols):
        filled = jnp.zeros((rows, slots), jnp.int32)
        touch = jnp.zeros((rows, slots), jnp.int32)
        for r in range(rows):
            filled = jnp.where(row == r, counts[c, r], filled)
            touch = jnp.where(row == r, contact[c, r], touch)
        marks[0, c] = jnp.where(slot < filled, 1.0, 0.0)
        marks[1, c] = touch.astype(F32)
        new.append([positions[0, c], positions[1, c], velocity[0, c], velocity[1, c], density[c]])
        for f in range(5):
            own[f, c] = new[c][f]
    offset = jnp.zeros((1, slots), F32) + first_tool[0]
    tool[0:1] = offset
    tool[1:2] = jnp.zeros((1, slots), F32) + first_tool[1]
    fill_depth(place, new, marks, own_force(new, marks, offset, origin(place, cols, rows)[2]), sent)


def extend_kernel(place, own, marks, got, *refs):
    left, right, force = refs[-3:]
    depth, ndepth = place[1], got.shape[0]
    cols, rows = own.shape[1:3]
    above = got[jnp.maximum(depth - 1, 0)]
    below = got[jnp.minimum(depth + 1, ndepth - 1)]
    blank = [FAR, 0.0, 0.0, 0.0, 1.0]
    for c, column in ((0, left), (cols - 1, right)):
        seen = visible([own[f, c] for f in range(5)], marks[0, c])
        for f in range(5):
            k = f * cols + c
            column[f, 0:1] = jnp.where(depth > 0, above[k : k + 1], blank[f])
            column[f, 1 : rows + 1] = seen[f]
            column[f, rows + 1 : rows + 2] = jnp.where(depth < ndepth - 1, below[k : k + 1], blank[f])
    total = jnp.sum(got[:, 5 * cols : 5 * cols + 1, :], axis=0)
    force[...] = jnp.broadcast_to(total[None], force.shape)


def pair_sums(columns, center, pairs, out, feat, acc2, acc3, earlier=None):
    x0, y0, _ = center
    tall, slots = columns[0][0].shape
    rows = len(pairs) // 2
    margin = (tall - rows) // 2
    for c, (x, y, u, v, s) in enumerate(columns):
        lx, ly = x - x0, y - y0
        press, inv = pressure(s)
        parts = [jnp.ones_like(x), lx, ly, press, press * lx, press * ly, u, v, u * lx + v * ly, inv, inv * u, inv * v]
        for k in range(16):
            high = parts[k].astype(BF16).astype(F32) if k < 12 else jnp.zeros_like(x)
            feat[pl.ds(c * tall * 32 + k, tall, stride=32), :] = high
            feat[pl.ds(c * tall * 32 + 16 + k, tall, stride=32), :] = parts[k] - high if k < 12 else high
    for i, ((c, r), around) in enumerate(pairs.items()):
        xi, yi = [jnp.broadcast_to(f[r : r + 1], (slots, slots)).T for f in columns[c][:2]]

        def weights(a, b):
            dx = (xi - columns[a][0][b : b + 1]).astype(BF16)
            dy = (yi - columns[a][1][b : b + 1]).astype(BF16)
            q = jnp.maximum(BF16(0.0), BF16(1.0) - dx * dx - dy * dy)
            q2 = q * q
            return jnp.concatenate([q2, q2 * q], axis=0)

        total = None
        for n in range(0, len(around), 2):
            pair = around[n : n + 2]
            w = jnp.concatenate([weights(a, b) for a, b in pair], axis=1)
            f = jnp.concatenate([feat[pl.ds((a * tall + b) * 32, 32), :] for a, b in pair], axis=1).astype(BF16)
            found = lax.dot_general(f, w, (((1,), (1,)), ((), ())), preferred_element_type=F32)
            total = found if total is None else total + found
        acc2[i * 32 : (i + 1) * 32] = total[:, :slots]
        acc3[i * 32 : (i + 1) * 32] = total[:, slots:]

    for n, c in enumerate(sorted({c for c, _ in pairs})):

        def summed(k):
            acc = acc2 if k < 9 else acc3
            return sum(acc[pl.ds(n * rows * 32 + k + low, rows, stride=32), :] for low in (0, 16))

        x, y, u, v, s = [f[margin : margin + rows] for f in columns[c]]
        x, y = x - x0, y - y0
        press, _ = pressure(s)
        a0, ax, ay, ap, apx, apy, au, av, aw, b0, bu, bv = [summed(k) for k in range(12)]
        sx, sy = x * a0 - ax, y * a0 - ay
        rates = [
            (6.0 * MASS) * (press * sx + x * ap - apx) - (VISCOSITY * MASS) * (u * b0 - bu),
            (6.0 * MASS) * (press * sy + y * ap - apy) - (VISCOSITY * MASS) * (v * b0 - bv),
            (-6.0 * MASS) * (u * sx + v * sy - x * au - y * av + aw),
        ]
        for f in range(3):
            out[f, n] = rates[f] if earlier is None else rates[f] + earlier[f, n]


def around_cell(c, r):
    return [(c + a, r + b) for a in (-1, 0, 1) for b in (-1, 0, 1)]


def inner_kernel(place, own, marks, out, feat, acc2, acc3):
    cols, rows = own.shape[1:3]
    columns = [visible([own[f, c] for f in range(5)], marks[0, c]) for c in range(cols)]
    cells = [(c, r) for c in range(cols) for r in range(rows)]
    pairs = {cell: [j for j in around_cell(*cell) if j in cells] for cell in cells}
    pair_sums(columns, origin(place, cols, rows), pairs, out, feat, acc2, acc3)


def outer_kernel(place, before, left, right, after, earlier, out, feat, acc2, acc3):
    cols, rows = earlier.shape[1:3]
    columns = []
    for c, ref in enumerate((before, left, right, after)):
        fields = [ref[f] for f in range(5)]
        if c in (0, 3):
            outside = place[0] == (0 if c == 0 else place[2] - 1)
            fields[0] = jnp.where(outside, FAR, fields[0])
            fields[4] = jnp.where(outside, 1.0, fields[4])
        columns.append(fields)
    cells = [(c + 1, r + 1) for c in range(cols) for r in range(rows)]
    pairs = {cell: [j for j in around_cell(*cell) if j not in cells] for cell in cells}
    pair_sums(columns, origin(place, cols, rows), pairs, out, feat, acc2, acc3, earlier)


def moved_state(own, found, marks, offset, first):
    new = []
    for c in range(own.shape[1]):
        live = marks[0, c]
        pen = penalties(own[0, c], marks[1, c], live, offset, first + c)
        u = own[2, c] + DT * live * (found[0, c] - STIFF * pen)
        v = own[3, c] + DT * live * found[1, c]
        x = own[0, c] + DT * live * u
        y = own[1, c] + DT * live * v
        rho = own[4, c] + DT * live * found[2, c]
        new.append([x, y, u, v, rho])
    return new


def tool_step(tool, force, scale):
    speed = tool[1:2] + DT * (1.0 - force * scale)
    return tool[0:1] + DT * speed, speed


def update_kernel(scale, place, own, found, marks, total, tool, new_own, new_tool, sent):
    first = origin(place, *own.shape[1:3])[2]
    new = moved_state(own, found, marks, tool[0:1], first)
    for c, fields in enumerate(new):
        for f in range(5):
            new_own[f, c] = fields[f]
    offset, speed = tool_step(tool, jnp.sum(total[...], axis=0), scale)
    new_tool[0:1] = offset
    new_tool[1:2] = speed
    fill_depth(place, new, marks, own_force(new, marks, offset, first), sent)


def last_kernel(near, place, own, found, marks, tool, force, sent):
    cols, rows, slots = own.shape[1:]
    size = 5 * cols * rows
    new = moved_state(own, found, marks, tool[0:1], origin(place, cols, rows)[2])
    sent[...] = jnp.zeros(sent.shape, F32)
    sent[:, size:, :] = jnp.broadcast_to(force[0:1], (near, sent.shape[1] - size, slots))
    digit = lax.rem(place[3 + place[0]], near)
    for f in range(5):
        for c in range(cols):
            at = (f * cols + c) * rows
            sent[digit, at : at + rows] = new[c][f]


def sort_kernel(near, size, place, got, sent):
    far, most, slots = sent.shape
    group, digit = lax.div(place[0], near), lax.rem(place[0], near)
    sent[...] = jnp.zeros(sent.shape, F32)
    total = jnp.sum(got[:, size : size + 1, :], axis=0, keepdims=True)
    sent[:, size:, :] = jnp.broadcast_to(total, (far, most - size, slots))
    for k in range(near):
        target = place[3 + group * near + k]

        @pl.when(lax.rem(target, near) == digit)
        def _():
            sent[lax.div(target, near), 0:size] = got[k, 0:size]


def take_kernel(near, scale, place, got, tool, out, new_tool):
    cols, rows, slots = out.shape[1:]
    size = 5 * cols * rows
    source = 0
    for k in range(got.shape[0] * near):
        source = jnp.where(place[3 + k] == place[0], k // near, source)
    for f in range(5):
        for c in range(cols):
            at = (f * cols + c) * rows
            out[f, c] = got[source, at : at + rows]
    offset, speed = tool_step(tool, jnp.sum(got[:, size : size + 1, :], axis=0), scale)
    new_tool[0] = offset[0, 0]
    new_tool[1] = speed[0, 0]


def body(positions, velocity, density, counts, contact_mask, destination, tool):
    cols, rows, slots = density.shape
    ncut, ndepth = lax.axis_size("cut"), lax.axis_size("depth")
    here, depth = lax.axis_index("cut"), lax.axis_index("depth")
    scale = 1.0 / (ncut * cols * ndepth * rows * slots)
    place = jnp.concatenate([jnp.stack([here, depth, jnp.int32(ncut)]).astype(jnp.int32), destination])
    near = 8 if ncut % 8 == 0 else 1
    far = ncut // near
    size = 5 * cols * rows
    tall = rows + 2
    state, block = shape(5, cols, rows, slots), shape(3, cols, rows, slots)
    message, vector = shape(ndepth, 16, slots), shape(2, slots)
    column = shape(5, tall, slots)
    sums = [pltpu.VMEM((cols * rows * 32, slots), F32)] * 2
    inner_scratch = [pltpu.VMEM((cols * rows * 32, slots), F32)] + sums
    outer_scratch = [pltpu.VMEM(((cols + 2) * tall * 32, slots), F32)] + sums
    forth = [(i, i + 1) for i in range(ncut - 1)]
    back = [(i + 1, i) for i in range(ncut - 1)]

    outs = [state, shape(2, cols, rows, slots), vector, message]
    own, marks, tool, sent = call(start_kernel, outs, (place, counts, contact_mask, tool), (positions, velocity, density))
    for step in range(STEPS):
        got = lax.all_to_all(sent, "depth", 0, 0, tiled=True)
        inner = call(inner_kernel, block, (place,), (own, marks), inner_scratch, COST)
        first = (inner,) if step < STEPS - 1 else ()
        left, right, force = call(extend_kernel, [column, column, shape(ncut, 1, slots)], (place,), (own, marks, got) + first)
        before = lax.ppermute(right, "cut", forth)
        after = lax.ppermute(left, "cut", back)
        if step < STEPS - 1:
            total = lax.all_to_all(force, "cut", 0, 0, tiled=True)
        found = call(outer_kernel, block, (place,), (before, left, right, after, inner), outer_scratch, COST)
        if step < STEPS - 1:
            kernel = functools.partial(update_kernel, scale)
            own, tool, sent = call(kernel, [state, vector, message], (place,), (own, found, marks, total, tool))
    kernel = functools.partial(last_kernel, near)
    sent = call(kernel, shape(near, size + 8, slots), (place,), (own, found, marks, tool, force[:, 0]))
    close = [[g * near + k for k in range(near)] for g in range(far)]
    apart = [[g * near + k for g in range(far)] for k in range(near)]
    got = lax.all_to_all(sent, "cut", 0, 0, tiled=True, axis_index_groups=close)
    sent = call(functools.partial(sort_kernel, near, size), shape(far, size + 8, slots), (place,), (got,))
    got = lax.all_to_all(sent, "cut", 0, 0, tiled=True, axis_index_groups=apart)
    return pl.pallas_call(
        functools.partial(take_kernel, near, scale),
        out_shape=[state, shape(2)],
        in_specs=[SMEM, VMEM, VMEM],
        out_specs=[VMEM, SMEM],
        compiler_params=PARAMS,
    )(place, got, tool)


def solution(mesh):
    return jax.shard_map(
        body,
        mesh=mesh,
        in_specs=(
            P(None, "cut", "depth", None),
            P(None, "cut", "depth", None),
            P("cut", "depth", None),
            P("cut", "depth"),
            P("cut", "depth"),
            P(),
            P(),
        ),
        out_specs=(P(None, "cut", "depth", None), P()),
        check_vma=False,
    )
```

```python
import functools

import jax
import jax.numpy as jnp
from jax import lax
from jax.experimental import pallas as pl
from jax.experimental.pallas import tpu as pltpu
from jax.sharding import PartitionSpec as P

STEPS = 4
MASS = 0.02
SOUND = 20.0
VISCOSITY = 2.0
STIFF = 50.0
DT = 0.05

FAR = 1.0e6

COST = 100_000_000

F32 = jnp.float32
BF16 = jnp.bfloat16
PARAMS = pltpu.CompilerParams(vmem_limit_bytes=40 * 1024 * 1024)
VMEM = pl.BlockSpec(memory_space=pltpu.VMEM)
SMEM = pl.BlockSpec(memory_space=pltpu.SMEM)


def shape(*dims):
    return jax.ShapeDtypeStruct(dims, F32)


def call(kernel, outs, scalars, arrays, scratch=(), estimate=0):
    return pl.pallas_call(
        kernel,
        out_shape=outs,
        in_specs=[SMEM] * len(scalars) + [VMEM] * len(arrays),
        out_specs=[VMEM] * len(outs) if isinstance(outs, list) else VMEM,
        scratch_shapes=scratch,
        compiler_params=PARAMS,
        cost_estimate=pl.CostEstimate(flops=estimate, bytes_accessed=1 << 20, transcendentals=0) if estimate else None,
    )(*scalars, *arrays)


def pressure(s):
    inv = 1.0 / s
    return SOUND * (s - 1.0) * inv * inv, inv


def penalties(x, touch, live, offset, column):
    return touch * live * jnp.maximum(0.0, x - column + offset - 0.5)


def own_force(new, marks, offset, first):
    total = 0.0
    for c, fields in enumerate(new):
        total = total + STIFF * penalties(fields[0], marks[1, c], marks[0, c], offset, first + c)
    total = jnp.sum(total, axis=0, keepdims=True)
    return jnp.broadcast_to(jnp.sum(total, axis=1, keepdims=True), total.shape)


def visible(fields, live):
    alive = live > 0
    x, y, u, v, rho = fields
    return [jnp.where(alive, x, FAR), y, u, v, jnp.where(alive, rho, 1.0)]


def fill_depth(place, new, marks, force, sent):
    depth, ndepth = place[1], sent.shape[0]
    cols, rows = marks.shape[1:3]
    sent[...] = jnp.zeros(sent.shape, F32)
    if force is not None:
        sent[:, 5 * cols : 5 * cols + 1, :] = jnp.broadcast_to(force[None], (ndepth, 1, force.shape[1]))
    seen = [visible(new[c], marks[0, c]) for c in range(cols)]

    @pl.when(depth > 0)
    def _():
        for c in range(cols):
            for f in range(5):
                sent[depth - 1, f * cols + c : f * cols + c + 1] = seen[c][f][0:1]

    @pl.when(depth < ndepth - 1)
    def _():
        for c in range(cols):
            for f in range(5):
                sent[depth + 1, f * cols + c : f * cols + c + 1] = seen[c][f][rows - 1 : rows]


def origin(place, cols, rows):
    first = (place[0] * cols).astype(F32)
    return first + 0.5 * cols, (place[1] * rows).astype(F32) + 0.5 * rows, first


def start_kernel(place, counts, contact, first_tool, positions, velocity, density, own, marks, tool, sent, force):
    cols, rows, slots = density.shape
    row = lax.broadcasted_iota(jnp.int32, (rows, slots), 0)
    slot = lax.broadcasted_iota(jnp.int32, (rows, slots), 1)
    new = []
    for c in range(cols):
        filled = jnp.zeros((rows, slots), jnp.int32)
        touch = jnp.zeros((rows, slots), jnp.int32)
        for r in range(rows):
            filled = jnp.where(row == r, counts[c, r], filled)
            touch = jnp.where(row == r, contact[c, r], touch)
        marks[0, c] = jnp.where(slot < filled, 1.0, 0.0)
        marks[1, c] = touch.astype(F32)
        new.append([positions[0, c], positions[1, c], velocity[0, c], velocity[1, c], density[c]])
        for f in range(5):
            own[f, c] = new[c][f]
    offset = jnp.zeros((1, slots), F32) + first_tool[0]
    tool[0:1] = offset
    tool[1:2] = jnp.zeros((1, slots), F32) + first_tool[1]
    part = own_force(new, marks, offset, origin(place, cols, rows)[2])
    force[...] = jnp.broadcast_to(part[None], force.shape)
    fill_depth(place, new, marks, None, sent)


def extend(place, own, marks, got, left, right):
    depth, ndepth = place[1], got.shape[0]
    cols, rows = own.shape[1:3]
    above = got[jnp.maximum(depth - 1, 0)]
    below = got[jnp.minimum(depth + 1, ndepth - 1)]
    blank = [FAR, 0.0, 0.0, 0.0, 1.0]
    for c, column in ((0, left), (cols - 1, right)):
        seen = visible([own[f, c] for f in range(5)], marks[0, c])
        for f in range(5):
            k = f * cols + c
            column[f, 0:1] = jnp.where(depth > 0, above[k : k + 1], blank[f])
            column[f, 1 : rows + 1] = seen[f]
            column[f, rows + 1 : rows + 2] = jnp.where(depth < ndepth - 1, below[k : k + 1], blank[f])


def first_extend_kernel(place, own, marks, got, inner, left, right):
    extend(place, own, marks, got, left, right)


def extend_kernel(scale, place, own, marks, got, inner, tool, left, right, new_tool, force):
    cols, rows = own.shape[1:3]
    row = 5 * cols
    offset, speed = tool_step(tool, jnp.sum(got[:, row : row + 1, :], axis=0), scale)
    new_tool[0:1] = offset
    new_tool[1:2] = speed
    state = [[own[f, c] for f in range(5)] for c in range(cols)]
    part = own_force(state, marks, offset, origin(place, cols, rows)[2])
    force[...] = jnp.broadcast_to(part[None], force.shape)
    extend(place, own, marks, got, left, right)


def pair_sums(columns, center, pairs, out, feat, acc2, acc3, earlier=None):
    x0, y0, _ = center
    tall, slots = columns[0][0].shape
    rows = len(pairs) // 2
    margin = (tall - rows) // 2
    for c, (x, y, u, v, s) in enumerate(columns):
        lx, ly = x - x0, y - y0
        press, inv = pressure(s)
        parts = [jnp.ones_like(x), lx, ly, press, press * lx, press * ly, u, v, u * lx + v * ly, inv, inv * u, inv * v]
        for k in range(16):
            high = parts[k].astype(BF16).astype(F32) if k < 12 else jnp.zeros_like(x)
            feat[pl.ds(c * tall * 32 + k, tall, stride=32), :] = high
            feat[pl.ds(c * tall * 32 + 16 + k, tall, stride=32), :] = parts[k] - high if k < 12 else high
    for i, ((c, r), around) in enumerate(pairs.items()):
        xi, yi = [jnp.broadcast_to(f[r : r + 1], (slots, slots)).T for f in columns[c][:2]]

        def weights(a, b):
            dx = (xi - columns[a][0][b : b + 1]).astype(BF16)
            dy = (yi - columns[a][1][b : b + 1]).astype(BF16)
            q = jnp.maximum(BF16(0.0), BF16(1.0) - dx * dx - dy * dy)
            q2 = q * q
            return jnp.concatenate([q2, q2 * q], axis=0)

        total = None
        for n in range(0, len(around), 2):
            pair = around[n : n + 2]
            w = jnp.concatenate([weights(a, b) for a, b in pair], axis=1)
            f = jnp.concatenate([feat[pl.ds((a * tall + b) * 32, 32), :] for a, b in pair], axis=1).astype(BF16)
            found = lax.dot_general(f, w, (((1,), (1,)), ((), ())), preferred_element_type=F32)
            total = found if total is None else total + found
        acc2[i * 32 : (i + 1) * 32] = total[:, :slots]
        acc3[i * 32 : (i + 1) * 32] = total[:, slots:]

    for n, c in enumerate(sorted({c for c, _ in pairs})):

        def summed(k):
            acc = acc2 if k < 9 else acc3
            return sum(acc[pl.ds(n * rows * 32 + k + low, rows, stride=32), :] for low in (0, 16))

        x, y, u, v, s = [f[margin : margin + rows] for f in columns[c]]
        x, y = x - x0, y - y0
        press, _ = pressure(s)
        a0, ax, ay, ap, apx, apy, au, av, aw, b0, bu, bv = [summed(k) for k in range(12)]
        sx, sy = x * a0 - ax, y * a0 - ay
        rates = [
            (6.0 * MASS) * (press * sx + x * ap - apx) - (VISCOSITY * MASS) * (u * b0 - bu),
            (6.0 * MASS) * (press * sy + y * ap - apy) - (VISCOSITY * MASS) * (v * b0 - bv),
            (-6.0 * MASS) * (u * sx + v * sy - x * au - y * av + aw),
        ]
        for f in range(3):
            out[f, n] = rates[f] if earlier is None else rates[f] + earlier[f, n]


def around_cell(c, r):
    return [(c + a, r + b) for a in (-1, 0, 1) for b in (-1, 0, 1)]


def inner_kernel(place, own, marks, out, feat, acc2, acc3):
    cols, rows = own.shape[1:3]
    columns = [visible([own[f, c] for f in range(5)], marks[0, c]) for c in range(cols)]
    cells = [(c, r) for c in range(cols) for r in range(rows)]
    pairs = {cell: [j for j in around_cell(*cell) if j in cells] for cell in cells}
    pair_sums(columns, origin(place, cols, rows), pairs, out, feat, acc2, acc3)


def outer_kernel(place, before, left, right, after, earlier, out, feat, acc2, acc3):
    cols, rows = earlier.shape[1:3]
    columns = []
    for c, ref in enumerate((before, left, right, after)):
        fields = [ref[f] for f in range(5)]
        if c in (0, 3):
            outside = place[0] == (0 if c == 0 else place[2] - 1)
            fields[0] = jnp.where(outside, FAR, fields[0])
            fields[4] = jnp.where(outside, 1.0, fields[4])
        columns.append(fields)
    cells = [(c + 1, r + 1) for c in range(cols) for r in range(rows)]
    pairs = {cell: [j for j in around_cell(*cell) if j not in cells] for cell in cells}
    pair_sums(columns, origin(place, cols, rows), pairs, out, feat, acc2, acc3, earlier)


def moved_state(own, found, marks, offset, first):
    new = []
    for c in range(own.shape[1]):
        live = marks[0, c]
        pen = penalties(own[0, c], marks[1, c], live, offset, first + c)
        u = own[2, c] + DT * live * (found[0, c] - STIFF * pen)
        v = own[3, c] + DT * live * found[1, c]
        x = own[0, c] + DT * live * u
        y = own[1, c] + DT * live * v
        rho = own[4, c] + DT * live * found[2, c]
        new.append([x, y, u, v, rho])
    return new


def tool_step(tool, force, scale):
    speed = tool[1:2] + DT * (1.0 - force * scale)
    return tool[0:1] + DT * speed, speed


def update_kernel(place, own, found, marks, tool, total, new_own, sent):
    new = moved_state(own, found, marks, tool[0:1], origin(place, *own.shape[1:3])[2])
    for c, fields in enumerate(new):
        for f in range(5):
            new_own[f, c] = fields[f]
    fill_depth(place, new, marks, jnp.sum(total[...], axis=0), sent)


def last_kernel(near, place, own, found, marks, tool, total, sent):
    cols, rows, slots = own.shape[1:]
    size = 5 * cols * rows
    new = moved_state(own, found, marks, tool[0:1], origin(place, cols, rows)[2])
    sent[...] = jnp.zeros(sent.shape, F32)
    sent[:, size:, :] = jnp.broadcast_to(jnp.sum(total[...], axis=0, keepdims=True), (near, sent.shape[1] - size, slots))
    digit = lax.rem(place[3 + place[0]], near)
    for f in range(5):
        for c in range(cols):
            at = (f * cols + c) * rows
            sent[digit, at : at + rows] = new[c][f]


def sort_kernel(near, size, place, got, sent):
    far, most, slots = sent.shape
    group, digit = lax.div(place[0], near), lax.rem(place[0], near)
    sent[...] = jnp.zeros(sent.shape, F32)
    total = jnp.sum(got[:, size : size + 1, :], axis=0, keepdims=True)
    sent[:, size:, :] = jnp.broadcast_to(total, (far, most - size, slots))
    for k in range(near):
        target = place[3 + group * near + k]

        @pl.when(lax.rem(target, near) == digit)
        def _():
            sent[lax.div(target, near), 0:size] = got[k, 0:size]


def take_kernel(near, scale, place, got, tool, out, new_tool):
    cols, rows, slots = out.shape[1:]
    size = 5 * cols * rows
    source = 0
    for k in range(got.shape[0] * near):
        source = jnp.where(place[3 + k] == place[0], k // near, source)
    for f in range(5):
        for c in range(cols):
            at = (f * cols + c) * rows
            out[f, c] = got[source, at : at + rows]
    offset, speed = tool_step(tool, jnp.sum(got[:, size : size + 1, :], axis=0), scale)
    new_tool[0] = offset[0, 0]
    new_tool[1] = speed[0, 0]


def body(positions, velocity, density, counts, contact_mask, destination, tool):
    cols, rows, slots = density.shape
    ncut, ndepth = lax.axis_size("cut"), lax.axis_size("depth")
    here, depth = lax.axis_index("cut"), lax.axis_index("depth")
    scale = 1.0 / (ncut * cols * ndepth * rows * slots)
    place = jnp.concatenate([jnp.stack([here, depth, jnp.int32(ncut)]).astype(jnp.int32), destination])
    near = 8 if ncut % 8 == 0 else 1
    far = ncut // near
    size = 5 * cols * rows
    tall = rows + 2
    state, block = shape(5, cols, rows, slots), shape(3, cols, rows, slots)
    message, vector = shape(ndepth, 16, slots), shape(2, slots)
    column = shape(5, tall, slots)
    sums = [pltpu.VMEM((cols * rows * 32, slots), F32)] * 2
    inner_scratch = [pltpu.VMEM((cols * rows * 32, slots), F32)] + sums
    outer_scratch = [pltpu.VMEM(((cols + 2) * tall * 32, slots), F32)] + sums
    forth = [(i, i + 1) for i in range(ncut - 1)]
    back = [(i + 1, i) for i in range(ncut - 1)]

    whole = [place]
    outs = [state, shape(2, cols, rows, slots), vector, message, shape(ncut, 1, slots)]
    own, marks, tool, sent, force = call(start_kernel, outs, (place, counts, contact_mask, tool), (positions, velocity, density))
    for step in range(STEPS):
        got = lax.all_to_all(sent, "depth", 0, 0, tiled=True)
        inner = call(inner_kernel, block, whole, (own, marks), inner_scratch, COST)
        if step == 0:
            left, right = call(first_extend_kernel, [column, column], whole, (own, marks, got, inner))
        else:
            kernel = functools.partial(extend_kernel, scale)
            outs = [column, column, vector, shape(ncut if step < STEPS - 1 else ndepth, 1, slots)]
            left, right, tool, force = call(kernel, outs, whole, (own, marks, got, inner, tool))
        before = lax.ppermute(right, "cut", forth)
        after = lax.ppermute(left, "cut", back)
        total = lax.all_to_all(force, "cut" if step < STEPS - 1 else "depth", 0, 0, tiled=True)
        found = call(outer_kernel, block, whole, (before, left, right, after, inner), outer_scratch, COST)
        if step < STEPS - 1:
            own, sent = call(update_kernel, [state, message], whole, (own, found, marks, tool, total))
    kernel = functools.partial(last_kernel, near)
    sent = call(kernel, shape(near, size + 8, slots), whole, (own, found, marks, tool, total))
    close = [[g * near + k for k in range(near)] for g in range(far)]
    apart = [[g * near + k for g in range(far)] for k in range(near)]
    got = lax.all_to_all(sent, "cut", 0, 0, tiled=True, axis_index_groups=close)
    sent = call(functools.partial(sort_kernel, near, size), shape(far, size + 8, slots), (place,), (got,))
    got = lax.all_to_all(sent, "cut", 0, 0, tiled=True, axis_index_groups=apart)
    return pl.pallas_call(
        functools.partial(take_kernel, near, scale),
        out_shape=[state, shape(2)],
        in_specs=[SMEM, VMEM, VMEM],
        out_specs=[VMEM, SMEM],
        compiler_params=PARAMS,
    )(place, got, tool)


def solution(mesh):
    return jax.shard_map(
        body,
        mesh=mesh,
        in_specs=(
            P(None, "cut", "depth", None),
            P(None, "cut", "depth", None),
            P("cut", "depth", None),
            P("cut", "depth"),
            P("cut", "depth"),
            P(),
            P(),
        ),
        out_specs=(P(None, "cut", "depth", None), P()),
        check_vma=False,
    )
```

```python
import functools

import jax
import jax.numpy as jnp
from jax import lax
from jax.experimental import pallas as pl
from jax.experimental.pallas import tpu as pltpu
from jax.sharding import PartitionSpec as P

HALO = 2
MASS = 0.02
SOUND = 20.0
VISCOSITY = 2.0
STIFF = 50.0
DT = 0.05

FAR = 1.0e6

COST = 20_000_000_000

F32 = jnp.float32
BF16 = jnp.bfloat16
PARAMS = pltpu.CompilerParams(vmem_limit_bytes=40 * 1024 * 1024)
VMEM = pl.BlockSpec(memory_space=pltpu.VMEM)
SMEM = pl.BlockSpec(memory_space=pltpu.SMEM)


def shape(*dims):
    return jax.ShapeDtypeStruct(dims, F32)


def call(kernel, outs, scalars, arrays, scratch=(), estimate=0):
    return pl.pallas_call(
        kernel,
        out_shape=outs,
        in_specs=[SMEM] * len(scalars) + [VMEM] * len(arrays),
        out_specs=[VMEM] * len(outs) if isinstance(outs, list) else VMEM,
        scratch_shapes=scratch,
        compiler_params=PARAMS,
        cost_estimate=pl.CostEstimate(flops=estimate, bytes_accessed=1 << 20, transcendentals=0) if estimate else None,
    )(*scalars, *arrays)


def pressure(s):
    inv = 1.0 / s
    return SOUND * (s - 1.0) * inv * inv, inv


def penalties(x, touch, live, offset, column):
    return touch * live * jnp.maximum(0.0, x - column + offset - 0.5)


def own_force(new, marks, offset, first):
    total = 0.0
    for c, fields in enumerate(new):
        total = total + STIFF * penalties(fields[0], marks[1, c], marks[0, c], offset, first + c)
    total = jnp.sum(total, axis=0, keepdims=True)
    return jnp.broadcast_to(jnp.sum(total, axis=1, keepdims=True), total.shape)


def visible(fields, live, touch):
    alive = live > 0
    x, y, u, v, rho = fields
    return [jnp.where(alive, x, FAR), y, u, v, jnp.where(alive, rho, 1.0), live * touch]


def fill_depth(place, state, marks, force, sent):
    depth, ndepth = place[1], sent.shape[0]
    cols, rows = marks.shape[1:3]
    row = 6 * cols * HALO
    sent[...] = jnp.zeros(sent.shape, F32)
    sent[:, row : row + 1, :] = jnp.broadcast_to(force[None], (ndepth, 1, force.shape[1]))
    seen = [visible(state[c], marks[0, c], marks[1, c]) for c in range(cols)]

    def put(target, rim):
        for c in range(cols):
            for f in range(6):
                at = (f * cols + c) * HALO
                sent[target, at : at + HALO] = seen[c][f][rim : rim + HALO]

    @pl.when(depth > 0)
    def _():
        put(depth - 1, 0)

    @pl.when(depth < ndepth - 1)
    def _():
        put(depth + 1, rows - HALO)


def origin(place, cols, rows):
    first = (place[0] * cols).astype(F32)
    return first + 0.5 * cols, (place[1] * rows).astype(F32) + 0.5 * rows, first


def start_kernel(place, counts, contact, first_tool, positions, velocity, density, own, marks, tool, sent):
    cols, rows, slots = density.shape
    row = lax.broadcasted_iota(jnp.int32, (rows, slots), 0)
    slot = lax.broadcasted_iota(jnp.int32, (rows, slots), 1)
    new = []
    for c in range(cols):
        filled = jnp.zeros((rows, slots), jnp.int32)
        touch = jnp.zeros((rows, slots), jnp.int32)
        for r in range(rows):
            filled = jnp.where(row == r, counts[c, r], filled)
            touch = jnp.where(row == r, contact[c, r], touch)
        marks[0, c] = jnp.where(slot < filled, 1.0, 0.0)
        marks[1, c] = touch.astype(F32)
        new.append([positions[0, c], positions[1, c], velocity[0, c], velocity[1, c], density[c]])
        for f in range(5):
            own[f, c] = new[c][f]
    offset = jnp.zeros((1, slots), F32) + first_tool[0]
    tool[0:1] = offset
    tool[1:2] = jnp.zeros((1, slots), F32) + first_tool[1]
    fill_depth(place, new, marks, own_force(new, marks, offset, origin(place, cols, rows)[2]), sent)


def extend_kernel(place, own, marks, got, wide, force):
    depth, ndepth = place[1], got.shape[0]
    cols, rows = own.shape[1:3]
    above = got[jnp.maximum(depth - 1, 0)]
    below = got[jnp.minimum(depth + 1, ndepth - 1)]
    blank = [FAR, 0.0, 0.0, 0.0, 1.0, 0.0]
    for c in range(cols):
        seen = visible([own[f, c] for f in range(5)], marks[0, c], marks[1, c])
        for f in range(6):
            at = (f * cols + c) * HALO
            wide[f, c, 0:HALO] = jnp.where(depth > 0, above[at : at + HALO], blank[f])
            wide[f, c, HALO : rows + HALO] = seen[f]
            wide[f, c, rows + HALO :] = jnp.where(depth < ndepth - 1, below[at : at + HALO], blank[f])
    row = 6 * cols * HALO
    total = jnp.sum(got[:, row : row + 1, :], axis=0)
    force[...] = jnp.broadcast_to(total[None], force.shape)


def spread_kernel(got, force):
    force[...] = jnp.broadcast_to(jnp.sum(got[...], axis=0, keepdims=True), force.shape)


def pair_sums(columns, center, out, feat, acc2, acc3):
    x0, y0, _ = center
    tall, slots = columns[0][0].shape
    rows = tall - 2
    for c, (x, y, u, v, s) in enumerate(columns):
        lx, ly = x - x0, y - y0
        press, inv = pressure(s)
        parts = [jnp.ones_like(x), lx, ly, press, press * lx, press * ly, u, v, u * lx + v * ly, inv, inv * u, inv * v]
        for k in range(16):
            high = parts[k].astype(BF16).astype(F32) if k < 12 else jnp.zeros_like(x)
            feat[pl.ds(c * tall * 32 + k, tall, stride=32), :] = high
            feat[pl.ds(c * tall * 32 + 16 + k, tall, stride=32), :] = parts[k] - high if k < 12 else high
    for i, (c, r) in enumerate([(c, r) for c in range(1, len(columns) - 1) for r in range(1, tall - 1)]):
        xi, yi = [jnp.broadcast_to(f[r : r + 1], (slots, slots)).T for f in columns[c][:2]]
        around = [(c + a, r + b) for a in (-1, 0, 1) for b in (-1, 0, 1)]

        def weights(a, b):
            dx = (xi - columns[a][0][b : b + 1]).astype(BF16)
            dy = (yi - columns[a][1][b : b + 1]).astype(BF16)
            q = jnp.maximum(BF16(0.0), BF16(1.0) - dx * dx - dy * dy)
            q2 = q * q
            return jnp.concatenate([q2, q2 * q], axis=0)

        total = None
        for n in range(0, 9, 2):
            pair = around[n : n + 2]
            w = jnp.concatenate([weights(a, b) for a, b in pair], axis=1)
            f = jnp.concatenate([feat[pl.ds((a * tall + b) * 32, 32), :] for a, b in pair], axis=1).astype(BF16)
            found = lax.dot_general(f, w, (((1,), (1,)), ((), ())), preferred_element_type=F32)
            total = found if total is None else total + found
        acc2[i * 32 : (i + 1) * 32] = total[:, :slots]
        acc3[i * 32 : (i + 1) * 32] = total[:, slots:]

    for n in range(len(columns) - 2):

        def summed(k):
            acc = acc2 if k < 9 else acc3
            return sum(acc[pl.ds(n * rows * 32 + k + low, rows, stride=32), :] for low in (0, 16))

        x, y, u, v, s = [f[1 : rows + 1] for f in columns[n + 1]]
        x, y = x - x0, y - y0
        press, _ = pressure(s)
        a0, ax, ay, ap, apx, apy, au, av, aw, b0, bu, bv = [summed(k) for k in range(12)]
        sx, sy = x * a0 - ax, y * a0 - ay
        out[0, n] = (6.0 * MASS) * (press * sx + x * ap - apx) - (VISCOSITY * MASS) * (u * b0 - bu)
        out[1, n] = (6.0 * MASS) * (press * sy + y * ap - apy) - (VISCOSITY * MASS) * (v * b0 - bv)
        out[2, n] = (-6.0 * MASS) * (u * sx + v * sy - x * au - y * av + aw)


def wide_columns(place, wide, swapped, other):
    even = lax.rem(place[0], 2) == 0
    cols = wide.shape[1]
    blank = [FAR, 0.0, 0.0, 0.0, 1.0, 0.0]
    columns = []
    for side in range(3):
        outside = place[0] == (0 if side == 0 else place[2] - 1)
        for c in range(cols):
            if side == 1:
                fields = [wide[f, c] for f in range(6)]
            else:
                first, second = (other, swapped) if side == 0 else (swapped, other)
                fields = [jnp.where(outside, blank[f], jnp.where(even, first[f, c], second[f, c])) for f in range(6)]
            columns.append(fields)
    return columns


def wide_rates_kernel(place, size, wide, swapped, other, out, feat, acc2, acc3):
    columns = [fields[:5] for fields in wide_columns(place, wide, swapped, other)]
    pair_sums(columns, origin(place, *size), out, feat, acc2, acc3)


def rates_kernel(place, size, ring, out, feat, acc2, acc3):
    columns = [[ring[f, c] for f in range(5)] for c in range(ring.shape[1])]
    pair_sums(columns, origin(place, *size), out, feat, acc2, acc3)


def moved_ring(place, columns, found, offset, first, ring):
    for n in range(ring.shape[1]):
        x, y, u, v, s, touch = [f[1:-1] for f in columns[n + 1]]
        live = jnp.where(x < 0.5 * FAR, 1.0, 0.0)
        pen = touch * jnp.maximum(0.0, x - (first + (n - 1)) + offset - 0.5)
        u = u + DT * live * (found[0, n] - STIFF * pen)
        v = v + DT * live * found[1, n]
        ring[0, n] = x + DT * live * u
        ring[1, n] = y + DT * live * v
        ring[2, n] = u
        ring[3, n] = v
        ring[4, n] = s + DT * live * found[2, n]


def moved_state(own, found, marks, offset, first):
    cols, rows = own.shape[1:3]
    side, rim = (found.shape[1] - cols) // 2, (found.shape[2] - rows) // 2
    new = []
    for c in range(cols):
        live = marks[0, c]
        ax, ay, drho = [found[f, c + side][rim : rim + rows] for f in range(3)]
        pen = penalties(own[0, c], marks[1, c], live, offset, first + c)
        u = own[2, c] + DT * live * (ax - STIFF * pen)
        v = own[3, c] + DT * live * ay
        x = own[0, c] + DT * live * u
        y = own[1, c] + DT * live * v
        rho = own[4, c] + DT * live * drho
        new.append([x, y, u, v, rho])
    return new


def keep(new, own):
    for c, fields in enumerate(new):
        for f in range(5):
            own[f, c] = fields[f]


def tool_step(tool, force, scale):
    speed = tool[1:2] + DT * (1.0 - force * scale)
    return tool[0:1] + DT * speed, speed


def first_update_kernel(scale, place, own, found, marks, wide, swapped, other, tool, total, new_own, ring, new_tool):
    first = origin(place, *own.shape[1:3])[2]
    keep(moved_state(own, found, marks, tool[0:1], first), new_own)
    moved_ring(place, wide_columns(place, wide, swapped, other), found, tool[0:1], first, ring)
    offset, speed = tool_step(tool, jnp.sum(total[...], axis=0), scale)
    new_tool[0:1] = offset
    new_tool[1:2] = speed


def second_update_kernel(place, own, found, marks, tool, new_own, sent):
    first = origin(place, *own.shape[1:3])[2]
    state = [[own[f, c] for f in range(5)] for c in range(own.shape[1])]
    new = moved_state(own, found, marks, tool[0:1], first)
    keep(new, new_own)
    fill_depth(place, new, marks, own_force(state, marks, tool[0:1], first), sent)


def third_update_kernel(scale, place, own, found, marks, wide, swapped, other, tool, total, new_own, ring, new_tool, force):
    first = origin(place, *own.shape[1:3])[2]
    offset, speed = tool_step(tool, jnp.sum(total[...], axis=0), scale)
    new_tool[0:1] = offset
    new_tool[1:2] = speed
    state = [[own[f, c] for f in range(5)] for c in range(own.shape[1])]
    force[...] = jnp.broadcast_to(own_force(state, marks, offset, first)[None], force.shape)
    keep(moved_state(own, found, marks, offset, first), new_own)
    moved_ring(place, wide_columns(place, wide, swapped, other), found, offset, first, ring)


def last_force_kernel(scale, place, own, marks, tool, total, new_tool, force):
    offset, speed = tool_step(tool, jnp.sum(total[...], axis=0), scale)
    new_tool[0:1] = offset
    new_tool[1:2] = speed
    state = [[own[f, c] for f in range(5)] for c in range(own.shape[1])]
    part = own_force(state, marks, offset, origin(place, *own.shape[1:3])[2])
    force[...] = jnp.broadcast_to(part[None], force.shape)


def last_kernel(near, place, own, found, marks, tool, total, sent):
    cols, rows, slots = own.shape[1:]
    size = 5 * cols * rows
    new = moved_state(own, found, marks, tool[0:1], origin(place, cols, rows)[2])
    sent[...] = jnp.zeros(sent.shape, F32)
    sent[:, size:, :] = jnp.broadcast_to(jnp.sum(total[...], axis=0, keepdims=True), (near, sent.shape[1] - size, slots))
    digit = lax.rem(place[3 + place[0]], near)
    for f in range(5):
        for c in range(cols):
            at = (f * cols + c) * rows
            sent[digit, at : at + rows] = new[c][f]


def sort_kernel(near, size, place, got, sent):
    far, most, slots = sent.shape
    group, digit = lax.div(place[0], near), lax.rem(place[0], near)
    sent[...] = jnp.zeros(sent.shape, F32)
    total = jnp.sum(got[:, size : size + 1, :], axis=0, keepdims=True)
    sent[:, size:, :] = jnp.broadcast_to(total, (far, most - size, slots))
    for k in range(near):
        target = place[3 + group * near + k]

        @pl.when(lax.rem(target, near) == digit)
        def _():
            sent[lax.div(target, near), 0:size] = got[k, 0:size]


def take_kernel(near, scale, place, got, tool, out, new_tool):
    cols, rows, slots = out.shape[1:]
    size = 5 * cols * rows
    source = 0
    for k in range(got.shape[0] * near):
        source = jnp.where(place[3 + k] == place[0], k // near, source)
    for f in range(5):
        for c in range(cols):
            at = (f * cols + c) * rows
            out[f, c] = got[source, at : at + rows]
    offset, speed = tool_step(tool, jnp.sum(got[:, size : size + 1, :], axis=0), scale)
    new_tool[0] = offset[0, 0]
    new_tool[1] = speed[0, 0]


def body(positions, velocity, density, counts, contact_mask, destination, tool):
    cols, rows, slots = density.shape
    ncut, ndepth = lax.axis_size("cut"), lax.axis_size("depth")
    here, depth = lax.axis_index("cut"), lax.axis_index("depth")
    scale = 1.0 / (ncut * cols * ndepth * rows * slots)
    place = jnp.concatenate([jnp.stack([here, depth, jnp.int32(ncut)]).astype(jnp.int32), destination])
    near = 8 if ncut % 8 == 0 else 1
    far = ncut // near
    size = 5 * cols * rows
    state, marking = shape(5, cols, rows, slots), shape(2, cols, rows, slots)
    message, vector = shape(ndepth, 32, slots), shape(2, slots)
    along_cut, along_depth = shape(ncut, 1, slots), shape(ndepth, 1, slots)
    ring, ring_rates = shape(5, cols + 2, rows + 2, slots), shape(3, cols + 2, rows + 2, slots)
    swap = [(i, i ^ 1) for i in range(ncut)]
    cross = [(i, i + 1 if i % 2 else i - 1) for i in range(1, ncut - 1)]

    def scratch(wide, tall):
        return [pltpu.VMEM((n * 32, slots), F32) for n in (wide * tall, (wide - 2) * (tall - 2), (wide - 2) * (tall - 2))]

    def rates_of(kernel, out, arrays, wide, tall):
        return call(lambda place, *refs: kernel(place, (cols, rows), *refs), out, (place,), arrays, scratch(wide, tall), COST)

    def exchange(own, marks, sent):
        got = lax.all_to_all(sent, "depth", 0, 0, tiled=True)
        wide, force = call(extend_kernel, [shape(6, cols, rows + 2 * HALO, slots), along_cut], (place,), (own, marks, got))
        swapped, other = lax.ppermute(wide, "cut", swap), lax.ppermute(wide, "cut", cross)
        total = lax.all_to_all(force, "cut", 0, 0, tiled=True)
        found = rates_of(wide_rates_kernel, ring_rates, (wide, swapped, other), 3 * cols, rows + 4)
        return found, (wide, swapped, other), total

    own, marks, tool, sent = call(
        start_kernel, [state, marking, vector, message], (place, counts, contact_mask, tool), (positions, velocity, density)
    )
    found, around, total = exchange(own, marks, sent)
    kernel = functools.partial(first_update_kernel, scale)
    own, ringed, tool = call(kernel, [state, ring, vector], (place,), (own, found, marks, *around, tool, total))

    found = rates_of(rates_kernel, shape(3, cols, rows, slots), (ringed,), cols + 2, rows + 2)
    own, sent = call(second_update_kernel, [state, message], (place,), (own, found, marks, tool))

    found, around, total = exchange(own, marks, sent)
    kernel = functools.partial(third_update_kernel, scale)
    outs = [state, ring, vector, along_depth]
    new_own, ringed, tool, force = call(kernel, outs, (place,), (own, found, marks, *around, tool, total))
    own = new_own

    got = lax.all_to_all(force, "depth", 0, 0, tiled=True)
    force = call(spread_kernel, along_cut, (), (got,))
    total = lax.all_to_all(force, "cut", 0, 0, tiled=True)
    found = rates_of(rates_kernel, shape(3, cols, rows, slots), (ringed,), cols + 2, rows + 2)
    kernel = functools.partial(last_force_kernel, scale)
    tool, force = call(kernel, [vector, along_depth], (place,), (own, marks, tool, total))
    total = lax.all_to_all(force, "depth", 0, 0, tiled=True)
    kernel = functools.partial(last_kernel, near)
    sent = call(kernel, shape(near, size + 8, slots), (place,), (own, found, marks, tool, total))
    close = [[g * near + k for k in range(near)] for g in range(far)]
    apart = [[g * near + k for g in range(far)] for k in range(near)]
    got = lax.all_to_all(sent, "cut", 0, 0, tiled=True, axis_index_groups=close)
    sent = call(functools.partial(sort_kernel, near, size), shape(far, size + 8, slots), (place,), (got,))
    got = lax.all_to_all(sent, "cut", 0, 0, tiled=True, axis_index_groups=apart)
    return pl.pallas_call(
        functools.partial(take_kernel, near, scale),
        out_shape=[state, shape(2)],
        in_specs=[SMEM, VMEM, VMEM],
        out_specs=[VMEM, SMEM],
        compiler_params=PARAMS,
    )(place, got, tool)


def solution(mesh):
    return jax.shard_map(
        body,
        mesh=mesh,
        in_specs=(
            P(None, "cut", "depth", None),
            P(None, "cut", "depth", None),
            P("cut", "depth", None),
            P("cut", "depth"),
            P("cut", "depth"),
            P(),
            P(),
        ),
        out_specs=(P(None, "cut", "depth", None), P()),
        check_vma=False,
    )
```

```python
import functools

import jax
import jax.numpy as jnp
from jax import lax
from jax.experimental import pallas as pl
from jax.experimental.pallas import tpu as pltpu
from jax.sharding import PartitionSpec as P

HALO = 2
MASS = 0.02
SOUND = 20.0
VISCOSITY = 2.0
STIFF = 50.0
DT = 0.05

FAR = 1.0e6

COST = 20_000_000_000

F32 = jnp.float32
BF16 = jnp.bfloat16
PARAMS = pltpu.CompilerParams(vmem_limit_bytes=40 * 1024 * 1024)
VMEM = pl.BlockSpec(memory_space=pltpu.VMEM)
SMEM = pl.BlockSpec(memory_space=pltpu.SMEM)


def shape(*dims):
    return jax.ShapeDtypeStruct(dims, F32)


def call(kernel, outs, scalars, arrays, scratch=(), estimate=0):
    return pl.pallas_call(
        kernel,
        out_shape=outs,
        in_specs=[SMEM] * len(scalars) + [VMEM] * len(arrays),
        out_specs=[VMEM] * len(outs) if isinstance(outs, list) else VMEM,
        scratch_shapes=scratch,
        compiler_params=PARAMS,
        cost_estimate=pl.CostEstimate(flops=estimate, bytes_accessed=1 << 20, transcendentals=0) if estimate else None,
    )(*scalars, *arrays)


def pressure(s):
    inv = 1.0 / s
    return SOUND * (s - 1.0) * inv * inv, inv


def penalties(x, touch, live, offset, column):
    return touch * live * jnp.maximum(0.0, x - column + offset - 0.5)


def own_force(new, marks, offset, first):
    total = 0.0
    for c, fields in enumerate(new):
        total = total + STIFF * penalties(fields[0], marks[1, c], marks[0, c], offset, first + c)
    total = jnp.sum(total, axis=0, keepdims=True)
    return jnp.broadcast_to(jnp.sum(total, axis=1, keepdims=True), total.shape)


def visible(fields, live, touch):
    alive = live > 0
    x, y, u, v, rho = fields
    return [jnp.where(alive, x, FAR), y, u, v, jnp.where(alive, rho, 1.0), live * touch]


def fill_depth(place, state, marks, force, sent):
    depth, ndepth = place[1], sent.shape[0]
    cols, rows = marks.shape[1:3]
    row = 6 * cols * HALO
    sent[...] = jnp.zeros(sent.shape, F32)
    sent[:, row : row + 1, :] = jnp.broadcast_to(force[None], (ndepth, 1, force.shape[1]))
    seen = [visible(state[c], marks[0, c], marks[1, c]) for c in range(cols)]

    def put(target, rim):
        for c in range(cols):
            for f in range(6):
                at = (f * cols + c) * HALO
                sent[target, at : at + HALO] = seen[c][f][rim : rim + HALO]

    @pl.when(depth > 0)
    def _():
        put(depth - 1, 0)

    @pl.when(depth < ndepth - 1)
    def _():
        put(depth + 1, rows - HALO)


def origin(place, cols, rows):
    first = (place[0] * cols).astype(F32)
    return first + 0.5 * cols, (place[1] * rows).astype(F32) + 0.5 * rows, first


def start_kernel(place, counts, contact, first_tool, positions, velocity, density, own, marks, tool, sent):
    cols, rows, slots = density.shape
    row = lax.broadcasted_iota(jnp.int32, (rows, slots), 0)
    slot = lax.broadcasted_iota(jnp.int32, (rows, slots), 1)
    new = []
    for c in range(cols):
        filled = jnp.zeros((rows, slots), jnp.int32)
        touch = jnp.zeros((rows, slots), jnp.int32)
        for r in range(rows):
            filled = jnp.where(row == r, counts[c, r], filled)
            touch = jnp.where(row == r, contact[c, r], touch)
        marks[0, c] = jnp.where(slot < filled, 1.0, 0.0)
        marks[1, c] = touch.astype(F32)
        new.append([positions[0, c], positions[1, c], velocity[0, c], velocity[1, c], density[c]])
        for f in range(5):
            own[f, c] = new[c][f]
    offset = jnp.zeros((1, slots), F32) + first_tool[0]
    tool[0:1] = offset
    tool[1:2] = jnp.zeros((1, slots), F32) + first_tool[1]
    fill_depth(place, new, marks, own_force(new, marks, offset, origin(place, cols, rows)[2]), sent)


def extend_kernel(place, own, marks, got, wide):
    depth, ndepth = place[1], got.shape[0]
    cols, rows = own.shape[1:3]
    above = got[jnp.maximum(depth - 1, 0)]
    below = got[jnp.minimum(depth + 1, ndepth - 1)]
    blank = [FAR, 0.0, 0.0, 0.0, 1.0, 0.0]
    for c in range(cols):
        seen = visible([own[f, c] for f in range(5)], marks[0, c], marks[1, c])
        for f in range(6):
            at = (f * cols + c) * HALO
            wide[f * cols + c, 0:HALO] = jnp.where(depth > 0, above[at : at + HALO], blank[f])
            wide[f * cols + c, HALO : rows + HALO] = seen[f]
            wide[f * cols + c, rows + HALO :] = jnp.where(depth < ndepth - 1, below[at : at + HALO], blank[f])
    row = 6 * cols * HALO
    wide[6 * cols] = jnp.broadcast_to(jnp.sum(got[:, row : row + 1, :], axis=0), wide.shape[1:])


def pair_force_kernel(wide, swapped, force):
    last = wide.shape[0] - 1
    force[...] = jnp.broadcast_to((wide[last, 0:1] + swapped[last, 0:1])[None], force.shape)


def spread_kernel(got, force):
    force[...] = jnp.broadcast_to(jnp.sum(got[...], axis=0, keepdims=True), force.shape)


def pair_sums(columns, center, out, feat, acc2, acc3):
    x0, y0, _ = center
    tall, slots = columns[0][0].shape
    rows = tall - 2
    for c, (x, y, u, v, s) in enumerate(columns):
        lx, ly = x - x0, y - y0
        press, inv = pressure(s)
        parts = [jnp.ones_like(x), lx, ly, press, press * lx, press * ly, u, v, u * lx + v * ly, inv, inv * u, inv * v]
        for k in range(16):
            high = parts[k].astype(BF16).astype(F32) if k < 12 else jnp.zeros_like(x)
            feat[pl.ds(c * tall * 32 + k, tall, stride=32), :] = high
            feat[pl.ds(c * tall * 32 + 16 + k, tall, stride=32), :] = parts[k] - high if k < 12 else high
    for i, (c, r) in enumerate([(c, r) for c in range(1, len(columns) - 1) for r in range(1, tall - 1)]):
        xi, yi = [jnp.broadcast_to(f[r : r + 1], (slots, slots)).T for f in columns[c][:2]]
        around = [(c + a, r + b) for a in (-1, 0, 1) for b in (-1, 0, 1)]

        def weights(a, b):
            dx = (xi - columns[a][0][b : b + 1]).astype(BF16)
            dy = (yi - columns[a][1][b : b + 1]).astype(BF16)
            q = jnp.maximum(BF16(0.0), BF16(1.0) - dx * dx - dy * dy)
            q2 = q * q
            return jnp.concatenate([q2, q2 * q], axis=0)

        total = None
        for n in range(0, 9, 2):
            pair = around[n : n + 2]
            w = jnp.concatenate([weights(a, b) for a, b in pair], axis=1)
            f = jnp.concatenate([feat[pl.ds((a * tall + b) * 32, 32), :] for a, b in pair], axis=1).astype(BF16)
            found = lax.dot_general(f, w, (((1,), (1,)), ((), ())), preferred_element_type=F32)
            total = found if total is None else total + found
        acc2[i * 32 : (i + 1) * 32] = total[:, :slots]
        acc3[i * 32 : (i + 1) * 32] = total[:, slots:]

    for n in range(len(columns) - 2):

        def summed(k):
            acc = acc2 if k < 9 else acc3
            return sum(acc[pl.ds(n * rows * 32 + k + low, rows, stride=32), :] for low in (0, 16))

        x, y, u, v, s = [f[1 : rows + 1] for f in columns[n + 1]]
        x, y = x - x0, y - y0
        press, _ = pressure(s)
        a0, ax, ay, ap, apx, apy, au, av, aw, b0, bu, bv = [summed(k) for k in range(12)]
        sx, sy = x * a0 - ax, y * a0 - ay
        out[0, n] = (6.0 * MASS) * (press * sx + x * ap - apx) - (VISCOSITY * MASS) * (u * b0 - bu)
        out[1, n] = (6.0 * MASS) * (press * sy + y * ap - apy) - (VISCOSITY * MASS) * (v * b0 - bv)
        out[2, n] = (-6.0 * MASS) * (u * sx + v * sy - x * au - y * av + aw)


def wide_columns(place, cols, wide, swapped, other):
    even = lax.rem(place[0], 2) == 0
    blank = [FAR, 0.0, 0.0, 0.0, 1.0, 0.0]
    columns = []
    for side in range(3):
        outside = place[0] == (0 if side == 0 else place[2] - 1)
        for c in range(cols):
            if side == 1:
                fields = [wide[f * cols + c] for f in range(6)]
            else:
                first, second = (other, swapped) if side == 0 else (swapped, other)
                fields = [jnp.where(outside, blank[f], jnp.where(even, first[f * cols + c], second[f * cols + c])) for f in range(6)]
            columns.append(fields)
    return columns


def wide_rates_kernel(place, size, wide, swapped, other, out, feat, acc2, acc3):
    columns = [fields[:5] for fields in wide_columns(place, size[0], wide, swapped, other)]
    pair_sums(columns, origin(place, *size), out, feat, acc2, acc3)


def rates_kernel(place, size, ring, out, feat, acc2, acc3):
    columns = [[ring[f, c] for f in range(5)] for c in range(ring.shape[1])]
    pair_sums(columns, origin(place, *size), out, feat, acc2, acc3)


def moved_ring(place, columns, found, offset, first, ring):
    for n in range(ring.shape[1]):
        x, y, u, v, s, touch = [f[1:-1] for f in columns[n + 1]]
        live = jnp.where(x < 0.5 * FAR, 1.0, 0.0)
        pen = touch * jnp.maximum(0.0, x - (first + (n - 1)) + offset - 0.5)
        u = u + DT * live * (found[0, n] - STIFF * pen)
        v = v + DT * live * found[1, n]
        ring[0, n] = x + DT * live * u
        ring[1, n] = y + DT * live * v
        ring[2, n] = u
        ring[3, n] = v
        ring[4, n] = s + DT * live * found[2, n]


def moved_state(own, found, marks, offset, first):
    cols, rows = own.shape[1:3]
    side, rim = (found.shape[1] - cols) // 2, (found.shape[2] - rows) // 2
    new = []
    for c in range(cols):
        live = marks[0, c]
        ax, ay, drho = [found[f, c + side][rim : rim + rows] for f in range(3)]
        pen = penalties(own[0, c], marks[1, c], live, offset, first + c)
        u = own[2, c] + DT * live * (ax - STIFF * pen)
        v = own[3, c] + DT * live * ay
        x = own[0, c] + DT * live * u
        y = own[1, c] + DT * live * v
        rho = own[4, c] + DT * live * drho
        new.append([x, y, u, v, rho])
    return new


def keep(new, own):
    for c, fields in enumerate(new):
        for f in range(5):
            own[f, c] = fields[f]


def tool_step(tool, force, scale):
    speed = tool[1:2] + DT * (1.0 - force * scale)
    return tool[0:1] + DT * speed, speed


def first_update_kernel(place, own, found, marks, wide, swapped, other, tool, new_own, ring):
    first = origin(place, *own.shape[1:3])[2]
    keep(moved_state(own, found, marks, tool[0:1], first), new_own)
    moved_ring(place, wide_columns(place, own.shape[1], wide, swapped, other), found, tool[0:1], first, ring)


def second_update_kernel(scale, place, own, found, marks, tool, total, new_own, new_tool, sent):
    first = origin(place, *own.shape[1:3])[2]
    offset, speed = tool_step(tool, jnp.sum(total[...], axis=0), scale)
    new_tool[0:1] = offset
    new_tool[1:2] = speed
    state = [[own[f, c] for f in range(5)] for c in range(own.shape[1])]
    new = moved_state(own, found, marks, offset, first)
    keep(new, new_own)
    fill_depth(place, new, marks, own_force(state, marks, offset, first), sent)


def third_update_kernel(scale, place, own, found, marks, wide, swapped, other, tool, total, new_own, ring, new_tool, force):
    first = origin(place, *own.shape[1:3])[2]
    offset, speed = tool_step(tool, jnp.sum(total[...], axis=0), scale)
    new_tool[0:1] = offset
    new_tool[1:2] = speed
    state = [[own[f, c] for f in range(5)] for c in range(own.shape[1])]
    force[...] = jnp.broadcast_to(own_force(state, marks, offset, first)[None], force.shape)
    keep(moved_state(own, found, marks, offset, first), new_own)
    moved_ring(place, wide_columns(place, own.shape[1], wide, swapped, other), found, offset, first, ring)


def last_force_kernel(scale, place, own, marks, tool, total, new_tool, force):
    offset, speed = tool_step(tool, jnp.sum(total[...], axis=0), scale)
    new_tool[0:1] = offset
    new_tool[1:2] = speed
    state = [[own[f, c] for f in range(5)] for c in range(own.shape[1])]
    part = own_force(state, marks, offset, origin(place, *own.shape[1:3])[2])
    force[...] = jnp.broadcast_to(part[None], force.shape)


def last_kernel(near, place, own, found, marks, tool, total, sent):
    cols, rows, slots = own.shape[1:]
    size = 5 * cols * rows
    new = moved_state(own, found, marks, tool[0:1], origin(place, cols, rows)[2])
    sent[...] = jnp.zeros(sent.shape, F32)
    sent[:, size:, :] = jnp.broadcast_to(jnp.sum(total[...], axis=0, keepdims=True), (near, sent.shape[1] - size, slots))
    digit = lax.rem(place[3 + place[0]], near)
    for f in range(5):
        for c in range(cols):
            at = (f * cols + c) * rows
            sent[digit, at : at + rows] = new[c][f]


def sort_kernel(near, size, place, got, sent):
    far, most, slots = sent.shape
    group, digit = lax.div(place[0], near), lax.rem(place[0], near)
    sent[...] = jnp.zeros(sent.shape, F32)
    total = jnp.sum(got[:, size : size + 1, :], axis=0, keepdims=True)
    sent[:, size:, :] = jnp.broadcast_to(total, (far, most - size, slots))
    for k in range(near):
        target = place[3 + group * near + k]

        @pl.when(lax.rem(target, near) == digit)
        def _():
            sent[lax.div(target, near), 0:size] = got[k, 0:size]


def take_kernel(near, scale, place, got, tool, out, new_tool):
    cols, rows, slots = out.shape[1:]
    size = 5 * cols * rows
    source = 0
    for k in range(got.shape[0] * near):
        source = jnp.where(place[3 + k] == place[0], k // near, source)
    for f in range(5):
        for c in range(cols):
            at = (f * cols + c) * rows
            out[f, c] = got[source, at : at + rows]
    offset, speed = tool_step(tool, jnp.sum(got[:, size : size + 1, :], axis=0), scale)
    new_tool[0] = offset[0, 0]
    new_tool[1] = speed[0, 0]


def body(positions, velocity, density, counts, contact_mask, destination, tool):
    cols, rows, slots = density.shape
    ncut, ndepth = lax.axis_size("cut"), lax.axis_size("depth")
    here, depth = lax.axis_index("cut"), lax.axis_index("depth")
    scale = 1.0 / (ncut * cols * ndepth * rows * slots)
    place = jnp.concatenate([jnp.stack([here, depth, jnp.int32(ncut)]).astype(jnp.int32), destination])
    near = 8 if ncut % 8 == 0 else 1
    far = ncut // near
    size = 5 * cols * rows
    state, marking = shape(5, cols, rows, slots), shape(2, cols, rows, slots)
    message, vector = shape(ndepth, 32, slots), shape(2, slots)
    along_depth, along_plane, along_line = [shape(n, 1, slots) for n in (ndepth, 2 * ndepth, ncut // 2)]
    both = ("cut", "depth")
    pairs = range(0, ncut, 2)
    planes = [[(c + k) * ndepth + d for k in range(2) for d in range(ndepth)] for c in pairs]
    lines = [[(c + k) * ndepth + d for c in pairs] for k in range(2) for d in range(ndepth)]
    ring, ring_rates = shape(5, cols + 2, rows + 2, slots), shape(3, cols + 2, rows + 2, slots)
    swap = [(i, i ^ 1) for i in range(ncut)]
    cross = [(i, i + 1 if i % 2 else i - 1) for i in range(1, ncut - 1)]

    def scratch(wide, tall):
        return [pltpu.VMEM((n * 32, slots), F32) for n in (wide * tall, (wide - 2) * (tall - 2), (wide - 2) * (tall - 2))]

    def rates_of(kernel, out, arrays, wide, tall):
        return call(lambda place, *refs: kernel(place, (cols, rows), *refs), out, (place,), arrays, scratch(wide, tall), COST)

    def exchange(own, marks, sent):
        got = lax.all_to_all(sent, "depth", 0, 0, tiled=True)
        wide = call(extend_kernel, shape(6 * cols + 1, rows + 2 * HALO, slots), (place,), (own, marks, got))
        swapped, other = lax.ppermute(wide, "cut", swap), lax.ppermute(wide, "cut", cross)
        force = call(pair_force_kernel, along_line, (), (wide, swapped))
        total = lax.all_to_all(force, both, 0, 0, tiled=True, axis_index_groups=lines)
        found = rates_of(wide_rates_kernel, ring_rates, (wide, swapped, other), 3 * cols, rows + 4)
        return found, (wide, swapped, other), total

    own, marks, tool, sent = call(
        start_kernel, [state, marking, vector, message], (place, counts, contact_mask, tool), (positions, velocity, density)
    )
    found, around, total = exchange(own, marks, sent)
    own, ringed = call(first_update_kernel, [state, ring], (place,), (own, found, marks, *around, tool))

    found = rates_of(rates_kernel, shape(3, cols, rows, slots), (ringed,), cols + 2, rows + 2)
    kernel = functools.partial(second_update_kernel, scale)
    own, tool, sent = call(kernel, [state, vector, message], (place,), (own, found, marks, tool, total))

    found, around, total = exchange(own, marks, sent)
    kernel = functools.partial(third_update_kernel, scale)
    outs = [state, ring, vector, along_plane]
    new_own, ringed, tool, force = call(kernel, outs, (place,), (own, found, marks, *around, tool, total))
    own = new_own

    got = lax.all_to_all(force, both, 0, 0, tiled=True, axis_index_groups=planes)
    force = call(spread_kernel, along_line, (), (got,))
    total = lax.all_to_all(force, both, 0, 0, tiled=True, axis_index_groups=lines)
    found = rates_of(rates_kernel, shape(3, cols, rows, slots), (ringed,), cols + 2, rows + 2)
    kernel = functools.partial(last_force_kernel, scale)
    tool, force = call(kernel, [vector, along_depth], (place,), (own, marks, tool, total))
    total = lax.all_to_all(force, "depth", 0, 0, tiled=True)
    kernel = functools.partial(last_kernel, near)
    sent = call(kernel, shape(near, size + 8, slots), (place,), (own, found, marks, tool, total))
    close = [[g * near + k for k in range(near)] for g in range(far)]
    apart = [[g * near + k for g in range(far)] for k in range(near)]
    got = lax.all_to_all(sent, "cut", 0, 0, tiled=True, axis_index_groups=close)
    sent = call(functools.partial(sort_kernel, near, size), shape(far, size + 8, slots), (place,), (got,))
    got = lax.all_to_all(sent, "cut", 0, 0, tiled=True, axis_index_groups=apart)
    return pl.pallas_call(
        functools.partial(take_kernel, near, scale),
        out_shape=[state, shape(2)],
        in_specs=[SMEM, VMEM, VMEM],
        out_specs=[VMEM, SMEM],
        compiler_params=PARAMS,
    )(place, got, tool)


def solution(mesh):
    return jax.shard_map(
        body,
        mesh=mesh,
        in_specs=(
            P(None, "cut", "depth", None),
            P(None, "cut", "depth", None),
            P("cut", "depth", None),
            P("cut", "depth"),
            P("cut", "depth"),
            P(),
            P(),
        ),
        out_specs=(P(None, "cut", "depth", None), P()),
        check_vma=False,
    )
```

```python
import functools

import jax
import jax.numpy as jnp
from jax import lax
from jax.experimental import pallas as pl
from jax.experimental.pallas import tpu as pltpu
from jax.sharding import PartitionSpec as P

HALO = 2
MASS = 0.02
SOUND = 20.0
VISCOSITY = 2.0
STIFF = 50.0
DT = 0.05

FAR = 1.0e6

COST = 20_000_000_000

F32 = jnp.float32
BF16 = jnp.bfloat16
PARAMS = pltpu.CompilerParams(vmem_limit_bytes=40 * 1024 * 1024)
VMEM = pl.BlockSpec(memory_space=pltpu.VMEM)
SMEM = pl.BlockSpec(memory_space=pltpu.SMEM)


def shape(*dims):
    return jax.ShapeDtypeStruct(dims, F32)


def call(kernel, outs, scalars, arrays, scratch=(), estimate=0):
    return pl.pallas_call(
        kernel,
        out_shape=outs,
        in_specs=[SMEM] * len(scalars) + [VMEM] * len(arrays),
        out_specs=[VMEM] * len(outs) if isinstance(outs, list) else VMEM,
        scratch_shapes=scratch,
        compiler_params=PARAMS,
        cost_estimate=pl.CostEstimate(flops=estimate, bytes_accessed=1 << 20, transcendentals=0) if estimate else None,
    )(*scalars, *arrays)


def pressure(s):
    inv = 1.0 / s
    return SOUND * (s - 1.0) * inv * inv, inv


def penalties(x, touch, live, offset, column):
    return touch * live * jnp.maximum(0.0, x - column + offset - 0.5)


def own_force(new, marks, offset, first):
    total = 0.0
    for c, fields in enumerate(new):
        total = total + STIFF * penalties(fields[0], marks[1, c], marks[0, c], offset, first + c)
    total = jnp.sum(total, axis=0, keepdims=True)
    return jnp.broadcast_to(jnp.sum(total, axis=1, keepdims=True), total.shape)


def visible(fields, live, touch):
    alive = live > 0
    x, y, u, v, rho = fields
    return [jnp.where(alive, x, FAR), y, u, v, jnp.where(alive, rho, 1.0), live * touch]


def fill_depth(place, state, marks, force, sent):
    depth, ndepth = place[1], sent.shape[0]
    cols, rows = marks.shape[1:3]
    row = 6 * cols * HALO
    sent[...] = jnp.zeros(sent.shape, F32)
    sent[:, row : row + 1, :] = jnp.broadcast_to(force[None], (ndepth, 1, force.shape[1]))
    seen = [visible(state[c], marks[0, c], marks[1, c]) for c in range(cols)]

    def put(target, rim):
        for c in range(cols):
            for f in range(6):
                at = (f * cols + c) * HALO
                sent[target, at : at + HALO] = seen[c][f][rim : rim + HALO]

    @pl.when(depth > 0)
    def _():
        put(depth - 1, 0)

    @pl.when(depth < ndepth - 1)
    def _():
        put(depth + 1, rows - HALO)


def origin(place, cols, rows):
    first = (place[0] * cols).astype(F32)
    return first + 0.5 * cols, (place[1] * rows).astype(F32) + 0.5 * rows, first


def start_kernel(place, counts, contact, first_tool, positions, velocity, density, own, marks, tool, sent, arrived):
    cols, rows, slots = density.shape
    parts = [(positions, own.at[0:2]), (velocity, own.at[2:4]), (density, own.at[4])]
    copies = [pltpu.make_async_copy(part, to, arrived.at[n]) for n, (part, to) in enumerate(parts)]
    for copy in copies:
        copy.start()
    row = lax.broadcasted_iota(jnp.int32, (rows, slots), 0)
    slot = lax.broadcasted_iota(jnp.int32, (rows, slots), 1)
    for c in range(cols):
        filled = jnp.zeros((rows, slots), jnp.int32)
        touch = jnp.zeros((rows, slots), jnp.int32)
        for r in range(rows):
            filled = jnp.where(row == r, counts[c, r], filled)
            touch = jnp.where(row == r, contact[c, r], touch)
        marks[0, c] = jnp.where(slot < filled, 1.0, 0.0)
        marks[1, c] = touch.astype(F32)
    for copy in copies:
        copy.wait()
    new = [[own[f, c] for f in range(5)] for c in range(cols)]
    offset = jnp.zeros((1, slots), F32) + first_tool[0]
    tool[0:1] = offset
    tool[1:2] = jnp.zeros((1, slots), F32) + first_tool[1]
    fill_depth(place, new, marks, own_force(new, marks, offset, origin(place, cols, rows)[2]), sent)


def extend_kernel(place, own, marks, got, inner, wide):
    depth, ndepth = place[1], got.shape[0]
    cols, rows = own.shape[1:3]
    above = got[jnp.maximum(depth - 1, 0)]
    below = got[jnp.minimum(depth + 1, ndepth - 1)]
    blank = [FAR, 0.0, 0.0, 0.0, 1.0, 0.0]
    for c in range(cols):
        seen = visible([own[f, c] for f in range(5)], marks[0, c], marks[1, c])
        for f in range(6):
            at = (f * cols + c) * HALO
            wide[f * cols + c, 0:HALO] = jnp.where(depth > 0, above[at : at + HALO], blank[f])
            wide[f * cols + c, HALO : rows + HALO] = seen[f]
            wide[f * cols + c, rows + HALO :] = jnp.where(depth < ndepth - 1, below[at : at + HALO], blank[f])
    row = 6 * cols * HALO
    wide[6 * cols] = jnp.broadcast_to(jnp.sum(got[:, row : row + 1, :], axis=0), wide.shape[1:])


def pair_force_kernel(wide, swapped, force):
    last = wide.shape[0] - 1
    force[...] = jnp.broadcast_to((wide[last, 0:1] + swapped[last, 0:1])[None], force.shape)


def spread_kernel(got, force):
    force[...] = jnp.broadcast_to(jnp.sum(got[...], axis=0, keepdims=True), force.shape)


def pair_sums(columns, center, pairs, out, feat, acc2, acc3, earlier=None):
    x0, y0, _ = center
    tall, slots = columns[0][0].shape
    row0 = min(r for _, r in pairs)
    rows = 1 + max(r for _, r in pairs) - row0
    for c, (x, y, u, v, s) in enumerate(columns):
        lx, ly = x - x0, y - y0
        press, inv = pressure(s)
        parts = [jnp.ones_like(x), press, u, v, u * lx + v * ly]
        for part in (lx, ly, press * lx, press * ly):
            high = part.astype(BF16).astype(F32)
            parts += [high, part - high]
        parts += [inv, inv * u, inv * v]
        for k, part in enumerate(parts):
            feat[pl.ds(c * tall * 16 + k, tall, stride=16), :] = part
    for i, ((c, r), around) in enumerate(pairs.items()):
        xi, yi = [jnp.broadcast_to(f[r : r + 1], (slots, slots)).T for f in columns[c][:2]]

        def weights(a, b):
            dx = (xi - columns[a][0][b : b + 1]).astype(BF16)
            dy = (yi - columns[a][1][b : b + 1]).astype(BF16)
            q = jnp.maximum(BF16(0.0), BF16(1.0) - dx * dx - dy * dy)
            q2 = q * q
            return jnp.concatenate([q2, q2 * q], axis=0)

        total = None
        for n in range(0, len(around), 2):
            pair = around[n : n + 2]
            w = jnp.concatenate([weights(a, b) for a, b in pair], axis=1)
            f = jnp.concatenate([feat[pl.ds((a * tall + b) * 16, 16), :] for a, b in pair], axis=1).astype(BF16)
            found = lax.dot_general(f, w, (((1,), (1,)), ((), ())), preferred_element_type=F32)
            total = found if total is None else total + found
        acc2[i * 16 : (i + 1) * 16] = total[:, :slots]
        acc3[i * 16 : (i + 1) * 16] = total[:, slots:]

    for n, c in enumerate(sorted({c for c, _ in pairs})):

        def summed(k):
            return (acc2 if k < 13 else acc3)[pl.ds(n * rows * 16 + k, rows, stride=16), :]

        x, y, u, v, s = [f[row0 : row0 + rows] for f in columns[c]]
        x, y = x - x0, y - y0
        press, _ = pressure(s)
        a0, ap, au, av, aw = [summed(k) for k in range(5)]
        ax, ay, apx, apy = [summed(k) + summed(k + 1) for k in range(5, 13, 2)]
        b0, bu, bv = [summed(k) for k in range(13, 16)]
        sx, sy = x * a0 - ax, y * a0 - ay
        rates = [
            (6.0 * MASS) * (press * sx + x * ap - apx) - (VISCOSITY * MASS) * (u * b0 - bu),
            (6.0 * MASS) * (press * sy + y * ap - apy) - (VISCOSITY * MASS) * (v * b0 - bv),
            (-6.0 * MASS) * (u * sx + v * sy - x * au - y * av + aw),
        ]
        for f in range(3):
            out[f, n] = rates[f]
            if earlier is not None and 0 < n <= earlier.shape[1]:
                inner = earlier[f, n - 1]
                out[f, n, 1 : rows - 1] = rates[f][1 : rows - 1] + inner


def around_cell(c, r):
    return [(c + a, r + b) for a in (-1, 0, 1) for b in (-1, 0, 1)]


def inner_rates_kernel(place, size, own, marks, out, feat, acc2, acc3):
    cols, rows = size
    columns = [visible([own[f, c] for f in range(5)], marks[0, c], marks[1, c])[:5] for c in range(cols)]
    cells = [(c, r) for c in range(cols) for r in range(rows)]
    pairs = {cell: [j for j in around_cell(*cell) if j in cells] for cell in cells}
    pair_sums(columns, origin(place, *size), pairs, out, feat, acc2, acc3)


def wide_columns(place, cols, wide, swapped, other):
    even = lax.rem(place[0], 2) == 0
    blank = [FAR, 0.0, 0.0, 0.0, 1.0, 0.0]
    columns = []
    for side in range(3):
        outside = place[0] == (0 if side == 0 else place[2] - 1)
        for c in range(cols):
            if side == 1:
                fields = [wide[f * cols + c] for f in range(6)]
            else:
                first, second = (other, swapped) if side == 0 else (swapped, other)
                fields = [jnp.where(outside, blank[f], jnp.where(even, first[f * cols + c], second[f * cols + c])) for f in range(6)]
            columns.append(fields)
    return columns


def wide_rates_kernel(place, size, wide, swapped, other, inner, out, feat, acc2, acc3):
    cols, rows = size
    columns = [fields[:5] for fields in wide_columns(place, cols, wide, swapped, other)]
    block = [(c + cols, r + HALO) for c in range(cols) for r in range(rows)]
    pairs = {}
    for c in range(1, 3 * cols - 1):
        for r in range(1, rows + 3):
            pairs[c, r] = [j for j in around_cell(c, r) if (c, r) not in block or j not in block]
    pair_sums(columns, origin(place, *size), pairs, out, feat, acc2, acc3, inner)


def rates_kernel(place, size, ring, out, feat, acc2, acc3):
    cols, rows = size
    columns = [[ring[f, c] for f in range(5)] for c in range(cols + 2)]
    pairs = {(c, r): around_cell(c, r) for c in range(1, cols + 1) for r in range(1, rows + 1)}
    pair_sums(columns, origin(place, *size), pairs, out, feat, acc2, acc3)


def moved_ring(place, columns, found, offset, first, ring):
    for n in range(ring.shape[1]):
        x, y, u, v, s, touch = [f[1:-1] for f in columns[n + 1]]
        live = jnp.where(x < 0.5 * FAR, 1.0, 0.0)
        pen = touch * jnp.maximum(0.0, x - (first + (n - 1)) + offset - 0.5)
        u = u + DT * live * (found[0, n] - STIFF * pen)
        v = v + DT * live * found[1, n]
        ring[0, n] = x + DT * live * u
        ring[1, n] = y + DT * live * v
        ring[2, n] = u
        ring[3, n] = v
        ring[4, n] = s + DT * live * found[2, n]


def moved_state(own, found, marks, offset, first):
    cols, rows = own.shape[1:3]
    side, rim = (found.shape[1] - cols) // 2, (found.shape[2] - rows) // 2
    new = []
    for c in range(cols):
        live = marks[0, c]
        ax, ay, drho = [found[f, c + side][rim : rim + rows] for f in range(3)]
        pen = penalties(own[0, c], marks[1, c], live, offset, first + c)
        u = own[2, c] + DT * live * (ax - STIFF * pen)
        v = own[3, c] + DT * live * ay
        x = own[0, c] + DT * live * u
        y = own[1, c] + DT * live * v
        rho = own[4, c] + DT * live * drho
        new.append([x, y, u, v, rho])
    return new


def keep(new, own):
    for c, fields in enumerate(new):
        for f in range(5):
            own[f, c] = fields[f]


def tool_step(tool, force, scale):
    speed = tool[1:2] + DT * (1.0 - force * scale)
    return tool[0:1] + DT * speed, speed


def first_update_kernel(place, own, found, marks, wide, swapped, other, tool, new_own, ring):
    first = origin(place, *own.shape[1:3])[2]
    keep(moved_state(own, found, marks, tool[0:1], first), new_own)
    moved_ring(place, wide_columns(place, own.shape[1], wide, swapped, other), found, tool[0:1], first, ring)


def second_update_kernel(scale, place, own, found, marks, tool, total, new_own, new_tool, sent):
    first = origin(place, *own.shape[1:3])[2]
    offset, speed = tool_step(tool, jnp.sum(total[...], axis=0), scale)
    new_tool[0:1] = offset
    new_tool[1:2] = speed
    state = [[own[f, c] for f in range(5)] for c in range(own.shape[1])]
    new = moved_state(own, found, marks, offset, first)
    keep(new, new_own)
    fill_depth(place, new, marks, own_force(state, marks, offset, first), sent)


def third_update_kernel(scale, place, own, found, marks, wide, swapped, other, tool, total, new_own, ring, new_tool, force):
    first = origin(place, *own.shape[1:3])[2]
    offset, speed = tool_step(tool, jnp.sum(total[...], axis=0), scale)
    new_tool[0:1] = offset
    new_tool[1:2] = speed
    state = [[own[f, c] for f in range(5)] for c in range(own.shape[1])]
    force[...] = jnp.broadcast_to(own_force(state, marks, offset, first)[None], force.shape)
    keep(moved_state(own, found, marks, offset, first), new_own)
    moved_ring(place, wide_columns(place, own.shape[1], wide, swapped, other), found, offset, first, ring)


def last_force_kernel(scale, place, own, marks, tool, total, new_tool, force):
    offset, speed = tool_step(tool, jnp.sum(total[...], axis=0), scale)
    new_tool[0:1] = offset
    new_tool[1:2] = speed
    state = [[own[f, c] for f in range(5)] for c in range(own.shape[1])]
    part = own_force(state, marks, offset, origin(place, *own.shape[1:3])[2])
    force[...] = jnp.broadcast_to(part[None], force.shape)


def last_kernel(near, place, own, found, marks, tool, total, sent):
    cols, rows, slots = own.shape[1:]
    size = 5 * cols * rows
    new = moved_state(own, found, marks, tool[0:1], origin(place, cols, rows)[2])
    sent[...] = jnp.zeros(sent.shape, F32)
    sent[:, size:, :] = jnp.broadcast_to(jnp.sum(total[...], axis=0, keepdims=True), (near, sent.shape[1] - size, slots))
    digit = lax.rem(place[3 + place[0]], near)
    for f in range(5):
        for c in range(cols):
            at = (f * cols + c) * rows
            sent[digit, at : at + rows] = new[c][f]


def sort_kernel(near, size, place, got, sent):
    far, most, slots = sent.shape
    group, digit = lax.div(place[0], near), lax.rem(place[0], near)
    sent[...] = jnp.zeros(sent.shape, F32)
    total = jnp.sum(got[:, size : size + 1, :], axis=0, keepdims=True)
    sent[:, size:, :] = jnp.broadcast_to(total, (far, most - size, slots))
    for k in range(near):
        target = place[3 + group * near + k]

        @pl.when(lax.rem(target, near) == digit)
        def _():
            sent[lax.div(target, near), 0:size] = got[k, 0:size]


def take_kernel(near, scale, place, got, tool, out, new_tool):
    cols, rows, slots = out.shape[1:]
    size = 5 * cols * rows
    source = 0
    for k in range(got.shape[0] * near):
        source = jnp.where(place[3 + k] == place[0], k // near, source)
    for f in range(5):
        for c in range(cols):
            at = (f * cols + c) * rows
            out[f, c] = got[source, at : at + rows]
    offset, speed = tool_step(tool, jnp.sum(got[:, size : size + 1, :], axis=0), scale)
    new_tool[0] = offset[0, 0]
    new_tool[1] = speed[0, 0]


def body(positions, velocity, density, counts, contact_mask, destination, tool):
    cols, rows, slots = density.shape
    ncut, ndepth = lax.axis_size("cut"), lax.axis_size("depth")
    here, depth = lax.axis_index("cut"), lax.axis_index("depth")
    scale = 1.0 / (ncut * cols * ndepth * rows * slots)
    place = jnp.concatenate([jnp.stack([here, depth, jnp.int32(ncut)]).astype(jnp.int32), destination])
    near = 8 if ncut % 8 == 0 else 1
    far = ncut // near
    size = 5 * cols * rows
    state, marking = shape(5, cols, rows, slots), shape(2, cols, rows, slots)
    message, vector = shape(ndepth, 32, slots), shape(2, slots)
    along_depth, along_plane, along_line = [shape(n, 1, slots) for n in (ndepth, 2 * ndepth, ncut // 2)]
    both = ("cut", "depth")
    pairs = range(0, ncut, 2)
    planes = [[(c + k) * ndepth + d for k in range(2) for d in range(ndepth)] for c in pairs]
    lines = [[(c + k) * ndepth + d for c in pairs] for k in range(2) for d in range(ndepth)]
    ring, ring_rates = shape(5, cols + 2, rows + 2, slots), shape(3, cols + 2, rows + 2, slots)
    block_rates = shape(3, cols, rows, slots)
    swap = [(i, i ^ 1) for i in range(ncut)]
    cross = [(i, i + 1 if i % 2 else i - 1) for i in range(1, ncut - 1)]

    def rates_of(kernel, out, arrays, read, summed):
        scratch = [pltpu.VMEM((n * 16, slots), F32) for n in (read, summed, summed)]
        return call(lambda place, *refs: kernel(place, (cols, rows), *refs), out, (place,), arrays, scratch, COST)

    def exchange(own, marks, sent):
        got = lax.all_to_all(sent, "depth", 0, 0, tiled=True)
        inner = rates_of(inner_rates_kernel, block_rates, (own, marks), cols * rows, cols * rows)
        wide = call(extend_kernel, shape(6 * cols + 1, rows + 2 * HALO, slots), (place,), (own, marks, got, inner))
        swapped, other = lax.ppermute(wide, "cut", swap), lax.ppermute(wide, "cut", cross)
        force = call(pair_force_kernel, along_line, (), (wide, swapped))
        total = lax.all_to_all(force, both, 0, 0, tiled=True, axis_index_groups=lines)
        found = rates_of(wide_rates_kernel, ring_rates, (wide, swapped, other, inner), 3 * cols * (rows + 4), (cols + 2) * (rows + 2))
        return found, (wide, swapped, other), total

    own, marks, tool, sent = pl.pallas_call(
        start_kernel,
        out_shape=[state, marking, vector, message],
        in_specs=[SMEM] * 4 + [pl.BlockSpec(memory_space=pl.ANY)] * 3,
        out_specs=[VMEM] * 4,
        scratch_shapes=[pltpu.SemaphoreType.DMA((3,))],
        compiler_params=pltpu.CompilerParams(vmem_limit_bytes=60 * 1024 * 1024),
    )(place, counts, contact_mask, tool, positions, velocity, density)
    found, around, total = exchange(own, marks, sent)
    own, ringed = call(first_update_kernel, [state, ring], (place,), (own, found, marks, *around, tool))

    found = rates_of(rates_kernel, block_rates, (ringed,), (cols + 2) * (rows + 2), cols * rows)
    kernel = functools.partial(second_update_kernel, scale)
    own, tool, sent = call(kernel, [state, vector, message], (place,), (own, found, marks, tool, total))

    found, around, total = exchange(own, marks, sent)
    kernel = functools.partial(third_update_kernel, scale)
    outs = [state, ring, vector, along_plane]
    new_own, ringed, tool, force = call(kernel, outs, (place,), (own, found, marks, *around, tool, total))
    own = new_own

    got = lax.all_to_all(force, both, 0, 0, tiled=True, axis_index_groups=planes)
    force = call(spread_kernel, along_line, (), (got,))
    total = lax.all_to_all(force, both, 0, 0, tiled=True, axis_index_groups=lines)
    found = rates_of(rates_kernel, block_rates, (ringed,), (cols + 2) * (rows + 2), cols * rows)
    kernel = functools.partial(last_force_kernel, scale)
    tool, force = call(kernel, [vector, along_depth], (place,), (own, marks, tool, total))
    total = lax.all_to_all(force, "depth", 0, 0, tiled=True)
    kernel = functools.partial(last_kernel, near)
    sent = call(kernel, shape(near, size + 8, slots), (place,), (own, found, marks, tool, total))
    close = [[g * near + k for k in range(near)] for g in range(far)]
    apart = [[g * near + k for g in range(far)] for k in range(near)]
    got = lax.all_to_all(sent, "cut", 0, 0, tiled=True, axis_index_groups=close)
    sent = call(functools.partial(sort_kernel, near, size), shape(far, size + 8, slots), (place,), (got,))
    got = lax.all_to_all(sent, "cut", 0, 0, tiled=True, axis_index_groups=apart)
    return pl.pallas_call(
        functools.partial(take_kernel, near, scale),
        out_shape=[state, shape(2)],
        in_specs=[SMEM, VMEM, VMEM],
        out_specs=[VMEM, SMEM],
        compiler_params=PARAMS,
    )(place, got, tool)


def solution(mesh):
    return jax.shard_map(
        body,
        mesh=mesh,
        in_specs=(
            P(None, "cut", "depth", None),
            P(None, "cut", "depth", None),
            P("cut", "depth", None),
            P("cut", "depth"),
            P("cut", "depth"),
            P(),
            P(),
        ),
        out_specs=(P(None, "cut", "depth", None), P()),
        check_vma=False,
    )
```

```python
import functools

import jax
import jax.numpy as jnp
from jax import lax
from jax.experimental import pallas as pl
from jax.experimental.pallas import tpu as pltpu
from jax.sharding import PartitionSpec as P

HALO = 2
MASS = 0.02
SOUND = 20.0
VISCOSITY = 2.0
STIFF = 50.0
DT = 0.05

FAR = 1.0e6

COST = 20_000_000_000

F32 = jnp.float32
BF16 = jnp.bfloat16
PARAMS = pltpu.CompilerParams(vmem_limit_bytes=40 * 1024 * 1024)
VMEM = pl.BlockSpec(memory_space=pltpu.VMEM)
SMEM = pl.BlockSpec(memory_space=pltpu.SMEM)


def here():
    return lax.axis_index("cut")


def row_block():
    return lax.axis_index("depth")


def shape(*dims):
    return jax.ShapeDtypeStruct(dims, F32)


def call(kernel, outs, scalars, arrays, scratch=(), estimate=0):
    return pl.pallas_call(
        kernel,
        out_shape=outs,
        in_specs=[SMEM] * len(scalars) + [VMEM] * len(arrays),
        out_specs=[VMEM] * len(outs) if isinstance(outs, list) else VMEM,
        scratch_shapes=scratch,
        compiler_params=PARAMS,
        cost_estimate=pl.CostEstimate(flops=estimate, bytes_accessed=1 << 20, transcendentals=0) if estimate else None,
    )(*scalars, *arrays)


def pressure(s):
    inv = 1.0 / s
    return SOUND * (s - 1.0) * inv * inv, inv


def penalties(x, touch, live, offset, column):
    return touch * live * jnp.maximum(0.0, x - column + offset - 0.5)


def own_force(new, marks, offset, first):
    total = 0.0
    for c, fields in enumerate(new):
        total = total + STIFF * penalties(fields[0], marks[1, c], marks[0, c], offset, first + c)
    total = jnp.sum(total, axis=0, keepdims=True)
    return jnp.broadcast_to(jnp.sum(total, axis=1, keepdims=True), total.shape)


def visible(fields, live, touch):
    alive = live > 0
    x, y, u, v, rho = fields
    return [jnp.where(alive, x, FAR), y, u, v, jnp.where(alive, rho, 1.0), live * touch]


def fill_depth(state, marks, force, sent):
    depth, ndepth = row_block(), sent.shape[0]
    cols, rows = marks.shape[1:3]
    row = 6 * cols * HALO
    sent[...] = jnp.zeros(sent.shape, F32)
    sent[:, row : row + 1, :] = jnp.broadcast_to(force[None], (ndepth, 1, force.shape[1]))
    seen = [visible(state[c], marks[0, c], marks[1, c]) for c in range(cols)]

    def put(target, rim):
        for c in range(cols):
            for f in range(6):
                at = (f * cols + c) * HALO
                sent[target, at : at + HALO] = seen[c][f][rim : rim + HALO]

    @pl.when(depth > 0)
    def _():
        put(depth - 1, 0)

    @pl.when(depth < ndepth - 1)
    def _():
        put(depth + 1, rows - HALO)


def origin(cols, rows):
    first = (here() * cols).astype(F32)
    return first + 0.5 * cols, (row_block() * rows).astype(F32) + 0.5 * rows, first


def start_kernel(counts, contact, first_tool, positions, velocity, density, own, marks, tool, sent, arrived):
    cols, rows, slots = density.shape
    parts = [(positions, own.at[0:2]), (velocity, own.at[2:4]), (density, own.at[4])]
    copies = [pltpu.make_async_copy(part, to, arrived.at[n]) for n, (part, to) in enumerate(parts)]
    for copy in copies:
        copy.start()
    row = lax.broadcasted_iota(jnp.int32, (rows, slots), 0)
    slot = lax.broadcasted_iota(jnp.int32, (rows, slots), 1)
    for c in range(cols):
        filled = jnp.zeros((rows, slots), jnp.int32)
        touch = jnp.zeros((rows, slots), jnp.int32)
        for r in range(rows):
            filled = jnp.where(row == r, counts[c, r], filled)
            touch = jnp.where(row == r, contact[c, r], touch)
        marks[0, c] = jnp.where(slot < filled, 1.0, 0.0)
        marks[1, c] = touch.astype(F32)
    for copy in copies:
        copy.wait()
    new = [[own[f, c] for f in range(5)] for c in range(cols)]
    offset = jnp.zeros((1, slots), F32) + first_tool[0]
    tool[0:1] = offset
    tool[1:2] = jnp.zeros((1, slots), F32) + first_tool[1]
    fill_depth(new, marks, own_force(new, marks, offset, origin(cols, rows)[2]), sent)


def extend_kernel(own, marks, got, inner, wide):
    depth, ndepth = row_block(), got.shape[0]
    cols, rows = own.shape[1:3]
    above = got[jnp.maximum(depth - 1, 0)]
    below = got[jnp.minimum(depth + 1, ndepth - 1)]
    blank = [FAR, 0.0, 0.0, 0.0, 1.0, 0.0]
    for c in range(cols):
        seen = visible([own[f, c] for f in range(5)], marks[0, c], marks[1, c])
        for f in range(6):
            at = (f * cols + c) * HALO
            wide[f * cols + c, 0:HALO] = jnp.where(depth > 0, above[at : at + HALO], blank[f])
            wide[f * cols + c, HALO : rows + HALO] = seen[f]
            wide[f * cols + c, rows + HALO :] = jnp.where(depth < ndepth - 1, below[at : at + HALO], blank[f])
    row = 6 * cols * HALO
    wide[6 * cols] = jnp.broadcast_to(jnp.sum(got[:, row : row + 1, :], axis=0), wide.shape[1:])


def pair_force_kernel(wide, swapped, force):
    last = wide.shape[0] - 1
    force[...] = jnp.broadcast_to((wide[last, 0:1] + swapped[last, 0:1])[None], force.shape)


def spread_kernel(got, force):
    force[...] = jnp.broadcast_to(jnp.sum(got[...], axis=0, keepdims=True), force.shape)


def pair_sums(columns, center, pairs, out, feat, acc2, acc3, earlier=None):
    x0, y0, _ = center
    tall, slots = columns[0][0].shape
    row0 = min(r for _, r in pairs)
    rows = 1 + max(r for _, r in pairs) - row0
    for c, (x, y, u, v, s) in enumerate(columns):
        lx, ly = x - x0, y - y0
        press, inv = pressure(s)
        parts = [jnp.ones_like(x), press, u, v, u * lx + v * ly]
        for part in (lx, ly, press * lx, press * ly):
            high = part.astype(BF16).astype(F32)
            parts += [high, part - high]
        parts += [inv, inv * u, inv * v]
        for k, part in enumerate(parts):
            feat[pl.ds(c * tall * 16 + k, tall, stride=16), :] = part
    for i, ((c, r), around) in enumerate(pairs.items()):
        xi, yi = [jnp.broadcast_to(f[r : r + 1], (slots, slots)).T for f in columns[c][:2]]

        def weights(a, b):
            dx = (xi - columns[a][0][b : b + 1]).astype(BF16)
            dy = (yi - columns[a][1][b : b + 1]).astype(BF16)
            q = jnp.maximum(BF16(0.0), BF16(1.0) - dx * dx - dy * dy)
            q2 = q * q
            return jnp.concatenate([q2, q2 * q], axis=0)

        total = None
        for n in range(0, len(around), 2):
            pair = around[n : n + 2]
            w = jnp.concatenate([weights(a, b) for a, b in pair], axis=1)
            f = jnp.concatenate([feat[pl.ds((a * tall + b) * 16, 16), :] for a, b in pair], axis=1).astype(BF16)
            found = lax.dot_general(f, w, (((1,), (1,)), ((), ())), preferred_element_type=F32)
            total = found if total is None else total + found
        acc2[i * 16 : (i + 1) * 16] = total[:, :slots]
        acc3[i * 16 : (i + 1) * 16] = total[:, slots:]

    for n, c in enumerate(sorted({c for c, _ in pairs})):

        def summed(k):
            return (acc2 if k < 13 else acc3)[pl.ds(n * rows * 16 + k, rows, stride=16), :]

        x, y, u, v, s = [f[row0 : row0 + rows] for f in columns[c]]
        x, y = x - x0, y - y0
        press, _ = pressure(s)
        a0, ap, au, av, aw = [summed(k) for k in range(5)]
        ax, ay, apx, apy = [summed(k) + summed(k + 1) for k in range(5, 13, 2)]
        b0, bu, bv = [summed(k) for k in range(13, 16)]
        sx, sy = x * a0 - ax, y * a0 - ay
        rates = [
            (6.0 * MASS) * (press * sx + x * ap - apx) - (VISCOSITY * MASS) * (u * b0 - bu),
            (6.0 * MASS) * (press * sy + y * ap - apy) - (VISCOSITY * MASS) * (v * b0 - bv),
            (-6.0 * MASS) * (u * sx + v * sy - x * au - y * av + aw),
        ]
        for f in range(3):
            out[f, n] = rates[f]
            if earlier is not None and 0 < n <= earlier.shape[1]:
                inner = earlier[f, n - 1]
                out[f, n, 1 : rows - 1] = rates[f][1 : rows - 1] + inner


def around_cell(c, r):
    return [(c + a, r + b) for a in (-1, 0, 1) for b in (-1, 0, 1)]


def inner_rates_kernel(size, own, marks, out, feat, acc2, acc3):
    cols, rows = size
    columns = [visible([own[f, c] for f in range(5)], marks[0, c], marks[1, c])[:5] for c in range(cols)]
    cells = [(c, r) for c in range(cols) for r in range(rows)]
    pairs = {cell: [j for j in around_cell(*cell) if j in cells] for cell in cells}
    pair_sums(columns, origin(*size), pairs, out, feat, acc2, acc3)


def wide_columns(cols, wide, swapped, other):
    even = lax.rem(here(), 2) == 0
    blank = [FAR, 0.0, 0.0, 0.0, 1.0, 0.0]
    columns = []
    for side in range(3):
        outside = here() == (0 if side == 0 else lax.axis_size("cut") - 1)
        for c in range(cols):
            if side == 1:
                fields = [wide[f * cols + c] for f in range(6)]
            else:
                first, second = (other, swapped) if side == 0 else (swapped, other)
                fields = [jnp.where(outside, blank[f], jnp.where(even, first[f * cols + c], second[f * cols + c])) for f in range(6)]
            columns.append(fields)
    return columns


def wide_rates_kernel(size, wide, swapped, other, inner, out, feat, acc2, acc3):
    cols, rows = size
    columns = [fields[:5] for fields in wide_columns(cols, wide, swapped, other)]
    block = [(c + cols, r + HALO) for c in range(cols) for r in range(rows)]
    pairs = {}
    for c in range(1, 3 * cols - 1):
        for r in range(1, rows + 3):
            pairs[c, r] = [j for j in around_cell(c, r) if (c, r) not in block or j not in block]
    pair_sums(columns, origin(*size), pairs, out, feat, acc2, acc3, inner)


def rates_kernel(size, ring, out, feat, acc2, acc3):
    cols, rows = size
    columns = [[ring[f, c] for f in range(5)] for c in range(cols + 2)]
    pairs = {(c, r): around_cell(c, r) for c in range(1, cols + 1) for r in range(1, rows + 1)}
    pair_sums(columns, origin(*size), pairs, out, feat, acc2, acc3)


def moved_ring(columns, found, offset, first, ring):
    for n in range(ring.shape[1]):
        x, y, u, v, s, touch = [f[1:-1] for f in columns[n + 1]]
        live = jnp.where(x < 0.5 * FAR, 1.0, 0.0)
        pen = touch * jnp.maximum(0.0, x - (first + (n - 1)) + offset - 0.5)
        u = u + DT * live * (found[0, n] - STIFF * pen)
        v = v + DT * live * found[1, n]
        ring[0, n] = x + DT * live * u
        ring[1, n] = y + DT * live * v
        ring[2, n] = u
        ring[3, n] = v
        ring[4, n] = s + DT * live * found[2, n]


def moved_state(own, found, marks, offset, first):
    cols, rows = own.shape[1:3]
    side, rim = (found.shape[1] - cols) // 2, (found.shape[2] - rows) // 2
    new = []
    for c in range(cols):
        live = marks[0, c]
        ax, ay, drho = [found[f, c + side][rim : rim + rows] for f in range(3)]
        pen = penalties(own[0, c], marks[1, c], live, offset, first + c)
        u = own[2, c] + DT * live * (ax - STIFF * pen)
        v = own[3, c] + DT * live * ay
        x = own[0, c] + DT * live * u
        y = own[1, c] + DT * live * v
        rho = own[4, c] + DT * live * drho
        new.append([x, y, u, v, rho])
    return new


def keep(new, own):
    for c, fields in enumerate(new):
        for f in range(5):
            own[f, c] = fields[f]


def tool_step(tool, force, scale):
    speed = tool[1:2] + DT * (1.0 - force * scale)
    return tool[0:1] + DT * speed, speed


def first_update_kernel(size, own, found, marks, wide, swapped, other, tool, new_own, out, feat, acc2, acc3, ring):
    first = origin(*size)[2]
    keep(moved_state(own, found, marks, tool[0:1], first), new_own)
    moved_ring(wide_columns(size[0], wide, swapped, other), found, tool[0:1], first, ring)
    rates_kernel(size, ring, out, feat, acc2, acc3)


def second_update_kernel(scale, own, found, marks, tool, total, new_own, new_tool, sent):
    first = origin(*own.shape[1:3])[2]
    offset, speed = tool_step(tool, jnp.sum(total[...], axis=0), scale)
    new_tool[0:1] = offset
    new_tool[1:2] = speed
    state = [[own[f, c] for f in range(5)] for c in range(own.shape[1])]
    new = moved_state(own, found, marks, offset, first)
    keep(new, new_own)
    fill_depth(new, marks, own_force(state, marks, offset, first), sent)


def third_update_kernel(scale, own, found, marks, wide, swapped, other, tool, total, new_own, ring, new_tool, force):
    first = origin(*own.shape[1:3])[2]
    offset, speed = tool_step(tool, jnp.sum(total[...], axis=0), scale)
    new_tool[0:1] = offset
    new_tool[1:2] = speed
    state = [[own[f, c] for f in range(5)] for c in range(own.shape[1])]
    force[...] = jnp.broadcast_to(own_force(state, marks, offset, first)[None], force.shape)
    keep(moved_state(own, found, marks, offset, first), new_own)
    moved_ring(wide_columns(own.shape[1], wide, swapped, other), found, offset, first, ring)


def last_force_kernel(scale, own, marks, tool, total, new_tool, force):
    offset, speed = tool_step(tool, jnp.sum(total[...], axis=0), scale)
    new_tool[0:1] = offset
    new_tool[1:2] = speed
    state = [[own[f, c] for f in range(5)] for c in range(own.shape[1])]
    part = own_force(state, marks, offset, origin(*own.shape[1:3])[2])
    force[...] = jnp.broadcast_to(part[None], force.shape)


def last_kernel(near, destination, own, found, marks, tool, total, sent):
    cols, rows, slots = own.shape[1:]
    size = 5 * cols * rows
    new = moved_state(own, found, marks, tool[0:1], origin(cols, rows)[2])
    sent[...] = jnp.zeros(sent.shape, F32)
    sent[:, size:, :] = jnp.broadcast_to(jnp.sum(total[...], axis=0, keepdims=True), (near, sent.shape[1] - size, slots))
    digit = lax.rem(destination[here()], near)
    for f in range(5):
        for c in range(cols):
            at = (f * cols + c) * rows
            sent[digit, at : at + rows] = new[c][f]


def sort_kernel(near, size, destination, got, sent):
    far, most, slots = sent.shape
    group, digit = lax.div(here(), near), lax.rem(here(), near)
    sent[...] = jnp.zeros(sent.shape, F32)
    total = jnp.sum(got[:, size : size + 1, :], axis=0, keepdims=True)
    sent[:, size:, :] = jnp.broadcast_to(total, (far, most - size, slots))
    for k in range(near):
        target = destination[group * near + k]

        @pl.when(lax.rem(target, near) == digit)
        def _():
            sent[lax.div(target, near), 0:size] = got[k, 0:size]


def take_kernel(near, scale, destination, got, tool, out, new_tool):
    cols, rows, slots = out.shape[1:]
    size = 5 * cols * rows
    source = 0
    for k in range(got.shape[0] * near):
        source = jnp.where(destination[k] == here(), k // near, source)
    for f in range(5):
        for c in range(cols):
            at = (f * cols + c) * rows
            out[f, c] = got[source, at : at + rows]
    offset, speed = tool_step(tool, jnp.sum(got[:, size : size + 1, :], axis=0), scale)
    new_tool[0] = offset[0, 0]
    new_tool[1] = speed[0, 0]


def body(positions, velocity, density, counts, contact_mask, destination, tool):
    cols, rows, slots = density.shape
    ncut, ndepth = lax.axis_size("cut"), lax.axis_size("depth")
    scale = 1.0 / (ncut * cols * ndepth * rows * slots)
    near = 8 if ncut % 8 == 0 else 1
    far = ncut // near
    size = 5 * cols * rows
    state, marking = shape(5, cols, rows, slots), shape(2, cols, rows, slots)
    message, vector = shape(ndepth, 32, slots), shape(2, slots)
    along_depth, along_plane, along_line = [shape(n, 1, slots) for n in (ndepth, 2 * ndepth, ncut // 2)]
    both = ("cut", "depth")
    pairs = range(0, ncut, 2)
    planes = [[(c + k) * ndepth + d for k in range(2) for d in range(ndepth)] for c in pairs]
    lines = [[(c + k) * ndepth + d for c in pairs] for k in range(2) for d in range(ndepth)]
    ring, ring_rates = shape(5, cols + 2, rows + 2, slots), shape(3, cols + 2, rows + 2, slots)
    block_rates = shape(3, cols, rows, slots)
    swap = [(i, i ^ 1) for i in range(ncut)]
    cross = [(i, i + 1 if i % 2 else i - 1) for i in range(1, ncut - 1)]

    def rates_of(kernel, out, arrays, read, summed, rest=()):
        scratch = [pltpu.VMEM((n * 16, slots), F32) for n in (read, summed, summed)] + list(rest)
        return call(lambda *refs: kernel((cols, rows), *refs), out, (), arrays, scratch, COST)

    def exchange(own, marks, sent):
        got = lax.all_to_all(sent, "depth", 0, 0, tiled=True)
        inner = rates_of(inner_rates_kernel, block_rates, (own, marks), cols * rows, cols * rows)
        wide = call(extend_kernel, shape(6 * cols + 1, rows + 2 * HALO, slots), (), (own, marks, got, inner))
        swapped, other = lax.ppermute(wide, "cut", swap), lax.ppermute(wide, "cut", cross)
        force = call(pair_force_kernel, along_line, (), (wide, swapped))
        total = lax.all_to_all(force, both, 0, 0, tiled=True, axis_index_groups=lines)
        found = rates_of(wide_rates_kernel, ring_rates, (wide, swapped, other, inner), 3 * cols * (rows + 4), (cols + 2) * (rows + 2))
        return found, (wide, swapped, other), total

    own, marks, tool, sent = pl.pallas_call(
        start_kernel,
        out_shape=[state, marking, vector, message],
        in_specs=[SMEM] * 3 + [pl.BlockSpec(memory_space=pl.ANY)] * 3,
        out_specs=[VMEM] * 4,
        scratch_shapes=[pltpu.SemaphoreType.DMA((3,))],
        compiler_params=pltpu.CompilerParams(vmem_limit_bytes=60 * 1024 * 1024),
    )(counts, contact_mask, tool, positions, velocity, density)
    found, around, total = exchange(own, marks, sent)
    rest = (pltpu.VMEM(ring.shape, F32),)
    read, summed = (cols + 2) * (rows + 2), cols * rows
    own, found = rates_of(first_update_kernel, [state, block_rates], (own, found, marks, *around, tool), read, summed, rest)

    kernel = functools.partial(second_update_kernel, scale)
    own, tool, sent = call(kernel, [state, vector, message], (), (own, found, marks, tool, total))

    found, around, total = exchange(own, marks, sent)
    kernel = functools.partial(third_update_kernel, scale)
    outs = [state, ring, vector, along_plane]
    new_own, ringed, tool, force = call(kernel, outs, (), (own, found, marks, *around, tool, total))
    own = new_own

    got = lax.all_to_all(force, both, 0, 0, tiled=True, axis_index_groups=planes)
    force = call(spread_kernel, along_line, (), (got,))
    total = lax.all_to_all(force, both, 0, 0, tiled=True, axis_index_groups=lines)
    found = rates_of(rates_kernel, block_rates, (ringed,), (cols + 2) * (rows + 2), cols * rows)
    kernel = functools.partial(last_force_kernel, scale)
    tool, force = call(kernel, [vector, along_depth], (), (own, marks, tool, total))
    total = lax.all_to_all(force, "depth", 0, 0, tiled=True)
    kernel = functools.partial(last_kernel, near)
    sent = call(kernel, shape(near, size + 8, slots), (destination,), (own, found, marks, tool, total))
    close = [[g * near + k for k in range(near)] for g in range(far)]
    apart = [[g * near + k for g in range(far)] for k in range(near)]
    got = lax.all_to_all(sent, "cut", 0, 0, tiled=True, axis_index_groups=close)
    sent = call(functools.partial(sort_kernel, near, size), shape(far, size + 8, slots), (destination,), (got,))
    got = lax.all_to_all(sent, "cut", 0, 0, tiled=True, axis_index_groups=apart)
    return pl.pallas_call(
        functools.partial(take_kernel, near, scale),
        out_shape=[state, shape(2)],
        in_specs=[SMEM, VMEM, VMEM],
        out_specs=[VMEM, SMEM],
        compiler_params=PARAMS,
    )(destination, got, tool)


def solution(mesh):
    return jax.shard_map(
        body,
        mesh=mesh,
        in_specs=(
            P(None, "cut", "depth", None),
            P(None, "cut", "depth", None),
            P("cut", "depth", None),
            P("cut", "depth"),
            P("cut", "depth"),
            P(),
            P(),
        ),
        out_specs=(P(None, "cut", "depth", None), P()),
        check_vma=False,
    )
```

```python
import functools

import jax
import jax.numpy as jnp
from jax import lax
from jax.experimental import pallas as pl
from jax.experimental.pallas import tpu as pltpu
from jax.sharding import PartitionSpec as P

HALO = 2
MASS = 0.02
SOUND = 20.0
VISCOSITY = 2.0
STIFF = 50.0
DT = 0.05

FAR = 1.0e6

COST = 20_000_000_000

F32 = jnp.float32
BF16 = jnp.bfloat16
PARAMS = pltpu.CompilerParams(vmem_limit_bytes=40 * 1024 * 1024)
VMEM = pl.BlockSpec(memory_space=pltpu.VMEM)
SMEM = pl.BlockSpec(memory_space=pltpu.SMEM)


def here():
    return lax.axis_index("cut")


def row_block():
    return lax.axis_index("depth")


def shape(*dims):
    return jax.ShapeDtypeStruct(dims, F32)


def call(kernel, outs, scalars, arrays, scratch=(), estimate=0):
    return pl.pallas_call(
        kernel,
        out_shape=outs,
        in_specs=[SMEM] * len(scalars) + [VMEM] * len(arrays),
        out_specs=[VMEM] * len(outs) if isinstance(outs, list) else VMEM,
        scratch_shapes=scratch,
        compiler_params=PARAMS,
        cost_estimate=pl.CostEstimate(flops=estimate, bytes_accessed=1 << 20, transcendentals=0) if estimate else None,
    )(*scalars, *arrays)


def pressure(s):
    inv = 1.0 / s
    return SOUND * (s - 1.0) * inv * inv, inv


def penalties(x, touch, live, offset, column):
    return touch * live * jnp.maximum(0.0, x - column + offset - 0.5)


def own_force(new, marks, offset, first):
    total = 0.0
    for c, fields in enumerate(new):
        total = total + STIFF * penalties(fields[0], marks[1, c], marks[0, c], offset, first + c)
    total = jnp.sum(total, axis=0, keepdims=True)
    return jnp.broadcast_to(jnp.sum(total, axis=1, keepdims=True), total.shape)


def visible(fields, live, touch):
    alive = live > 0
    x, y, u, v, rho = fields
    return [jnp.where(alive, x, FAR), y, u, v, jnp.where(alive, rho, 1.0), live * touch]


def fill_depth(state, marks, force, sent):
    depth, ndepth = row_block(), sent.shape[0]
    cols, rows = marks.shape[1:3]
    row = 6 * cols * HALO
    sent[...] = jnp.zeros(sent.shape, F32)
    sent[:, row : row + 1, :] = jnp.broadcast_to(force[None], (ndepth, 1, force.shape[1]))
    seen = [visible(state[c], marks[0, c], marks[1, c]) for c in range(cols)]

    def put(target, rim):
        for c in range(cols):
            for f in range(6):
                at = (f * cols + c) * HALO
                sent[target, at : at + HALO] = seen[c][f][rim : rim + HALO]

    @pl.when(depth > 0)
    def _():
        put(depth - 1, 0)

    @pl.when(depth < ndepth - 1)
    def _():
        put(depth + 1, rows - HALO)


def origin(cols, rows):
    first = (here() * cols).astype(F32)
    return first + 0.5 * cols, (row_block() * rows).astype(F32) + 0.5 * rows, first


def start_kernel(near, *refs):
    inputs, (own, marks, route, sent), (counts, contact, target, first_tool, arrived) = refs[:7], refs[7:11], refs[11:]
    homes = [own.at[0:2], own.at[2:4], own.at[4], counts, contact, target, first_tool]
    copies = [pltpu.make_async_copy(part, to, arrived.at[n]) for n, (part, to) in enumerate(zip(inputs, homes))]
    for copy in copies:
        copy.start()
    for copy in copies:
        copy.wait()
    cols, rows, slots = own.shape[1:]
    row = lax.broadcasted_iota(jnp.int32, (rows, slots), 0)
    slot = lax.broadcasted_iota(jnp.int32, (rows, slots), 1)
    for c in range(cols):
        filled = jnp.zeros((rows, slots), jnp.int32)
        touch = jnp.zeros((rows, slots), jnp.int32)
        for r in range(rows):
            filled = jnp.where(row == r, counts[c : c + 1, r : r + 1], filled)
            touch = jnp.where(row == r, contact[c : c + 1, r : r + 1], touch)
        marks[0, c] = jnp.where(slot < filled, 1.0, 0.0)
        marks[1, c] = touch.astype(F32)
    new = [[own[f, c] for f in range(5)] for c in range(cols)]
    offset = jnp.broadcast_to(first_tool[0:1, 0:1], (1, slots))
    marks[2, 0] = jnp.broadcast_to(offset, (rows, slots))
    marks[2, 1] = jnp.broadcast_to(first_tool[0:1, 1:2], (rows, slots))
    fill_depth(new, marks, own_force(new, marks, offset, origin(cols, rows)[2]), sent)

    block = lax.broadcasted_iota(jnp.int32, target.shape, 1)

    def entry(at):
        return jnp.sum(jnp.where(block == at, target[...], 0), axis=1, keepdims=True)

    route[...] = jnp.zeros(route.shape, jnp.int32)
    route[0:1] = jnp.broadcast_to(entry(here()), (1, slots))
    source = jnp.sum(jnp.where(target[...] == here(), block, 0), axis=1, keepdims=True)
    route[1:2] = jnp.broadcast_to(source, (1, slots))
    group = lax.div(here(), near)
    for k in range(near):
        route[2 + k : 3 + k] = jnp.broadcast_to(entry(group * near + k), (1, slots))


def extend_kernel(own, marks, got, inner, wide):
    depth, ndepth = row_block(), got.shape[0]
    cols, rows = own.shape[1:3]
    above = got[jnp.maximum(depth - 1, 0)]
    below = got[jnp.minimum(depth + 1, ndepth - 1)]
    blank = [FAR, 0.0, 0.0, 0.0, 1.0, 0.0]
    for c in range(cols):
        seen = visible([own[f, c] for f in range(5)], marks[0, c], marks[1, c])
        for f in range(6):
            at = (f * cols + c) * HALO
            wide[f * cols + c, 0:HALO] = jnp.where(depth > 0, above[at : at + HALO], blank[f])
            wide[f * cols + c, HALO : rows + HALO] = seen[f]
            wide[f * cols + c, rows + HALO :] = jnp.where(depth < ndepth - 1, below[at : at + HALO], blank[f])
    row = 6 * cols * HALO
    wide[6 * cols] = jnp.broadcast_to(jnp.sum(got[:, row : row + 1, :], axis=0), wide.shape[1:])


def pair_force_kernel(wide, swapped, force):
    last = wide.shape[0] - 1
    force[...] = jnp.broadcast_to((wide[last, 0:1] + swapped[last, 0:1])[None], force.shape)


def spread_kernel(got, force):
    force[...] = jnp.broadcast_to(jnp.sum(got[...], axis=0, keepdims=True), force.shape)


def pair_sums(columns, center, pairs, out, feat, acc2, acc3, earlier=None):
    x0, y0, _ = center
    tall, slots = columns[0][0].shape
    row0 = min(r for _, r in pairs)
    rows = 1 + max(r for _, r in pairs) - row0
    for c, (x, y, u, v, s) in enumerate(columns):
        lx, ly = x - x0, y - y0
        press, inv = pressure(s)
        parts = [jnp.ones_like(x), press, u, v, u * lx + v * ly]
        for part in (lx, ly, press * lx, press * ly):
            high = part.astype(BF16).astype(F32)
            parts += [high, part - high]
        parts += [inv, inv * u, inv * v]
        for k, part in enumerate(parts):
            feat[pl.ds(c * tall * 16 + k, tall, stride=16), :] = part
    for i, ((c, r), around) in enumerate(pairs.items()):
        xi, yi = [jnp.broadcast_to(f[r : r + 1], (slots, slots)).T for f in columns[c][:2]]

        def weights(a, b):
            dx = (xi - columns[a][0][b : b + 1]).astype(BF16)
            dy = (yi - columns[a][1][b : b + 1]).astype(BF16)
            q = jnp.maximum(BF16(0.0), BF16(1.0) - dx * dx - dy * dy)
            q2 = q * q
            return jnp.concatenate([q2, q2 * q], axis=0)

        total = None
        for n in range(0, len(around), 2):
            pair = around[n : n + 2]
            w = jnp.concatenate([weights(a, b) for a, b in pair], axis=1)
            f = jnp.concatenate([feat[pl.ds((a * tall + b) * 16, 16), :] for a, b in pair], axis=1).astype(BF16)
            found = lax.dot_general(f, w, (((1,), (1,)), ((), ())), preferred_element_type=F32)
            total = found if total is None else total + found
        acc2[i * 16 : (i + 1) * 16] = total[:, :slots]
        acc3[i * 16 : (i + 1) * 16] = total[:, slots:]

    for n, c in enumerate(sorted({c for c, _ in pairs})):

        def summed(k):
            return (acc2 if k < 13 else acc3)[pl.ds(n * rows * 16 + k, rows, stride=16), :]

        x, y, u, v, s = [f[row0 : row0 + rows] for f in columns[c]]
        x, y = x - x0, y - y0
        press, _ = pressure(s)
        a0, ap, au, av, aw = [summed(k) for k in range(5)]
        ax, ay, apx, apy = [summed(k) + summed(k + 1) for k in range(5, 13, 2)]
        b0, bu, bv = [summed(k) for k in range(13, 16)]
        sx, sy = x * a0 - ax, y * a0 - ay
        rates = [
            (6.0 * MASS) * (press * sx + x * ap - apx) - (VISCOSITY * MASS) * (u * b0 - bu),
            (6.0 * MASS) * (press * sy + y * ap - apy) - (VISCOSITY * MASS) * (v * b0 - bv),
            (-6.0 * MASS) * (u * sx + v * sy - x * au - y * av + aw),
        ]
        for f in range(3):
            out[f, n] = rates[f]
            if earlier is not None and 0 < n <= earlier.shape[1]:
                inner = earlier[f, n - 1]
                out[f, n, 1 : rows - 1] = rates[f][1 : rows - 1] + inner


def around_cell(c, r):
    return [(c + a, r + b) for a in (-1, 0, 1) for b in (-1, 0, 1)]


def inner_rates_kernel(size, own, marks, out, feat, acc2, acc3):
    cols, rows = size
    columns = [visible([own[f, c] for f in range(5)], marks[0, c], marks[1, c])[:5] for c in range(cols)]
    cells = [(c, r) for c in range(cols) for r in range(rows)]
    pairs = {cell: [j for j in around_cell(*cell) if j in cells] for cell in cells}
    pair_sums(columns, origin(*size), pairs, out, feat, acc2, acc3)


def wide_columns(cols, wide, swapped, other):
    even = lax.rem(here(), 2) == 0
    blank = [FAR, 0.0, 0.0, 0.0, 1.0, 0.0]
    columns = []
    for side in range(3):
        outside = here() == (0 if side == 0 else lax.axis_size("cut") - 1)
        for c in range(cols):
            if side == 1:
                fields = [wide[f * cols + c] for f in range(6)]
            else:
                first, second = (other, swapped) if side == 0 else (swapped, other)
                fields = [jnp.where(outside, blank[f], jnp.where(even, first[f * cols + c], second[f * cols + c])) for f in range(6)]
            columns.append(fields)
    return columns


def wide_rates_kernel(size, wide, swapped, other, inner, out, feat, acc2, acc3):
    cols, rows = size
    columns = [fields[:5] for fields in wide_columns(cols, wide, swapped, other)]
    block = [(c + cols, r + HALO) for c in range(cols) for r in range(rows)]
    pairs = {}
    for c in range(1, 3 * cols - 1):
        for r in range(1, rows + 3):
            pairs[c, r] = [j for j in around_cell(c, r) if (c, r) not in block or j not in block]
    pair_sums(columns, origin(*size), pairs, out, feat, acc2, acc3, inner)


def rates_kernel(size, ring, out, feat, acc2, acc3):
    cols, rows = size
    columns = [[ring[f, c] for f in range(5)] for c in range(cols + 2)]
    pairs = {(c, r): around_cell(c, r) for c in range(1, cols + 1) for r in range(1, rows + 1)}
    pair_sums(columns, origin(*size), pairs, out, feat, acc2, acc3)


def moved_ring(columns, found, offset, first, ring):
    for n in range(ring.shape[1]):
        x, y, u, v, s, touch = [f[1:-1] for f in columns[n + 1]]
        live = jnp.where(x < 0.5 * FAR, 1.0, 0.0)
        pen = touch * jnp.maximum(0.0, x - (first + (n - 1)) + offset - 0.5)
        u = u + DT * live * (found[0, n] - STIFF * pen)
        v = v + DT * live * found[1, n]
        ring[0, n] = x + DT * live * u
        ring[1, n] = y + DT * live * v
        ring[2, n] = u
        ring[3, n] = v
        ring[4, n] = s + DT * live * found[2, n]


def moved_state(own, found, marks, offset, first):
    cols, rows = own.shape[1:3]
    side, rim = (found.shape[1] - cols) // 2, (found.shape[2] - rows) // 2
    new = []
    for c in range(cols):
        live = marks[0, c]
        ax, ay, drho = [found[f, c + side][rim : rim + rows] for f in range(3)]
        pen = penalties(own[0, c], marks[1, c], live, offset, first + c)
        u = own[2, c] + DT * live * (ax - STIFF * pen)
        v = own[3, c] + DT * live * ay
        x = own[0, c] + DT * live * u
        y = own[1, c] + DT * live * v
        rho = own[4, c] + DT * live * drho
        new.append([x, y, u, v, rho])
    return new


def keep(new, own):
    for c, fields in enumerate(new):
        for f in range(5):
            own[f, c] = fields[f]


def tool_step(offset, speed, force, scale):
    speed = speed + DT * (1.0 - force * scale)
    return offset + DT * speed, speed


def first_update_kernel(size, own, found, marks, wide, swapped, other, new_own, out, feat, acc2, acc3, ring):
    first = origin(*size)[2]
    offset = marks[2, 0, 0:1]
    keep(moved_state(own, found, marks, offset, first), new_own)
    moved_ring(wide_columns(size[0], wide, swapped, other), found, offset, first, ring)
    rates_kernel(size, ring, out, feat, acc2, acc3)


def second_update_kernel(scale, own, found, marks, total, new_own, new_tool, sent):
    first = origin(*own.shape[1:3])[2]
    offset, speed = tool_step(marks[2, 0, 0:1], marks[2, 1, 0:1], jnp.sum(total[...], axis=0), scale)
    new_tool[0:1] = offset
    new_tool[1:2] = speed
    state = [[own[f, c] for f in range(5)] for c in range(own.shape[1])]
    new = moved_state(own, found, marks, offset, first)
    keep(new, new_own)
    fill_depth(new, marks, own_force(state, marks, offset, first), sent)


def third_update_kernel(scale, own, found, marks, wide, swapped, other, tool, total, new_own, ring, new_tool, force):
    first = origin(*own.shape[1:3])[2]
    offset, speed = tool_step(tool[0:1], tool[1:2], jnp.sum(total[...], axis=0), scale)
    new_tool[0:1] = offset
    new_tool[1:2] = speed
    state = [[own[f, c] for f in range(5)] for c in range(own.shape[1])]
    force[...] = jnp.broadcast_to(own_force(state, marks, offset, first)[None], force.shape)
    keep(moved_state(own, found, marks, offset, first), new_own)
    moved_ring(wide_columns(own.shape[1], wide, swapped, other), found, offset, first, ring)


def last_force_kernel(scale, own, marks, tool, total, new_tool, force):
    offset, speed = tool_step(tool[0:1], tool[1:2], jnp.sum(total[...], axis=0), scale)
    new_tool[0:1] = offset
    new_tool[1:2] = speed
    state = [[own[f, c] for f in range(5)] for c in range(own.shape[1])]
    part = own_force(state, marks, offset, origin(*own.shape[1:3])[2])
    force[...] = jnp.broadcast_to(part[None], force.shape)


def last_kernel(near, route, own, found, marks, tool, total, sent):
    cols, rows, slots = own.shape[1:]
    size = 5 * cols * rows
    new = moved_state(own, found, marks, tool[0:1], origin(cols, rows)[2])
    sent[:, size:, :] = jnp.broadcast_to(jnp.sum(total[...], axis=0, keepdims=True), (near, sent.shape[1] - size, slots))
    target = route[0:1]
    for k in range(near):
        chosen = jnp.bitwise_and(target, near - 1) == k
        for f in range(5):
            for c in range(cols):
                at = (f * cols + c) * rows
                sent[k, at : at + rows] = jnp.where(chosen, new[c][f], 0.0)


def sort_kernel(near, size, route, got, sent):
    far, most, slots = sent.shape
    digit = lax.rem(here(), near)
    total = jnp.sum(got[:, size : size + 1, :], axis=0, keepdims=True)
    sent[:, size:, :] = jnp.broadcast_to(total, (far, most - size, slots))
    for g in range(far):
        block = jnp.zeros((size, slots), F32)
        for k in range(near):
            block = jnp.where(route[2 + k : 3 + k] == g * near + digit, got[k, 0:size], block)
        sent[g, 0:size] = block


def take_kernel(near, scale, route, got, tool, out, new_tool):
    cols, rows, slots = out.shape[1:]
    size = 5 * cols * rows
    source = route[1:2]
    for f in range(5):
        for c in range(cols):
            at = (f * cols + c) * rows
            field = got[0, at : at + rows]
            for g in range(1, got.shape[0]):
                field = jnp.where(source >= g * near, got[g, at : at + rows], field)
            out[f, c] = field
    offset, speed = tool_step(tool[0:1], tool[1:2], jnp.sum(got[:, size : size + 1, :], axis=0), scale)
    slot = lax.broadcasted_iota(jnp.int32, (1, slots), 1)
    new_tool[...] = jnp.where(slot == 0, offset, speed)[:, 0:2]


def body(positions, velocity, density, counts, contact_mask, destination, tool):
    cols, rows, slots = density.shape
    ncut, ndepth = lax.axis_size("cut"), lax.axis_size("depth")
    scale = 1.0 / (ncut * cols * ndepth * rows * slots)
    near = 8 if ncut % 8 == 0 else 1
    far = ncut // near
    size = 5 * cols * rows
    state, marking = shape(5, cols, rows, slots), shape(3, cols, rows, slots)
    message, vector = shape(ndepth, 32, slots), shape(2, slots)
    along_depth, along_plane, along_line = [shape(n, 1, slots) for n in (ndepth, 2 * ndepth, ncut // 2)]
    both = ("cut", "depth")
    pairs = range(0, ncut, 2)
    planes = [[(c + k) * ndepth + d for k in range(2) for d in range(ndepth)] for c in pairs]
    lines = [[(c + k) * ndepth + d for c in pairs] for k in range(2) for d in range(ndepth)]
    ring, ring_rates = shape(5, cols + 2, rows + 2, slots), shape(3, cols + 2, rows + 2, slots)
    block_rates = shape(3, cols, rows, slots)
    swap = [(i, i ^ 1) for i in range(ncut)]
    cross = [(i, i + 1 if i % 2 else i - 1) for i in range(1, ncut - 1)]

    def rates_of(kernel, out, arrays, read, summed, rest=()):
        scratch = [pltpu.VMEM((n * 16, slots), F32) for n in (read, summed, summed)] + list(rest)
        return call(lambda *refs: kernel((cols, rows), *refs), out, (), arrays, scratch, COST)

    def exchange(own, marks, sent):
        got = lax.all_to_all(sent, "depth", 0, 0, tiled=True)
        inner = rates_of(inner_rates_kernel, block_rates, (own, marks), cols * rows, cols * rows)
        wide = call(extend_kernel, shape(6 * cols + 1, rows + 2 * HALO, slots), (), (own, marks, got, inner))
        swapped, other = lax.ppermute(wide, "cut", swap), lax.ppermute(wide, "cut", cross)
        force = call(pair_force_kernel, along_line, (), (wide, swapped))
        total = lax.all_to_all(force, both, 0, 0, tiled=True, axis_index_groups=lines)
        found = rates_of(wide_rates_kernel, ring_rates, (wide, swapped, other, inner), 3 * cols * (rows + 4), (cols + 2) * (rows + 2))
        return found, (wide, swapped, other), total

    inputs = (positions, velocity, density, counts, contact_mask, destination[None], tool[None])
    own, marks, route, sent = pl.pallas_call(
        functools.partial(start_kernel, near),
        out_shape=[state, marking, jax.ShapeDtypeStruct((16, slots), jnp.int32), message],
        in_specs=[pl.BlockSpec(memory_space=pl.ANY)] * 7,
        out_specs=[VMEM] * 4,
        scratch_shapes=[pltpu.VMEM(part.shape, part.dtype) for part in inputs[3:]] + [pltpu.SemaphoreType.DMA((7,))],
        compiler_params=pltpu.CompilerParams(vmem_limit_bytes=60 * 1024 * 1024),
    )(*inputs)
    found, around, total = exchange(own, marks, sent)
    rest = (pltpu.VMEM(ring.shape, F32),)
    read, summed = (cols + 2) * (rows + 2), cols * rows
    own, found = rates_of(first_update_kernel, [state, block_rates], (own, found, marks, *around), read, summed, rest)

    kernel = functools.partial(second_update_kernel, scale)
    own, tool, sent = call(kernel, [state, vector, message], (), (own, found, marks, total))

    found, around, total = exchange(own, marks, sent)
    kernel = functools.partial(third_update_kernel, scale)
    outs = [state, ring, vector, along_plane]
    new_own, ringed, tool, force = call(kernel, outs, (), (own, found, marks, *around, tool, total))
    own = new_own

    got = lax.all_to_all(force, both, 0, 0, tiled=True, axis_index_groups=planes)
    force = call(spread_kernel, along_line, (), (got,))
    total = lax.all_to_all(force, both, 0, 0, tiled=True, axis_index_groups=lines)
    found = rates_of(rates_kernel, block_rates, (ringed,), (cols + 2) * (rows + 2), cols * rows)
    kernel = functools.partial(last_force_kernel, scale)
    tool, force = call(kernel, [vector, along_depth], (), (own, marks, tool, total))
    total = lax.all_to_all(force, "depth", 0, 0, tiled=True)
    kernel = functools.partial(last_kernel, near)
    sent = call(kernel, shape(near, size + 8, slots), (), (route, own, found, marks, tool, total))
    close = [[g * near + k for k in range(near)] for g in range(far)]
    apart = [[g * near + k for g in range(far)] for k in range(near)]
    got = lax.all_to_all(sent, "cut", 0, 0, tiled=True, axis_index_groups=close)
    sent = call(functools.partial(sort_kernel, near, size), shape(far, size + 8, slots), (), (route, got))
    got = lax.all_to_all(sent, "cut", 0, 0, tiled=True, axis_index_groups=apart)
    moved, tool = call(functools.partial(take_kernel, near, scale), [state, shape(1, 2)], (), (route, got, tool))
    return moved, tool[0]


def solution(mesh):
    return jax.shard_map(
        body,
        mesh=mesh,
        in_specs=(
            P(None, "cut", "depth", None),
            P(None, "cut", "depth", None),
            P("cut", "depth", None),
            P("cut", "depth"),
            P("cut", "depth"),
            P(),
            P(),
        ),
        out_specs=(P(None, "cut", "depth", None), P()),
        check_vma=False,
    )
```

```python
import functools

import jax
import jax.numpy as jnp
from jax import lax
from jax.experimental import pallas as pl
from jax.experimental.pallas import tpu as pltpu
from jax.sharding import PartitionSpec as P

HALO = 2
MASS = 0.02
SOUND = 20.0
VISCOSITY = 2.0
STIFF = 50.0
DT = 0.05

FAR = 1.0e6

COST = 20_000_000_000

F32 = jnp.float32
BF16 = jnp.bfloat16
PARAMS = pltpu.CompilerParams(vmem_limit_bytes=40 * 1024 * 1024)
VMEM = pl.BlockSpec(memory_space=pltpu.VMEM)
SMEM = pl.BlockSpec(memory_space=pltpu.SMEM)


def here():
    return lax.axis_index("cut")


def row_block():
    return lax.axis_index("depth")


def shape(*dims):
    return jax.ShapeDtypeStruct(dims, F32)


def call(kernel, outs, scalars, arrays, scratch=(), estimate=0):
    return pl.pallas_call(
        kernel,
        out_shape=outs,
        in_specs=[SMEM] * len(scalars) + [VMEM] * len(arrays),
        out_specs=[VMEM] * len(outs) if isinstance(outs, list) else VMEM,
        scratch_shapes=scratch,
        compiler_params=PARAMS,
        cost_estimate=pl.CostEstimate(flops=estimate, bytes_accessed=1 << 20, transcendentals=0) if estimate else None,
    )(*scalars, *arrays)


def pressure(s):
    inv = 1.0 / s
    return SOUND * (s - 1.0) * inv * inv, inv


def penalties(x, touch, live, offset, column):
    return touch * live * jnp.maximum(0.0, x - column + offset - 0.5)


def own_force(new, marks, offset, first):
    total = 0.0
    for c, fields in enumerate(new):
        total = total + STIFF * penalties(fields[0], marks[1, c], marks[0, c], offset, first + c)
    total = jnp.sum(total, axis=0, keepdims=True)
    return jnp.broadcast_to(jnp.sum(total, axis=1, keepdims=True), total.shape)


def visible(fields, live, touch):
    alive = live > 0
    x, y, u, v, rho = fields
    return [jnp.where(alive, x, FAR), y, u, v, jnp.where(alive, rho, 1.0), live * touch]


def fill_depth(state, marks, force, sent):
    depth, ndepth = row_block(), sent.shape[0]
    cols, rows = marks.shape[1:3]
    row = 6 * cols * HALO
    sent[...] = jnp.zeros(sent.shape, F32)
    sent[:, row : row + 1, :] = jnp.broadcast_to(force[None], (ndepth, 1, force.shape[1]))
    seen = [visible(state[c], marks[0, c], marks[1, c]) for c in range(cols)]

    def put(target, rim):
        for c in range(cols):
            for f in range(6):
                at = (f * cols + c) * HALO
                sent[target, at : at + HALO] = seen[c][f][rim : rim + HALO]

    @pl.when(depth > 0)
    def _():
        put(depth - 1, 0)

    @pl.when(depth < ndepth - 1)
    def _():
        put(depth + 1, rows - HALO)


def origin(cols, rows):
    first = (here() * cols).astype(F32)
    return first + 0.5 * cols, (row_block() * rows).astype(F32) + 0.5 * rows, first


def start_kernel(near, *refs):
    inputs, (own, marks, route, sent), (counts, contact, target, first_tool, arrived) = refs[:7], refs[7:11], refs[11:]
    homes = [own.at[0:2], own.at[2:4], own.at[4], counts, contact, target, first_tool]
    copies = [pltpu.make_async_copy(part, to, arrived.at[n]) for n, (part, to) in enumerate(zip(inputs, homes))]
    for copy in copies:
        copy.start()
    for copy in copies:
        copy.wait()
    cols, rows, slots = own.shape[1:]
    row = lax.broadcasted_iota(jnp.int32, (rows, slots), 0)
    slot = lax.broadcasted_iota(jnp.int32, (rows, slots), 1)
    for c in range(cols):
        filled = jnp.zeros((rows, slots), jnp.int32)
        touch = jnp.zeros((rows, slots), jnp.int32)
        for r in range(rows):
            filled = jnp.where(row == r, counts[c : c + 1, r : r + 1], filled)
            touch = jnp.where(row == r, contact[c : c + 1, r : r + 1], touch)
        marks[0, c] = jnp.where(slot < filled, 1.0, 0.0)
        marks[1, c] = touch.astype(F32)
    new = [[own[f, c] for f in range(5)] for c in range(cols)]
    offset = jnp.broadcast_to(first_tool[0:1, 0:1], (1, slots))
    marks[2, 0] = jnp.broadcast_to(offset, (rows, slots))
    marks[2, 1] = jnp.broadcast_to(first_tool[0:1, 1:2], (rows, slots))
    fill_depth(new, marks, own_force(new, marks, offset, origin(cols, rows)[2]), sent)

    block = lax.broadcasted_iota(jnp.int32, target.shape, 1)

    def entry(at):
        return jnp.sum(jnp.where(block == at, target[...], 0), axis=1, keepdims=True)

    route[...] = jnp.zeros(route.shape, jnp.int32)
    route[0:1] = jnp.broadcast_to(entry(here()), (1, slots))
    source = jnp.sum(jnp.where(target[...] == here(), block, 0), axis=1, keepdims=True)
    route[1:2] = jnp.broadcast_to(source, (1, slots))
    group = lax.div(here(), near)
    for k in range(near):
        route[2 + k : 3 + k] = jnp.broadcast_to(entry(group * near + k), (1, slots))


def extend_kernel(own, marks, got, inner, wide):
    depth, ndepth = row_block(), got.shape[0]
    cols, rows = own.shape[1:3]
    above = got[jnp.maximum(depth - 1, 0)]
    below = got[jnp.minimum(depth + 1, ndepth - 1)]
    blank = [FAR, 0.0, 0.0, 0.0, 1.0, 0.0]
    for c in range(cols):
        seen = visible([own[f, c] for f in range(5)], marks[0, c], marks[1, c])
        for f in range(6):
            at = (f * cols + c) * HALO
            wide[f * cols + c, 0:HALO] = jnp.where(depth > 0, above[at : at + HALO], blank[f])
            wide[f * cols + c, HALO : rows + HALO] = seen[f]
            wide[f * cols + c, rows + HALO :] = jnp.where(depth < ndepth - 1, below[at : at + HALO], blank[f])
    row = 6 * cols * HALO
    wide[6 * cols] = jnp.broadcast_to(jnp.sum(got[:, row : row + 1, :], axis=0), wide.shape[1:])


def pair_force_kernel(wide, swapped, force):
    last = wide.shape[0] - 1
    force[...] = jnp.broadcast_to((wide[last, 0:1] + swapped[last, 0:1])[None], force.shape)


def spread_kernel(got, before, force):
    force[...] = jnp.broadcast_to(jnp.sum(got[...], axis=0, keepdims=True), force.shape)


def pair_sums(columns, center, pairs, out, feat, acc2, acc3, earlier={}):
    x0, y0, _ = center
    tall, slots = columns[0][0].shape
    row0 = min(r for _, r in pairs)
    rows = 1 + max(r for _, r in pairs) - row0
    for c, (x, y, u, v, s) in enumerate(columns):
        lx, ly = x - x0, y - y0
        press, inv = pressure(s)
        parts = [jnp.ones_like(x), press, u, v, u * lx + v * ly]
        for part in (lx, ly, press * lx, press * ly):
            high = part.astype(BF16).astype(F32)
            parts += [high, part - high]
        parts += [inv, inv * u, inv * v]
        for k, part in enumerate(parts):
            feat[pl.ds(c * tall * 16 + k, tall, stride=16), :] = part
    for i, ((c, r), around) in enumerate(pairs.items()):
        xi, yi = [jnp.broadcast_to(f[r : r + 1], (slots, slots)).T for f in columns[c][:2]]

        def weights(a, b):
            dx = (xi - columns[a][0][b : b + 1]).astype(BF16)
            dy = (yi - columns[a][1][b : b + 1]).astype(BF16)
            q = jnp.maximum(BF16(0.0), BF16(1.0) - dx * dx - dy * dy)
            q2 = q * q
            return jnp.concatenate([q2, q2 * q], axis=0)

        total = None
        for n in range(0, len(around), 2):
            pair = around[n : n + 2]
            w = jnp.concatenate([weights(a, b) for a, b in pair], axis=1)
            f = jnp.concatenate([feat[pl.ds((a * tall + b) * 16, 16), :] for a, b in pair], axis=1).astype(BF16)
            found = lax.dot_general(f, w, (((1,), (1,)), ((), ())), preferred_element_type=F32)
            total = found if total is None else total + found
        acc2[i * 16 : (i + 1) * 16] = total[:, :slots]
        acc3[i * 16 : (i + 1) * 16] = total[:, slots:]

    for n, c in enumerate(sorted({c for c, _ in pairs})):

        def summed(k):
            return (acc2 if k < 13 else acc3)[pl.ds(n * rows * 16 + k, rows, stride=16), :]

        x, y, u, v, s = [f[row0 : row0 + rows] for f in columns[c]]
        x, y = x - x0, y - y0
        press, _ = pressure(s)
        a0, ap, au, av, aw = [summed(k) for k in range(5)]
        ax, ay, apx, apy = [summed(k) + summed(k + 1) for k in range(5, 13, 2)]
        b0, bu, bv = [summed(k) for k in range(13, 16)]
        sx, sy = x * a0 - ax, y * a0 - ay
        rates = [
            (6.0 * MASS) * (press * sx + x * ap - apx) - (VISCOSITY * MASS) * (u * b0 - bu),
            (6.0 * MASS) * (press * sy + y * ap - apy) - (VISCOSITY * MASS) * (v * b0 - bv),
            (-6.0 * MASS) * (u * sx + v * sy - x * au - y * av + aw),
        ]
        for f in range(3):
            out[f, n] = rates[f]
            if c in earlier:
                out[f, n, 1 : rows - 1] = rates[f][1 : rows - 1] + earlier[c][f]


def around_cell(c, r):
    return [(c + a, r + b) for a in (-1, 0, 1) for b in (-1, 0, 1)]


def inner_rates_kernel(size, own, marks, out, feat, acc2, acc3):
    cols, rows = size
    columns = [visible([own[f, c] for f in range(5)], marks[0, c], marks[1, c])[:5] for c in range(cols)]
    cells = [(c, r) for c in range(cols) for r in range(rows)]
    pairs = {cell: [j for j in around_cell(*cell) if j in cells] for cell in cells}
    pair_sums(columns, origin(*size), pairs, out, feat, acc2, acc3)


def wide_columns(cols, wide, swapped, other):
    even = lax.rem(here(), 2) == 0
    blank = [FAR, 0.0, 0.0, 0.0, 1.0, 0.0]
    columns = []
    for side in range(3):
        outside = here() == (0 if side == 0 else lax.axis_size("cut") - 1)
        for c in range(cols):
            if side == 1:
                fields = [wide[f * cols + c] for f in range(6)]
            else:
                first, second = (other, swapped) if side == 0 else (swapped, other)
                fields = [jnp.where(outside, blank[f], jnp.where(even, first[f * cols + c], second[f * cols + c])) for f in range(6)]
            columns.append(fields)
    return columns


def wide_rates_kernel(wanted, size, wide, swapped, other, inner, out, feat, acc2, acc3):
    cols, rows = size
    start, stop = wanted[0] - 1, wanted[-1] + 2
    columns = [fields[:5] for fields in wide_columns(cols, wide, swapped, other)[start:stop]]
    block = [(c + cols, r + HALO) for c in range(cols) for r in range(rows)]
    pairs = {}
    for c in wanted:
        for r in range(1, rows + 3):
            around = [j for j in around_cell(c, r) if (c, r) not in block or j not in block]
            pairs[c - start, r] = [(a - start, b) for a, b in around]
    earlier = {c + cols - start: [inner[f, c] for f in range(3)] for c in range(cols)}
    pair_sums(columns, origin(*size), pairs, out, feat, acc2, acc3, earlier)


def rates_kernel(size, ring, out, feat, acc2, acc3):
    cols, rows = size
    columns = [[ring[f, c] for f in range(5)] for c in range(cols + 2)]
    pairs = {(c, r): around_cell(c, r) for c in range(1, cols + 1) for r in range(1, rows + 1)}
    pair_sums(columns, origin(*size), pairs, out, feat, acc2, acc3)


def by_column(*found):
    return [[part[f, n] for f in range(3)] for part in found for n in range(part.shape[1])]


def moved_ring(columns, found, offset, first, ring):
    for n in range(ring.shape[1]):
        x, y, u, v, s, touch = [f[1:-1] for f in columns[n + 1]]
        live = jnp.where(x < 0.5 * FAR, 1.0, 0.0)
        pen = touch * jnp.maximum(0.0, x - (first + (n - 1)) + offset - 0.5)
        u = u + DT * live * (found[n][0] - STIFF * pen)
        v = v + DT * live * found[n][1]
        ring[0, n] = x + DT * live * u
        ring[1, n] = y + DT * live * v
        ring[2, n] = u
        ring[3, n] = v
        ring[4, n] = s + DT * live * found[n][2]


def moved_state(own, found, marks, offset, first):
    cols, rows = own.shape[1:3]
    side, rim = (len(found) - cols) // 2, (found[0][0].shape[0] - rows) // 2
    new = []
    for c in range(cols):
        live = marks[0, c]
        ax, ay, drho = [part[rim : rim + rows] for part in found[c + side]]
        pen = penalties(own[0, c], marks[1, c], live, offset, first + c)
        u = own[2, c] + DT * live * (ax - STIFF * pen)
        v = own[3, c] + DT * live * ay
        x = own[0, c] + DT * live * u
        y = own[1, c] + DT * live * v
        rho = own[4, c] + DT * live * drho
        new.append([x, y, u, v, rho])
    return new


def keep(new, own):
    for c, fields in enumerate(new):
        for f in range(5):
            own[f, c] = fields[f]


def tool_step(offset, speed, force, scale):
    speed = speed + DT * (1.0 - force * scale)
    return offset + DT * speed, speed


def first_update_kernel(size, own, found, marks, wide, swapped, other, new_own, out, feat, acc2, acc3, ring):
    first = origin(*size)[2]
    offset = marks[2, 0, 0:1]
    found = by_column(found)
    keep(moved_state(own, found, marks, offset, first), new_own)
    moved_ring(wide_columns(size[0], wide, swapped, other), found, offset, first, ring)
    rates_kernel(size, ring, out, feat, acc2, acc3)


def second_update_kernel(scale, own, found, marks, total, new_own, new_tool, sent):
    first = origin(*own.shape[1:3])[2]
    offset, speed = tool_step(marks[2, 0, 0:1], marks[2, 1, 0:1], jnp.sum(total[...], axis=0), scale)
    new_tool[0:1] = offset
    new_tool[1:2] = speed
    state = [[own[f, c] for f in range(5)] for c in range(own.shape[1])]
    new = moved_state(own, by_column(found), marks, offset, first)
    keep(new, new_own)
    fill_depth(new, marks, own_force(state, marks, offset, first), sent)


def third_update_kernel(own, first_found, last_found, marks, wide, swapped, other, tool, new_own, ring):
    first = origin(*own.shape[1:3])[2]
    found = by_column(first_found, last_found)
    keep(moved_state(own, found, marks, tool[0:1], first), new_own)
    moved_ring(wide_columns(own.shape[1], wide, swapped, other), found, tool[0:1], first, ring)


def next_force_kernel(scale, own, marks, tool, total, new_tool, force):
    offset, speed = tool_step(tool[0:1], tool[1:2], jnp.sum(total[...], axis=0), scale)
    new_tool[0:1] = offset
    new_tool[1:2] = speed
    state = [[own[f, c] for f in range(5)] for c in range(own.shape[1])]
    part = own_force(state, marks, offset, origin(*own.shape[1:3])[2])
    force[...] = jnp.broadcast_to(part[None], force.shape)


def last_kernel(near, route, own, found, marks, tool, total, sent):
    cols, rows, slots = own.shape[1:]
    size = 5 * cols * rows
    new = moved_state(own, by_column(found), marks, tool[0:1], origin(cols, rows)[2])
    sent[:, size:, :] = jnp.broadcast_to(jnp.sum(total[...], axis=0, keepdims=True), (near, sent.shape[1] - size, slots))
    target = route[0:1]
    for k in range(near):
        chosen = jnp.bitwise_and(target, near - 1) == k
        for f in range(5):
            for c in range(cols):
                at = (f * cols + c) * rows
                sent[k, at : at + rows] = jnp.where(chosen, new[c][f], 0.0)


def sort_kernel(near, size, route, got, sent):
    far, most, slots = sent.shape
    digit = lax.rem(here(), near)
    total = jnp.sum(got[:, size : size + 1, :], axis=0, keepdims=True)
    sent[:, size:, :] = jnp.broadcast_to(total, (far, most - size, slots))
    for g in range(far):
        block = jnp.zeros((size, slots), F32)
        for k in range(near):
            block = jnp.where(route[2 + k : 3 + k] == g * near + digit, got[k, 0:size], block)
        sent[g, 0:size] = block


def take_kernel(near, scale, route, got, tool, out, new_tool):
    cols, rows, slots = out.shape[1:]
    size = 5 * cols * rows
    source = route[1:2]
    for f in range(5):
        for c in range(cols):
            at = (f * cols + c) * rows
            field = got[0, at : at + rows]
            for g in range(1, got.shape[0]):
                field = jnp.where(source >= g * near, got[g, at : at + rows], field)
            out[f, c] = field
    offset, speed = tool_step(tool[0:1], tool[1:2], jnp.sum(got[:, size : size + 1, :], axis=0), scale)
    slot = lax.broadcasted_iota(jnp.int32, (1, slots), 1)
    new_tool[...] = jnp.where(slot == 0, offset, speed)[:, 0:2]


def body(positions, velocity, density, counts, contact_mask, destination, tool):
    cols, rows, slots = density.shape
    ncut, ndepth = lax.axis_size("cut"), lax.axis_size("depth")
    scale = 1.0 / (ncut * cols * ndepth * rows * slots)
    near = 8 if ncut % 8 == 0 else 1
    far = ncut // near
    size = 5 * cols * rows
    state, marking = shape(5, cols, rows, slots), shape(3, cols, rows, slots)
    message, vector = shape(ndepth, 32, slots), shape(2, slots)
    along_depth, along_plane, along_line = [shape(n, 1, slots) for n in (ndepth, 2 * ndepth, ncut // 2)]
    both = ("cut", "depth")
    pairs = range(0, ncut, 2)
    planes = [[(c + k) * ndepth + d for k in range(2) for d in range(ndepth)] for c in pairs]
    lines = [[(c + k) * ndepth + d for c in pairs] for k in range(2) for d in range(ndepth)]
    ring = shape(5, cols + 2, rows + 2, slots)
    block_rates = shape(3, cols, rows, slots)
    swap = [(i, i ^ 1) for i in range(ncut)]
    cross = [(i, i + 1 if i % 2 else i - 1) for i in range(1, ncut - 1)]

    def rates_of(kernel, out, arrays, read, summed, rest=()):
        scratch = [pltpu.VMEM((n * 16, slots), F32) for n in (read, summed, summed)] + list(rest)
        return call(lambda *refs: kernel((cols, rows), *refs), out, (), arrays, scratch, COST)

    def exchange(own, marks, sent):
        got = lax.all_to_all(sent, "depth", 0, 0, tiled=True)
        inner = rates_of(inner_rates_kernel, block_rates, (own, marks), cols * rows, cols * rows)
        wide = call(extend_kernel, shape(6 * cols + 1, rows + 2 * HALO, slots), (), (own, marks, got, inner))
        swapped, other = lax.ppermute(wide, "cut", swap), lax.ppermute(wide, "cut", cross)
        force = call(pair_force_kernel, along_line, (), (wide, swapped))
        total = lax.all_to_all(force, both, 0, 0, tiled=True, axis_index_groups=lines)
        return (wide, swapped, other), inner, total

    def wide_rates(around, inner, first, last):
        out = shape(3, last - first, rows + 2, slots)
        read, summed = (last - first + 2) * (rows + 4), (last - first) * (rows + 2)
        return rates_of(functools.partial(wide_rates_kernel, range(first, last)), out, (*around, inner), read, summed)

    inputs = (positions, velocity, density, counts, contact_mask, destination[None], tool[None])
    own, marks, route, sent = pl.pallas_call(
        functools.partial(start_kernel, near),
        out_shape=[state, marking, jax.ShapeDtypeStruct((16, slots), jnp.int32), message],
        in_specs=[pl.BlockSpec(memory_space=pl.ANY)] * 7,
        out_specs=[VMEM] * 4,
        scratch_shapes=[pltpu.VMEM(part.shape, part.dtype) for part in inputs[3:]] + [pltpu.SemaphoreType.DMA((7,))],
        compiler_params=pltpu.CompilerParams(vmem_limit_bytes=60 * 1024 * 1024),
    )(*inputs)
    around, inner, total = exchange(own, marks, sent)
    found = wide_rates(around, inner, 1, 3 * cols - 1)
    rest = (pltpu.VMEM(ring.shape, F32),)
    read, summed = (cols + 2) * (rows + 2), cols * rows
    own, found = rates_of(first_update_kernel, [state, block_rates], (own, found, marks, *around), read, summed, rest)

    kernel = functools.partial(second_update_kernel, scale)
    own, tool, sent = call(kernel, [state, vector, message], (), (own, found, marks, total))

    around, inner, total = exchange(own, marks, sent)
    kernel = functools.partial(next_force_kernel, scale)
    tool, force = call(kernel, [vector, along_plane], (), (own, marks, tool, total))
    got = lax.all_to_all(force, both, 0, 0, tiled=True, axis_index_groups=planes)
    middle = 3 * cols // 2
    first_found = wide_rates(around, inner, 1, middle)
    force = call(spread_kernel, along_line, (), (got, first_found))
    total = lax.all_to_all(force, both, 0, 0, tiled=True, axis_index_groups=lines)
    last_found = wide_rates(around, inner, middle, 3 * cols - 1)
    own, ringed = call(third_update_kernel, [state, ring], (), (own, first_found, last_found, marks, *around, tool))
    found = rates_of(rates_kernel, block_rates, (ringed,), (cols + 2) * (rows + 2), cols * rows)
    kernel = functools.partial(next_force_kernel, scale)
    tool, force = call(kernel, [vector, along_depth], (), (own, marks, tool, total))
    total = lax.all_to_all(force, "depth", 0, 0, tiled=True)
    kernel = functools.partial(last_kernel, near)
    sent = call(kernel, shape(near, size + 8, slots), (), (route, own, found, marks, tool, total))
    close = [[g * near + k for k in range(near)] for g in range(far)]
    apart = [[g * near + k for g in range(far)] for k in range(near)]
    got = lax.all_to_all(sent, "cut", 0, 0, tiled=True, axis_index_groups=close)
    sent = call(functools.partial(sort_kernel, near, size), shape(far, size + 8, slots), (), (route, got))
    got = lax.all_to_all(sent, "cut", 0, 0, tiled=True, axis_index_groups=apart)
    moved, tool = call(functools.partial(take_kernel, near, scale), [state, shape(1, 2)], (), (route, got, tool))
    return moved, tool[0]


def solution(mesh):
    return jax.shard_map(
        body,
        mesh=mesh,
        in_specs=(
            P(None, "cut", "depth", None),
            P(None, "cut", "depth", None),
            P("cut", "depth", None),
            P("cut", "depth"),
            P("cut", "depth"),
            P(),
            P(),
        ),
        out_specs=(P(None, "cut", "depth", None), P()),
        check_vma=False,
    )
```

```python
import functools

import jax
import jax.numpy as jnp
from jax import lax
from jax.experimental import pallas as pl
from jax.experimental.pallas import tpu as pltpu
from jax.sharding import PartitionSpec as P

HALO = 2
MASS = 0.02
SOUND = 20.0
VISCOSITY = 2.0
STIFF = 50.0
DT = 0.05

FAR = 1.0e6

ROWS = 32

COST = 20_000_000_000

F32 = jnp.float32
BF16 = jnp.bfloat16
PARAMS = pltpu.CompilerParams(vmem_limit_bytes=40 * 1024 * 1024)
VMEM = pl.BlockSpec(memory_space=pltpu.VMEM)
SMEM = pl.BlockSpec(memory_space=pltpu.SMEM)


def here():
    return lax.axis_index("cut")


def row_block():
    return lax.axis_index("depth")


def shape(*dims):
    return jax.ShapeDtypeStruct(dims, F32)


def call(kernel, outs, scalars, arrays, scratch=(), estimate=0):
    return pl.pallas_call(
        kernel,
        out_shape=outs,
        in_specs=[SMEM] * len(scalars) + [VMEM] * len(arrays),
        out_specs=[VMEM] * len(outs) if isinstance(outs, list) else VMEM,
        scratch_shapes=scratch,
        compiler_params=PARAMS,
        cost_estimate=pl.CostEstimate(flops=estimate, bytes_accessed=1 << 20, transcendentals=0) if estimate else None,
    )(*scalars, *arrays)


def pressure(s):
    inv = 1.0 / s
    return SOUND * (s - 1.0) * inv * inv, inv


def penalties(x, touch, live, offset, column):
    return touch * live * jnp.maximum(0.0, x - column + offset - 0.5)


def own_force(new, marks, offset, first):
    total = 0.0
    for c, fields in enumerate(new):
        total = total + STIFF * penalties(fields[0], marks[1, c], marks[0, c], offset, first + c)
    total = jnp.sum(total, axis=0, keepdims=True)
    return jnp.broadcast_to(jnp.sum(total, axis=1, keepdims=True), total.shape)


def visible(fields, live, touch):
    alive = live > 0
    x, y, u, v, rho = fields
    return [jnp.where(alive, x, FAR), y, u, v, jnp.where(alive, rho, 1.0), live * touch]


def fill_depth(state, marks, force, sent):
    depth, ndepth = row_block(), sent.shape[0]
    cols, rows = marks.shape[1:3]
    row = 6 * cols * HALO
    sent[...] = jnp.zeros(sent.shape, F32)
    sent[:, row : row + 1, :] = jnp.broadcast_to(force[None], (ndepth, 1, force.shape[1]))
    seen = [visible(state[c], marks[0, c], marks[1, c]) for c in range(cols)]

    def put(target, rim):
        for c in range(cols):
            for f in range(6):
                at = (f * cols + c) * HALO
                sent[target, at : at + HALO] = seen[c][f][rim : rim + HALO]

    @pl.when(depth > 0)
    def _():
        put(depth - 1, 0)

    @pl.when(depth < ndepth - 1)
    def _():
        put(depth + 1, rows - HALO)


def origin(cols, rows):
    first = (here() * cols).astype(F32)
    return first + 0.5 * cols, (row_block() * rows).astype(F32) + 0.5 * rows, first


def start_kernel(near, *refs):
    inputs, (own, marks, route, sent), (counts, contact, target, first_tool, arrived) = refs[:7], refs[7:11], refs[11:]
    homes = [own.at[0:2], own.at[2:4], own.at[4], counts, contact, target, first_tool]
    copies = [pltpu.make_async_copy(part, to, arrived.at[n]) for n, (part, to) in enumerate(zip(inputs, homes))]
    for copy in copies:
        copy.start()
    for copy in copies:
        copy.wait()
    cols, rows, slots = own.shape[1:]
    row = lax.broadcasted_iota(jnp.int32, (rows, slots), 0)
    slot = lax.broadcasted_iota(jnp.int32, (rows, slots), 1)
    for c in range(cols):
        filled = jnp.zeros((rows, slots), jnp.int32)
        touch = jnp.zeros((rows, slots), jnp.int32)
        for r in range(rows):
            filled = jnp.where(row == r, counts[c : c + 1, r : r + 1], filled)
            touch = jnp.where(row == r, contact[c : c + 1, r : r + 1], touch)
        marks[0, c] = jnp.where(slot < filled, 1.0, 0.0)
        marks[1, c] = touch.astype(F32)
    new = [[own[f, c] for f in range(5)] for c in range(cols)]
    offset = jnp.broadcast_to(first_tool[0:1, 0:1], (1, slots))
    marks[2, 0] = jnp.broadcast_to(offset, (rows, slots))
    marks[2, 1] = jnp.broadcast_to(first_tool[0:1, 1:2], (rows, slots))
    fill_depth(new, marks, own_force(new, marks, offset, origin(cols, rows)[2]), sent)

    block = lax.broadcasted_iota(jnp.int32, target.shape, 1)

    def entry(at):
        return jnp.sum(jnp.where(block == at, target[...], 0), axis=1, keepdims=True)

    route[...] = jnp.zeros(route.shape, jnp.int32)
    route[0:1] = jnp.broadcast_to(entry(here()), (1, slots))
    source = jnp.sum(jnp.where(target[...] == here(), block, 0), axis=1, keepdims=True)
    route[1:2] = jnp.broadcast_to(source, (1, slots))
    group = lax.div(here(), near)
    for k in range(near):
        route[2 + k : 3 + k] = jnp.broadcast_to(entry(group * near + k), (1, slots))


def extend_kernel(own, marks, got, inner, wide):
    depth, ndepth = row_block(), got.shape[0]
    cols, rows = own.shape[1:3]
    above = got[jnp.maximum(depth - 1, 0)]
    below = got[jnp.minimum(depth + 1, ndepth - 1)]
    blank = [FAR, 0.0, 0.0, 0.0, 1.0, 0.0]
    for c in range(cols):
        seen = visible([own[f, c] for f in range(5)], marks[0, c], marks[1, c])
        for f in range(6):
            at = (f * cols + c) * HALO
            wide[f * cols + c, 0:HALO] = jnp.where(depth > 0, above[at : at + HALO], blank[f])
            wide[f * cols + c, HALO : rows + HALO] = seen[f]
            wide[f * cols + c, rows + HALO :] = jnp.where(depth < ndepth - 1, below[at : at + HALO], blank[f])
    row = 6 * cols * HALO
    wide[6 * cols] = jnp.broadcast_to(jnp.sum(got[:, row : row + 1, :], axis=0), wide.shape[1:])


def pair_force_kernel(wide, swapped, force):
    last = wide.shape[0] - 1
    force[...] = jnp.broadcast_to((wide[last, 0:1] + swapped[last, 0:1])[None], force.shape)


def spread_kernel(got, before, force):
    force[...] = jnp.broadcast_to(jnp.sum(got[...], axis=0, keepdims=True), force.shape)


def pair_sums(columns, center, pairs, out, feat, acc2, acc3, earlier={}):
    x0, y0, _ = center
    tall, slots = columns[0][0].shape
    row0 = min(r for _, r in pairs)
    rows = 1 + max(r for _, r in pairs) - row0
    for c, (x, y, u, v, s) in enumerate(columns):
        lx, ly = x - x0, y - y0
        press, inv = pressure(s)
        parts = [jnp.ones_like(x), lx, ly, press, press * lx, press * ly, u, v, u * lx + v * ly, inv, inv * u, inv * v]
        highs = [part.astype(BF16).astype(F32) for part in parts]
        lows = [part - high for part, high in zip(parts, highs)]
        for k, part in enumerate(highs + lows + [jnp.zeros_like(x)] * (ROWS - 24)):
            feat[pl.ds(c * tall * ROWS + k, tall, stride=ROWS), :] = part
    for i, ((c, r), around) in enumerate(pairs.items()):
        xi, yi = [jnp.broadcast_to(f[r : r + 1], (slots, slots)).T for f in columns[c][:2]]

        def weights(a, b):
            dx = xi - columns[a][0][b : b + 1]
            dy = yi - columns[a][1][b : b + 1]
            q = jnp.maximum(0.0, 1.0 - dx * dx - dy * dy).astype(BF16)
            q2 = q * q
            return jnp.concatenate([q2, q2 * q], axis=0)

        total = None
        for n in range(0, len(around), 2):
            pair = around[n : n + 2]
            w = jnp.concatenate([weights(a, b) for a, b in pair], axis=1)
            f = jnp.concatenate([feat[pl.ds((a * tall + b) * ROWS, ROWS), :] for a, b in pair], axis=1).astype(BF16)
            found = lax.dot_general(f, w, (((1,), (1,)), ((), ())), preferred_element_type=F32)
            total = found if total is None else total + found
        acc2[i * ROWS : (i + 1) * ROWS] = total[:, :slots]
        acc3[i * ROWS : (i + 1) * ROWS] = total[:, slots:]

    for n, c in enumerate(sorted({c for c, _ in pairs})):

        def summed(k):
            acc = acc2 if k < 9 else acc3
            return sum(acc[pl.ds(n * rows * ROWS + k + low, rows, stride=ROWS), :] for low in (0, 12))

        x, y, u, v, s = [f[row0 : row0 + rows] for f in columns[c]]
        x, y = x - x0, y - y0
        press, _ = pressure(s)
        a0, ax, ay, ap, apx, apy, au, av, aw, b0, bu, bv = [summed(k) for k in range(12)]
        sx, sy = x * a0 - ax, y * a0 - ay
        rates = [
            (6.0 * MASS) * (press * sx + x * ap - apx) - (VISCOSITY * MASS) * (u * b0 - bu),
            (6.0 * MASS) * (press * sy + y * ap - apy) - (VISCOSITY * MASS) * (v * b0 - bv),
            (-6.0 * MASS) * (u * sx + v * sy - x * au - y * av + aw),
        ]
        for f in range(3):
            out[f, n] = rates[f]
            if c in earlier:
                out[f, n, 1 : rows - 1] = rates[f][1 : rows - 1] + earlier[c][f]


def around_cell(c, r):
    return [(c + a, r + b) for a in (-1, 0, 1) for b in (-1, 0, 1)]


def inner_rates_kernel(size, own, marks, out, feat, acc2, acc3):
    cols, rows = size
    columns = [visible([own[f, c] for f in range(5)], marks[0, c], marks[1, c])[:5] for c in range(cols)]
    cells = [(c, r) for c in range(cols) for r in range(rows)]
    pairs = {cell: [j for j in around_cell(*cell) if j in cells] for cell in cells}
    pair_sums(columns, origin(*size), pairs, out, feat, acc2, acc3)


def wide_columns(cols, wide, swapped, other):
    even = lax.rem(here(), 2) == 0
    blank = [FAR, 0.0, 0.0, 0.0, 1.0, 0.0]
    columns = []
    for side in range(3):
        outside = here() == (0 if side == 0 else lax.axis_size("cut") - 1)
        for c in range(cols):
            if side == 1:
                fields = [wide[f * cols + c] for f in range(6)]
            else:
                first, second = (other, swapped) if side == 0 else (swapped, other)
                fields = [jnp.where(outside, blank[f], jnp.where(even, first[f * cols + c], second[f * cols + c])) for f in range(6)]
            columns.append(fields)
    return columns


def wide_rates_kernel(wanted, size, wide, swapped, other, inner, out, feat, acc2, acc3):
    cols, rows = size
    start, stop = wanted[0] - 1, wanted[-1] + 2
    columns = [fields[:5] for fields in wide_columns(cols, wide, swapped, other)[start:stop]]
    block = [(c + cols, r + HALO) for c in range(cols) for r in range(rows)]
    pairs = {}
    for c in wanted:
        for r in range(1, rows + 3):
            around = [j for j in around_cell(c, r) if (c, r) not in block or j not in block]
            pairs[c - start, r] = [(a - start, b) for a, b in around]
    earlier = {c + cols - start: [inner[f, c] for f in range(3)] for c in range(cols)}
    pair_sums(columns, origin(*size), pairs, out, feat, acc2, acc3, earlier)


def rates_kernel(size, ring, out, feat, acc2, acc3):
    cols, rows = size
    columns = [[ring[f, c] for f in range(5)] for c in range(cols + 2)]
    pairs = {(c, r): around_cell(c, r) for c in range(1, cols + 1) for r in range(1, rows + 1)}
    pair_sums(columns, origin(*size), pairs, out, feat, acc2, acc3)


def by_column(*found):
    return [[part[f, n] for f in range(3)] for part in found for n in range(part.shape[1])]


def moved_ring(columns, found, offset, first, ring):
    for n in range(ring.shape[1]):
        x, y, u, v, s, touch = [f[1:-1] for f in columns[n + 1]]
        live = jnp.where(x < 0.5 * FAR, 1.0, 0.0)
        pen = touch * jnp.maximum(0.0, x - (first + (n - 1)) + offset - 0.5)
        u = u + DT * live * (found[n][0] - STIFF * pen)
        v = v + DT * live * found[n][1]
        ring[0, n] = x + DT * live * u
        ring[1, n] = y + DT * live * v
        ring[2, n] = u
        ring[3, n] = v
        ring[4, n] = s + DT * live * found[n][2]


def moved_state(own, found, marks, offset, first):
    cols, rows = own.shape[1:3]
    side, rim = (len(found) - cols) // 2, (found[0][0].shape[0] - rows) // 2
    new = []
    for c in range(cols):
        live = marks[0, c]
        ax, ay, drho = [part[rim : rim + rows] for part in found[c + side]]
        pen = penalties(own[0, c], marks[1, c], live, offset, first + c)
        u = own[2, c] + DT * live * (ax - STIFF * pen)
        v = own[3, c] + DT * live * ay
        x = own[0, c] + DT * live * u
        y = own[1, c] + DT * live * v
        rho = own[4, c] + DT * live * drho
        new.append([x, y, u, v, rho])
    return new


def keep(new, own):
    for c, fields in enumerate(new):
        for f in range(5):
            own[f, c] = fields[f]


def tool_step(offset, speed, force, scale):
    speed = speed + DT * (1.0 - force * scale)
    return offset + DT * speed, speed


def first_update_kernel(size, own, found, marks, wide, swapped, other, new_own, out, feat, acc2, acc3, ring):
    first = origin(*size)[2]
    offset = marks[2, 0, 0:1]
    found = by_column(found)
    keep(moved_state(own, found, marks, offset, first), new_own)
    moved_ring(wide_columns(size[0], wide, swapped, other), found, offset, first, ring)
    rates_kernel(size, ring, out, feat, acc2, acc3)


def second_update_kernel(scale, own, found, marks, total, new_own, new_tool, sent):
    first = origin(*own.shape[1:3])[2]
    offset, speed = tool_step(marks[2, 0, 0:1], marks[2, 1, 0:1], jnp.sum(total[...], axis=0), scale)
    new_tool[0:1] = offset
    new_tool[1:2] = speed
    state = [[own[f, c] for f in range(5)] for c in range(own.shape[1])]
    new = moved_state(own, by_column(found), marks, offset, first)
    keep(new, new_own)
    fill_depth(new, marks, own_force(state, marks, offset, first), sent)


def third_update_kernel(own, first_found, last_found, marks, wide, swapped, other, tool, new_own, ring):
    first = origin(*own.shape[1:3])[2]
    found = by_column(first_found, last_found)
    keep(moved_state(own, found, marks, tool[0:1], first), new_own)
    moved_ring(wide_columns(own.shape[1], wide, swapped, other), found, tool[0:1], first, ring)


def next_force_kernel(scale, own, marks, tool, total, new_tool, force):
    offset, speed = tool_step(tool[0:1], tool[1:2], jnp.sum(total[...], axis=0), scale)
    new_tool[0:1] = offset
    new_tool[1:2] = speed
    state = [[own[f, c] for f in range(5)] for c in range(own.shape[1])]
    part = own_force(state, marks, offset, origin(*own.shape[1:3])[2])
    force[...] = jnp.broadcast_to(part[None], force.shape)


def last_kernel(near, route, own, found, marks, tool, total, sent):
    cols, rows, slots = own.shape[1:]
    size = 5 * cols * rows
    new = moved_state(own, by_column(found), marks, tool[0:1], origin(cols, rows)[2])
    sent[:, size:, :] = jnp.broadcast_to(jnp.sum(total[...], axis=0, keepdims=True), (near, sent.shape[1] - size, slots))
    target = route[0:1]
    for k in range(near):
        chosen = jnp.bitwise_and(target, near - 1) == k
        for f in range(5):
            for c in range(cols):
                at = (f * cols + c) * rows
                sent[k, at : at + rows] = jnp.where(chosen, new[c][f], 0.0)


def sort_kernel(near, size, route, got, sent):
    far, most, slots = sent.shape
    digit = lax.rem(here(), near)
    total = jnp.sum(got[:, size : size + 1, :], axis=0, keepdims=True)
    sent[:, size:, :] = jnp.broadcast_to(total, (far, most - size, slots))
    for g in range(far):
        block = jnp.zeros((size, slots), F32)
        for k in range(near):
            block = jnp.where(route[2 + k : 3 + k] == g * near + digit, got[k, 0:size], block)
        sent[g, 0:size] = block


def take_kernel(near, scale, route, got, tool, out, new_tool):
    cols, rows, slots = out.shape[1:]
    size = 5 * cols * rows
    source = route[1:2]
    for f in range(5):
        for c in range(cols):
            at = (f * cols + c) * rows
            field = got[0, at : at + rows]
            for g in range(1, got.shape[0]):
                field = jnp.where(source >= g * near, got[g, at : at + rows], field)
            out[f, c] = field
    offset, speed = tool_step(tool[0:1], tool[1:2], jnp.sum(got[:, size : size + 1, :], axis=0), scale)
    slot = lax.broadcasted_iota(jnp.int32, (1, slots), 1)
    new_tool[...] = jnp.where(slot == 0, offset, speed)[:, 0:2]


def body(positions, velocity, density, counts, contact_mask, destination, tool):
    cols, rows, slots = density.shape
    ncut, ndepth = lax.axis_size("cut"), lax.axis_size("depth")
    scale = 1.0 / (ncut * cols * ndepth * rows * slots)
    near = 8 if ncut % 8 == 0 else 1
    far = ncut // near
    size = 5 * cols * rows
    state, marking = shape(5, cols, rows, slots), shape(3, cols, rows, slots)
    message, vector = shape(ndepth, 32, slots), shape(2, slots)
    along_depth, along_plane, along_line = [shape(n, 1, slots) for n in (ndepth, 2 * ndepth, ncut // 2)]
    both = ("cut", "depth")
    pairs = range(0, ncut, 2)
    planes = [[(c + k) * ndepth + d for k in range(2) for d in range(ndepth)] for c in pairs]
    lines = [[(c + k) * ndepth + d for c in pairs] for k in range(2) for d in range(ndepth)]
    ring = shape(5, cols + 2, rows + 2, slots)
    block_rates = shape(3, cols, rows, slots)
    swap = [(i, i ^ 1) for i in range(ncut)]
    cross = [(i, i + 1 if i % 2 else i - 1) for i in range(1, ncut - 1)]

    def rates_of(kernel, out, arrays, read, summed, rest=()):
        scratch = [pltpu.VMEM((n * ROWS, slots), F32) for n in (read, summed, summed)] + list(rest)
        return call(lambda *refs: kernel((cols, rows), *refs), out, (), arrays, scratch, COST)

    def exchange(own, marks, sent):
        got = lax.all_to_all(sent, "depth", 0, 0, tiled=True)
        inner = rates_of(inner_rates_kernel, block_rates, (own, marks), cols * rows, cols * rows)
        wide = call(extend_kernel, shape(6 * cols + 1, rows + 2 * HALO, slots), (), (own, marks, got, inner))
        swapped, other = lax.ppermute(wide, "cut", swap), lax.ppermute(wide, "cut", cross)
        force = call(pair_force_kernel, along_line, (), (wide, swapped))
        total = lax.all_to_all(force, both, 0, 0, tiled=True, axis_index_groups=lines)
        return (wide, swapped, other), inner, total

    def wide_rates(around, inner, first, last):
        out = shape(3, last - first, rows + 2, slots)
        read, summed = (last - first + 2) * (rows + 4), (last - first) * (rows + 2)
        return rates_of(functools.partial(wide_rates_kernel, range(first, last)), out, (*around, inner), read, summed)

    inputs = (positions, velocity, density, counts, contact_mask, destination[None], tool[None])
    own, marks, route, sent = pl.pallas_call(
        functools.partial(start_kernel, near),
        out_shape=[state, marking, jax.ShapeDtypeStruct((16, slots), jnp.int32), message],
        in_specs=[pl.BlockSpec(memory_space=pl.ANY)] * 7,
        out_specs=[VMEM] * 4,
        scratch_shapes=[pltpu.VMEM(part.shape, part.dtype) for part in inputs[3:]] + [pltpu.SemaphoreType.DMA((7,))],
        compiler_params=pltpu.CompilerParams(vmem_limit_bytes=60 * 1024 * 1024),
    )(*inputs)
    around, inner, total = exchange(own, marks, sent)
    found = wide_rates(around, inner, 1, 3 * cols - 1)
    rest = (pltpu.VMEM(ring.shape, F32),)
    read, summed = (cols + 2) * (rows + 2), cols * rows
    own, found = rates_of(first_update_kernel, [state, block_rates], (own, found, marks, *around), read, summed, rest)

    kernel = functools.partial(second_update_kernel, scale)
    own, tool, sent = call(kernel, [state, vector, message], (), (own, found, marks, total))

    around, inner, total = exchange(own, marks, sent)
    kernel = functools.partial(next_force_kernel, scale)
    tool, force = call(kernel, [vector, along_plane], (), (own, marks, tool, total))
    got = lax.all_to_all(force, both, 0, 0, tiled=True, axis_index_groups=planes)
    middle = 3 * cols // 2
    first_found = wide_rates(around, inner, 1, middle)
    force = call(spread_kernel, along_line, (), (got, first_found))
    total = lax.all_to_all(force, both, 0, 0, tiled=True, axis_index_groups=lines)
    last_found = wide_rates(around, inner, middle, 3 * cols - 1)
    own, ringed = call(third_update_kernel, [state, ring], (), (own, first_found, last_found, marks, *around, tool))
    found = rates_of(rates_kernel, block_rates, (ringed,), (cols + 2) * (rows + 2), cols * rows)
    kernel = functools.partial(next_force_kernel, scale)
    tool, force = call(kernel, [vector, along_depth], (), (own, marks, tool, total))
    total = lax.all_to_all(force, "depth", 0, 0, tiled=True)
    kernel = functools.partial(last_kernel, near)
    sent = call(kernel, shape(near, size + 8, slots), (), (route, own, found, marks, tool, total))
    close = [[g * near + k for k in range(near)] for g in range(far)]
    apart = [[g * near + k for g in range(far)] for k in range(near)]
    got = lax.all_to_all(sent, "cut", 0, 0, tiled=True, axis_index_groups=close)
    sent = call(functools.partial(sort_kernel, near, size), shape(far, size + 8, slots), (), (route, got))
    got = lax.all_to_all(sent, "cut", 0, 0, tiled=True, axis_index_groups=apart)
    moved, tool = call(functools.partial(take_kernel, near, scale), [state, shape(1, 2)], (), (route, got, tool))
    return moved, tool[0]


def solution(mesh):
    return jax.shard_map(
        body,
        mesh=mesh,
        in_specs=(
            P(None, "cut", "depth", None),
            P(None, "cut", "depth", None),
            P("cut", "depth", None),
            P("cut", "depth"),
            P("cut", "depth"),
            P(),
            P(),
        ),
        out_specs=(P(None, "cut", "depth", None), P()),
        check_vma=False,
    )
```

```python
import functools

import jax
import jax.numpy as jnp
from jax import lax
from jax.experimental import pallas as pl
from jax.experimental.pallas import tpu as pltpu
from jax.sharding import PartitionSpec as P

HALO = 2
MASS = 0.02
SOUND = 20.0
VISCOSITY = 2.0
STIFF = 50.0
DT = 0.05

FAR = 1.0e6

ROWS = 32

COST = 20_000_000_000

F32 = jnp.float32
BF16 = jnp.bfloat16
PARAMS = pltpu.CompilerParams(vmem_limit_bytes=40 * 1024 * 1024)
VMEM = pl.BlockSpec(memory_space=pltpu.VMEM)
SMEM = pl.BlockSpec(memory_space=pltpu.SMEM)


def here():
    return lax.axis_index("cut")


def row_block():
    return lax.axis_index("depth")


def shape(*dims):
    return jax.ShapeDtypeStruct(dims, F32)


def call(kernel, outs, scalars, arrays, scratch=(), estimate=0):
    return pl.pallas_call(
        kernel,
        out_shape=outs,
        in_specs=[SMEM] * len(scalars) + [VMEM] * len(arrays),
        out_specs=[VMEM] * len(outs) if isinstance(outs, list) else VMEM,
        scratch_shapes=scratch,
        compiler_params=PARAMS,
        cost_estimate=pl.CostEstimate(flops=estimate, bytes_accessed=1 << 20, transcendentals=0) if estimate else None,
    )(*scalars, *arrays)


def pressure(s):
    inv = 1.0 / s
    return SOUND * (s - 1.0) * inv * inv, inv


def penalties(x, touch, live, offset, column):
    return touch * live * jnp.maximum(0.0, x - column + offset - 0.5)


def own_force(new, marks, offset, first):
    total = 0.0
    for c, fields in enumerate(new):
        total = total + STIFF * penalties(fields[0], marks[1, c], marks[0, c], offset, first + c)
    total = jnp.sum(total, axis=0, keepdims=True)
    return jnp.broadcast_to(jnp.sum(total, axis=1, keepdims=True), total.shape)


def visible(fields, live, touch):
    alive = live > 0
    x, y, u, v, rho = fields
    return [jnp.where(alive, x, FAR), y, u, v, jnp.where(alive, rho, 1.0), live * touch]


def fill_depth(state, marks, force, sent):
    depth, ndepth = row_block(), sent.shape[0]
    cols, rows = marks.shape[1:3]
    row = 6 * cols * HALO
    sent[...] = jnp.zeros(sent.shape, F32)
    sent[:, row : row + 1, :] = jnp.broadcast_to(force[None], (ndepth, 1, force.shape[1]))
    seen = [visible(state[c], marks[0, c], marks[1, c]) for c in range(cols)]

    def put(target, rim):
        for c in range(cols):
            for f in range(6):
                at = (f * cols + c) * HALO
                sent[target, at : at + HALO] = seen[c][f][rim : rim + HALO]

    @pl.when(depth > 0)
    def _():
        put(depth - 1, 0)

    @pl.when(depth < ndepth - 1)
    def _():
        put(depth + 1, rows - HALO)


def origin(cols, rows):
    first = (here() * cols).astype(F32)
    return first + 0.5 * cols, (row_block() * rows).astype(F32) + 0.5 * rows, first


def start_kernel(near, *refs):
    inputs, (own, marks, route, sent), (counts, contact, target, first_tool, arrived) = refs[:7], refs[7:11], refs[11:]
    homes = [own.at[0:2], own.at[2:4], own.at[4], counts, contact, target, first_tool]
    copies = [pltpu.make_async_copy(part, to, arrived.at[n]) for n, (part, to) in enumerate(zip(inputs, homes))]
    for copy in copies:
        copy.start()
    for copy in copies:
        copy.wait()
    cols, rows, slots = own.shape[1:]
    row = lax.broadcasted_iota(jnp.int32, (rows, slots), 0)
    slot = lax.broadcasted_iota(jnp.int32, (rows, slots), 1)
    for c in range(cols):
        filled = jnp.zeros((rows, slots), jnp.int32)
        touch = jnp.zeros((rows, slots), jnp.int32)
        for r in range(rows):
            filled = jnp.where(row == r, counts[c : c + 1, r : r + 1], filled)
            touch = jnp.where(row == r, contact[c : c + 1, r : r + 1], touch)
        marks[0, c] = jnp.where(slot < filled, 1.0, 0.0)
        marks[1, c] = touch.astype(F32)
    new = [[own[f, c] for f in range(5)] for c in range(cols)]
    offset = jnp.broadcast_to(first_tool[0:1, 0:1], (1, slots))
    marks[2, 0] = jnp.broadcast_to(offset, (rows, slots))
    marks[2, 1] = jnp.broadcast_to(first_tool[0:1, 1:2], (rows, slots))
    fill_depth(new, marks, own_force(new, marks, offset, origin(cols, rows)[2]), sent)

    block = lax.broadcasted_iota(jnp.int32, target.shape, 1)

    def entry(at):
        return jnp.sum(jnp.where(block == at, target[...], 0), axis=1, keepdims=True)

    route[...] = jnp.zeros(route.shape, jnp.int32)
    route[0:1] = jnp.broadcast_to(entry(here()), (1, slots))
    source = jnp.sum(jnp.where(target[...] == here(), block, 0), axis=1, keepdims=True)
    route[1:2] = jnp.broadcast_to(source, (1, slots))
    group = lax.div(here(), near)
    for k in range(near):
        route[2 + k : 3 + k] = jnp.broadcast_to(entry(group * near + k), (1, slots))


def extend_kernel(own, marks, got, inner, wide):
    depth, ndepth = row_block(), got.shape[0]
    cols, rows = own.shape[1:3]
    above = got[jnp.maximum(depth - 1, 0)]
    below = got[jnp.minimum(depth + 1, ndepth - 1)]
    blank = [FAR, 0.0, 0.0, 0.0, 1.0, 0.0]
    for c in range(cols):
        seen = visible([own[f, c] for f in range(5)], marks[0, c], marks[1, c])
        for f in range(6):
            at = (f * cols + c) * HALO
            wide[f * cols + c, 0:HALO] = jnp.where(depth > 0, above[at : at + HALO], blank[f])
            wide[f * cols + c, HALO : rows + HALO] = seen[f]
            wide[f * cols + c, rows + HALO :] = jnp.where(depth < ndepth - 1, below[at : at + HALO], blank[f])
    row = 6 * cols * HALO
    wide[6 * cols] = jnp.broadcast_to(jnp.sum(got[:, row : row + 1, :], axis=0), wide.shape[1:])


def pair_force_kernel(wide, swapped, force):
    last = wide.shape[0] - 1
    force[...] = jnp.broadcast_to((wide[last, 0:1] + swapped[last, 0:1])[None], force.shape)


def spread_kernel(got, before, force):
    force[...] = jnp.broadcast_to(jnp.sum(got[...], axis=0, keepdims=True), force.shape)


def pair_sums(columns, center, pairs, out, feat, acc2, acc3, earlier={}):
    x0, y0, _ = center
    tall, slots = columns[0][0].shape
    row0 = min(r for _, r in pairs)
    rows = 1 + max(r for _, r in pairs) - row0
    for c, (x, y, u, v, s) in enumerate(columns):
        lx, ly = x - x0, y - y0
        press, inv = pressure(s)
        parts = [jnp.ones_like(x), lx, ly, press, press * lx, press * ly, u, v, u * lx + v * ly, inv, inv * u, inv * v]
        highs = [part.astype(BF16).astype(F32) for part in parts]
        lows = [part - high for part, high in zip(parts, highs)]
        for k, part in enumerate(highs + lows + [jnp.zeros_like(x)] * (ROWS - 24)):
            feat[pl.ds(c * tall * ROWS + k, tall, stride=ROWS), :] = part
    for i, ((c, r), around) in enumerate(pairs.items()):
        xi, yi = [jnp.broadcast_to(f[r : r + 1], (slots, slots)).T for f in columns[c][:2]]

        def weights(a, b):
            dx = xi - columns[a][0][b : b + 1]
            dy = yi - columns[a][1][b : b + 1]
            q = jnp.maximum(0.0, 1.0 - dx * dx - dy * dy).astype(BF16)
            q2 = q * q
            return jnp.concatenate([q2, q2 * q], axis=0)

        total = None
        for n in range(0, len(around), 2):
            pair = around[n : n + 2]
            w = jnp.concatenate([weights(a, b) for a, b in pair], axis=1)
            f = jnp.concatenate([feat[pl.ds((a * tall + b) * ROWS, ROWS), :] for a, b in pair], axis=1).astype(BF16)
            found = lax.dot_general(f, w, (((1,), (1,)), ((), ())), preferred_element_type=F32)
            total = found if total is None else total + found
        acc2[i * ROWS : (i + 1) * ROWS] = total[:, :slots]
        acc3[i * ROWS : (i + 1) * ROWS] = total[:, slots:]

    for n, c in enumerate(sorted({c for c, _ in pairs})):

        def summed(k):
            acc = acc2 if k < 9 else acc3
            return sum(acc[pl.ds(n * rows * ROWS + k + low, rows, stride=ROWS), :] for low in (0, 12))

        x, y, u, v, s = [f[row0 : row0 + rows] for f in columns[c]]
        x, y = x - x0, y - y0
        press, _ = pressure(s)
        a0, ax, ay, ap, apx, apy, au, av, aw, b0, bu, bv = [summed(k) for k in range(12)]
        sx, sy = x * a0 - ax, y * a0 - ay
        rates = [
            (6.0 * MASS) * (press * sx + x * ap - apx) - (VISCOSITY * MASS) * (u * b0 - bu),
            (6.0 * MASS) * (press * sy + y * ap - apy) - (VISCOSITY * MASS) * (v * b0 - bv),
            (-6.0 * MASS) * (u * sx + v * sy - x * au - y * av + aw),
        ]
        for f in range(3):
            out[f, n] = rates[f]
            if c in earlier:
                out[f, n, 1 : rows - 1] = rates[f][1 : rows - 1] + earlier[c][f]


def around_cell(c, r):
    return [(c + a, r + b) for a in (-1, 0, 1) for b in (-1, 0, 1)]


def inner_rates_kernel(size, own, marks, out, feat, acc2, acc3):
    cols, rows = size
    columns = [visible([own[f, c] for f in range(5)], marks[0, c], marks[1, c])[:5] for c in range(cols)]
    cells = [(c, r) for c in range(cols) for r in range(rows)]
    pairs = {cell: [j for j in around_cell(*cell) if j in cells] for cell in cells}
    pair_sums(columns, origin(*size), pairs, out, feat, acc2, acc3)


def wide_columns(cols, wide, swapped, other):
    even = lax.rem(here(), 2) == 0
    blank = [FAR, 0.0, 0.0, 0.0, 1.0, 0.0]
    columns = []
    for side in range(3):
        outside = here() == (0 if side == 0 else lax.axis_size("cut") - 1)
        for c in range(cols):
            if side == 1:
                fields = [wide[f * cols + c] for f in range(6)]
            else:
                first, second = (other, swapped) if side == 0 else (swapped, other)
                fields = [jnp.where(outside, blank[f], jnp.where(even, first[f * cols + c], second[f * cols + c])) for f in range(6)]
            columns.append(fields)
    return columns


def wide_rates_kernel(wanted, size, wide, swapped, other, inner, out, feat, acc2, acc3):
    cols, rows = size
    start, stop = wanted[0] - 1, wanted[-1] + 2
    columns = [fields[:5] for fields in wide_columns(cols, wide, swapped, other)[start:stop]]
    block = [(c + cols, r + HALO) for c in range(cols) for r in range(rows)]
    pairs = {}
    for c in wanted:
        for r in range(1, rows + 3):
            around = [j for j in around_cell(c, r) if (c, r) not in block or j not in block]
            pairs[c - start, r] = [(a - start, b) for a, b in around]
    earlier = {c + cols - start: [inner[f, c] for f in range(3)] for c in range(cols)}
    pair_sums(columns, origin(*size), pairs, out, feat, acc2, acc3, earlier)


def rates_kernel(size, ring, out, feat, acc2, acc3):
    cols, rows = size
    columns = [[ring[f, c] for f in range(5)] for c in range(cols + 2)]
    pairs = {(c, r): around_cell(c, r) for c in range(1, cols + 1) for r in range(1, rows + 1)}
    pair_sums(columns, origin(*size), pairs, out, feat, acc2, acc3)


def by_column(*found):
    return [[part[f, n] for f in range(3)] for part in found for n in range(part.shape[1])]


def moved_ring(columns, found, offset, first, ring):
    for n in range(ring.shape[1]):
        x, y, u, v, s, touch = [f[1:-1] for f in columns[n + 1]]
        live = jnp.where(x < 0.5 * FAR, 1.0, 0.0)
        pen = touch * jnp.maximum(0.0, x - (first + (n - 1)) + offset - 0.5)
        u = u + DT * live * (found[n][0] - STIFF * pen)
        v = v + DT * live * found[n][1]
        ring[0, n] = x + DT * live * u
        ring[1, n] = y + DT * live * v
        ring[2, n] = u
        ring[3, n] = v
        ring[4, n] = s + DT * live * found[n][2]


def moved_state(own, found, marks, offset, first):
    cols, rows = own.shape[1:3]
    side, rim = (len(found) - cols) // 2, (found[0][0].shape[0] - rows) // 2
    new = []
    for c in range(cols):
        live = marks[0, c]
        ax, ay, drho = [part[rim : rim + rows] for part in found[c + side]]
        pen = penalties(own[0, c], marks[1, c], live, offset, first + c)
        u = own[2, c] + DT * live * (ax - STIFF * pen)
        v = own[3, c] + DT * live * ay
        x = own[0, c] + DT * live * u
        y = own[1, c] + DT * live * v
        rho = own[4, c] + DT * live * drho
        new.append([x, y, u, v, rho])
    return new


def keep(new, own):
    for c, fields in enumerate(new):
        for f in range(5):
            own[f, c] = fields[f]


def tool_step(offset, speed, force, scale):
    speed = speed + DT * (1.0 - force * scale)
    return offset + DT * speed, speed


def first_update_kernel(size, own, found, marks, wide, swapped, other, new_own, out, feat, acc2, acc3, ring):
    first = origin(*size)[2]
    offset = marks[2, 0, 0:1]
    found = by_column(found)
    keep(moved_state(own, found, marks, offset, first), new_own)
    moved_ring(wide_columns(size[0], wide, swapped, other), found, offset, first, ring)
    rates_kernel(size, ring, out, feat, acc2, acc3)


def second_update_kernel(scale, own, found, marks, total, new_own, new_tool, sent):
    first = origin(*own.shape[1:3])[2]
    offset, speed = tool_step(marks[2, 0, 0:1], marks[2, 1, 0:1], jnp.sum(total[...], axis=0), scale)
    new_tool[0:1] = offset
    new_tool[1:2] = speed
    state = [[own[f, c] for f in range(5)] for c in range(own.shape[1])]
    new = moved_state(own, by_column(found), marks, offset, first)
    keep(new, new_own)
    fill_depth(new, marks, own_force(state, marks, offset, first), sent)


def third_update_kernel(own, first_found, last_found, marks, wide, swapped, other, tool, new_own, ring):
    first = origin(*own.shape[1:3])[2]
    found = by_column(first_found, last_found)
    keep(moved_state(own, found, marks, tool[0:1], first), new_own)
    moved_ring(wide_columns(own.shape[1], wide, swapped, other), found, tool[0:1], first, ring)


def next_force_kernel(scale, own, marks, tool, total, new_tool, force):
    offset, speed = tool_step(tool[0:1], tool[1:2], jnp.sum(total[...], axis=0), scale)
    new_tool[0:1] = offset
    new_tool[1:2] = speed
    state = [[own[f, c] for f in range(5)] for c in range(own.shape[1])]
    part = own_force(state, marks, offset, origin(*own.shape[1:3])[2])
    force[...] = jnp.broadcast_to(part[None], force.shape)


def last_kernel(near, route, own, found, marks, tool, total, sent):
    cols, rows, slots = own.shape[1:]
    size = 5 * cols * rows
    new = moved_state(own, by_column(found), marks, tool[0:1], origin(cols, rows)[2])
    sent[:, size:, :] = jnp.broadcast_to(jnp.sum(total[...], axis=0, keepdims=True), (near, sent.shape[1] - size, slots))
    target = route[0:1]
    for k in range(near):
        chosen = jnp.bitwise_and(target, near - 1) == k
        for f in range(5):
            for c in range(cols):
                at = (f * cols + c) * rows
                sent[k, at : at + rows] = jnp.where(chosen, new[c][f], 0.0)


def sort_kernel(near, size, route, got, sent):
    far, most, slots = sent.shape
    digit = lax.rem(here(), near)
    total = jnp.sum(got[:, size : size + 1, :], axis=0, keepdims=True)
    sent[:, size:, :] = jnp.broadcast_to(total, (far, most - size, slots))
    for g in range(far):
        block = jnp.zeros((size, slots), F32)
        for k in range(near):
            block = jnp.where(route[2 + k : 3 + k] == g * near + digit, got[k, 0:size], block)
        sent[g, 0:size] = block


def take_kernel(near, scale, route, got, tool, out, new_tool):
    cols, rows, slots = out.shape[1:]
    size = 5 * cols * rows
    source = route[1:2]
    for f in range(5):
        for c in range(cols):
            at = (f * cols + c) * rows
            field = got[0, at : at + rows]
            for g in range(1, got.shape[0]):
                field = jnp.where(source >= g * near, got[g, at : at + rows], field)
            out[f, c] = field
    offset, speed = tool_step(tool[0:1], tool[1:2], jnp.sum(got[:, size : size + 1, :], axis=0), scale)
    slot = lax.broadcasted_iota(jnp.int32, (1, slots), 1)
    new_tool[...] = jnp.where(slot == 0, offset, speed)[:, 0:2]


def body(positions, velocity, density, counts, contact_mask, destination, tool):
    cols, rows, slots = density.shape
    ncut, ndepth = lax.axis_size("cut"), lax.axis_size("depth")
    scale = 1.0 / (ncut * cols * ndepth * rows * slots)
    near = 4 if ncut % 4 == 0 else 1
    far = ncut // near
    size = 5 * cols * rows
    state, marking = shape(5, cols, rows, slots), shape(3, cols, rows, slots)
    message, vector = shape(ndepth, 32, slots), shape(2, slots)
    along_depth, along_plane, along_line = [shape(n, 1, slots) for n in (ndepth, 2 * ndepth, ncut // 2)]
    both = ("cut", "depth")
    pairs = range(0, ncut, 2)
    planes = [[(c + k) * ndepth + d for k in range(2) for d in range(ndepth)] for c in pairs]
    lines = [[(c + k) * ndepth + d for c in pairs] for k in range(2) for d in range(ndepth)]
    ring = shape(5, cols + 2, rows + 2, slots)
    block_rates = shape(3, cols, rows, slots)
    swap = [(i, i ^ 1) for i in range(ncut)]
    cross = [(i, i + 1 if i % 2 else i - 1) for i in range(1, ncut - 1)]

    def rates_of(kernel, out, arrays, read, summed, rest=()):
        scratch = [pltpu.VMEM((n * ROWS, slots), F32) for n in (read, summed, summed)] + list(rest)
        return call(lambda *refs: kernel((cols, rows), *refs), out, (), arrays, scratch, COST)

    def exchange(own, marks, sent):
        got = lax.all_to_all(sent, "depth", 0, 0, tiled=True)
        inner = rates_of(inner_rates_kernel, block_rates, (own, marks), cols * rows, cols * rows)
        wide = call(extend_kernel, shape(6 * cols + 1, rows + 2 * HALO, slots), (), (own, marks, got, inner))
        swapped, other = lax.ppermute(wide, "cut", swap), lax.ppermute(wide, "cut", cross)
        force = call(pair_force_kernel, along_line, (), (wide, swapped))
        total = lax.all_to_all(force, both, 0, 0, tiled=True, axis_index_groups=lines)
        return (wide, swapped, other), inner, total

    def wide_rates(around, inner, first, last):
        out = shape(3, last - first, rows + 2, slots)
        read, summed = (last - first + 2) * (rows + 4), (last - first) * (rows + 2)
        return rates_of(functools.partial(wide_rates_kernel, range(first, last)), out, (*around, inner), read, summed)

    inputs = (positions, velocity, density, counts, contact_mask, destination[None], tool[None])
    own, marks, route, sent = pl.pallas_call(
        functools.partial(start_kernel, near),
        out_shape=[state, marking, jax.ShapeDtypeStruct((16, slots), jnp.int32), message],
        in_specs=[pl.BlockSpec(memory_space=pl.ANY)] * 7,
        out_specs=[VMEM] * 4,
        scratch_shapes=[pltpu.VMEM(part.shape, part.dtype) for part in inputs[3:]] + [pltpu.SemaphoreType.DMA((7,))],
        compiler_params=pltpu.CompilerParams(vmem_limit_bytes=60 * 1024 * 1024),
    )(*inputs)
    around, inner, total = exchange(own, marks, sent)
    found = wide_rates(around, inner, 1, 3 * cols - 1)
    rest = (pltpu.VMEM(ring.shape, F32),)
    read, summed = (cols + 2) * (rows + 2), cols * rows
    own, found = rates_of(first_update_kernel, [state, block_rates], (own, found, marks, *around), read, summed, rest)

    kernel = functools.partial(second_update_kernel, scale)
    own, tool, sent = call(kernel, [state, vector, message], (), (own, found, marks, total))

    around, inner, total = exchange(own, marks, sent)
    kernel = functools.partial(next_force_kernel, scale)
    tool, force = call(kernel, [vector, along_plane], (), (own, marks, tool, total))
    got = lax.all_to_all(force, both, 0, 0, tiled=True, axis_index_groups=planes)
    middle = 3 * cols // 2
    first_found = wide_rates(around, inner, 1, middle)
    force = call(spread_kernel, along_line, (), (got, first_found))
    total = lax.all_to_all(force, both, 0, 0, tiled=True, axis_index_groups=lines)
    last_found = wide_rates(around, inner, middle, 3 * cols - 1)
    own, ringed = call(third_update_kernel, [state, ring], (), (own, first_found, last_found, marks, *around, tool))
    found = rates_of(rates_kernel, block_rates, (ringed,), (cols + 2) * (rows + 2), cols * rows)
    kernel = functools.partial(next_force_kernel, scale)
    tool, force = call(kernel, [vector, along_depth], (), (own, marks, tool, total))
    total = lax.all_to_all(force, "depth", 0, 0, tiled=True)
    kernel = functools.partial(last_kernel, near)
    sent = call(kernel, shape(near, size + 8, slots), (), (route, own, found, marks, tool, total))
    close = [[g * near + k for k in range(near)] for g in range(far)]
    apart = [[g * near + k for g in range(far)] for k in range(near)]
    got = lax.all_to_all(sent, "cut", 0, 0, tiled=True, axis_index_groups=close)
    sent = call(functools.partial(sort_kernel, near, size), shape(far, size + 8, slots), (), (route, got))
    got = lax.all_to_all(sent, "cut", 0, 0, tiled=True, axis_index_groups=apart)
    moved, tool = call(functools.partial(take_kernel, near, scale), [state, shape(1, 2)], (), (route, got, tool))
    return moved, tool[0]


def solution(mesh):
    return jax.shard_map(
        body,
        mesh=mesh,
        in_specs=(
            P(None, "cut", "depth", None),
            P(None, "cut", "depth", None),
            P("cut", "depth", None),
            P("cut", "depth"),
            P("cut", "depth"),
            P(),
            P(),
        ),
        out_specs=(P(None, "cut", "depth", None), P()),
        check_vma=False,
    )
```

```python
import functools

import jax
import jax.numpy as jnp
from jax import lax
from jax.experimental import pallas as pl
from jax.experimental.pallas import tpu as pltpu
from jax.sharding import PartitionSpec as P

HALO = 2
MASS = 0.02
SOUND = 20.0
VISCOSITY = 2.0
STIFF = 50.0
DT = 0.05

FAR = 1.0e6

ROWS = 32

COST = 20_000_000_000

F32 = jnp.float32
BF16 = jnp.bfloat16
PARAMS = pltpu.CompilerParams(vmem_limit_bytes=40 * 1024 * 1024)
VMEM = pl.BlockSpec(memory_space=pltpu.VMEM)
SMEM = pl.BlockSpec(memory_space=pltpu.SMEM)


def here():
    return lax.axis_index("cut")


def row_block():
    return lax.axis_index("depth")


def shape(*dims):
    return jax.ShapeDtypeStruct(dims, F32)


def call(kernel, outs, scalars, arrays, scratch=(), estimate=0):
    return pl.pallas_call(
        kernel,
        out_shape=outs,
        in_specs=[SMEM] * len(scalars) + [VMEM] * len(arrays),
        out_specs=[VMEM] * len(outs) if isinstance(outs, list) else VMEM,
        scratch_shapes=scratch,
        compiler_params=PARAMS,
        cost_estimate=pl.CostEstimate(flops=estimate, bytes_accessed=1 << 20, transcendentals=0) if estimate else None,
    )(*scalars, *arrays)


def pressure(s):
    inv = 1.0 / s
    return SOUND * (s - 1.0) * inv * inv, inv


def penalties(x, touch, live, offset, column):
    return touch * live * jnp.maximum(0.0, x - column + offset - 0.5)


def own_force(new, marks, offset, first):
    total = 0.0
    for c, fields in enumerate(new):
        total = total + STIFF * penalties(fields[0], marks[1, c], marks[0, c], offset, first + c)
    total = jnp.sum(total, axis=0, keepdims=True)
    return jnp.broadcast_to(jnp.sum(total, axis=1, keepdims=True), total.shape)


def visible(fields, live, touch):
    alive = live > 0
    x, y, u, v, rho = fields
    return [jnp.where(alive, x, FAR), y, u, v, jnp.where(alive, rho, 1.0), live * touch]


def fill_depth(state, marks, force, sent):
    depth, ndepth = row_block(), sent.shape[0]
    cols, rows = marks.shape[1:3]
    row = 6 * cols * HALO
    sent[...] = jnp.zeros(sent.shape, F32)
    sent[:, row : row + 1, :] = jnp.broadcast_to(force[None], (ndepth, 1, force.shape[1]))
    seen = [visible(state[c], marks[0, c], marks[1, c]) for c in range(cols)]

    def put(target, rim):
        for c in range(cols):
            for f in range(6):
                at = (f * cols + c) * HALO
                sent[target, at : at + HALO] = seen[c][f][rim : rim + HALO]

    @pl.when(depth > 0)
    def _():
        put(depth - 1, 0)

    @pl.when(depth < ndepth - 1)
    def _():
        put(depth + 1, rows - HALO)


def origin(cols, rows):
    first = (here() * cols).astype(F32)
    return first + 0.5 * cols, (row_block() * rows).astype(F32) + 0.5 * rows, first


def start_kernel(near, *refs):
    inputs, (own, marks, route, sent), (counts, contact, target, first_tool, arrived) = refs[:7], refs[7:11], refs[11:]
    homes = [own.at[0:2], own.at[2:4], own.at[4], counts, contact, target, first_tool]
    copies = [pltpu.make_async_copy(part, to, arrived.at[n]) for n, (part, to) in enumerate(zip(inputs, homes))]
    for copy in copies:
        copy.start()
    for copy in copies:
        copy.wait()
    cols, rows, slots = own.shape[1:]
    row = lax.broadcasted_iota(jnp.int32, (rows, slots), 0)
    slot = lax.broadcasted_iota(jnp.int32, (rows, slots), 1)
    for c in range(cols):
        filled = jnp.zeros((rows, slots), jnp.int32)
        touch = jnp.zeros((rows, slots), jnp.int32)
        for r in range(rows):
            filled = jnp.where(row == r, counts[c : c + 1, r : r + 1], filled)
            touch = jnp.where(row == r, contact[c : c + 1, r : r + 1], touch)
        marks[0, c] = jnp.where(slot < filled, 1.0, 0.0)
        marks[1, c] = touch.astype(F32)
    new = [[own[f, c] for f in range(5)] for c in range(cols)]
    offset = jnp.broadcast_to(first_tool[0:1, 0:1], (1, slots))
    marks[2, 0] = jnp.broadcast_to(offset, (rows, slots))
    marks[2, 1] = jnp.broadcast_to(first_tool[0:1, 1:2], (rows, slots))
    fill_depth(new, marks, own_force(new, marks, offset, origin(cols, rows)[2]), sent)

    block = lax.broadcasted_iota(jnp.int32, target.shape, 1)

    def entry(at):
        return jnp.sum(jnp.where(block == at, target[...], 0), axis=1, keepdims=True)

    route[...] = jnp.zeros(route.shape, jnp.int32)
    route[0:1] = jnp.broadcast_to(entry(here()), (1, slots))
    source = jnp.sum(jnp.where(target[...] == here(), block, 0), axis=1, keepdims=True)
    route[1:2] = jnp.broadcast_to(source, (1, slots))
    group = lax.div(here(), near)
    for k in range(near):
        route[2 + k : 3 + k] = jnp.broadcast_to(entry(group * near + k), (1, slots))


def extend_kernel(own, marks, got, inner, wide):
    depth, ndepth = row_block(), got.shape[0]
    cols, rows = own.shape[1:3]
    above = got[jnp.maximum(depth - 1, 0)]
    below = got[jnp.minimum(depth + 1, ndepth - 1)]
    blank = [FAR, 0.0, 0.0, 0.0, 1.0, 0.0]
    for c in range(cols):
        seen = visible([own[f, c] for f in range(5)], marks[0, c], marks[1, c])
        for f in range(6):
            at = (f * cols + c) * HALO
            wide[f * cols + c, 0:HALO] = jnp.where(depth > 0, above[at : at + HALO], blank[f])
            wide[f * cols + c, HALO : rows + HALO] = seen[f]
            wide[f * cols + c, rows + HALO :] = jnp.where(depth < ndepth - 1, below[at : at + HALO], blank[f])
    row = 6 * cols * HALO
    wide[6 * cols] = jnp.broadcast_to(jnp.sum(got[:, row : row + 1, :], axis=0), wide.shape[1:])


def pair_force_kernel(wide, swapped, force):
    last = wide.shape[0] - 1
    force[...] = jnp.broadcast_to((wide[last, 0:1] + swapped[last, 0:1])[None], force.shape)


def spread_kernel(got, before, force):
    force[...] = jnp.broadcast_to(jnp.sum(got[...], axis=0, keepdims=True), force.shape)


def pair_sums(columns, center, pairs, out, feat, acc2, acc3, earlier={}):
    x0, y0, _ = center
    tall, slots = columns[0][0].shape
    row0 = min(r for _, r in pairs)
    rows = 1 + max(r for _, r in pairs) - row0
    for c, (x, y, u, v, s) in enumerate(columns):
        lx, ly = x - x0, y - y0
        press, inv = pressure(s)
        parts = [jnp.ones_like(x), lx, ly, press, press * lx, press * ly, u, v, u * lx + v * ly, inv, inv * u, inv * v]
        highs = [part.astype(BF16).astype(F32) for part in parts]
        lows = [part - high for part, high in zip(parts, highs)]
        for k, part in enumerate(highs + lows + [jnp.zeros_like(x)] * (ROWS - 24)):
            feat[pl.ds(c * tall * ROWS + k, tall, stride=ROWS), :] = part
    for i, ((c, r), around) in enumerate(pairs.items()):
        xi, yi = [jnp.broadcast_to(f[r : r + 1], (slots, slots)).T for f in columns[c][:2]]

        def weights(a, b):
            dx = xi - columns[a][0][b : b + 1]
            dy = yi - columns[a][1][b : b + 1]
            q = jnp.maximum(BF16(0.0), (1.0 - dx * dx - dy * dy).astype(BF16))
            q2 = q * q
            return jnp.concatenate([q2, q2 * q], axis=0)

        total = None
        for n in range(0, len(around), 2):
            pair = around[n : n + 2]
            w = jnp.concatenate([weights(a, b) for a, b in pair], axis=1)
            f = jnp.concatenate([feat[pl.ds((a * tall + b) * ROWS, ROWS), :] for a, b in pair], axis=1).astype(BF16)
            found = lax.dot_general(f, w, (((1,), (1,)), ((), ())), preferred_element_type=F32)
            total = found if total is None else total + found
        acc2[i * ROWS : (i + 1) * ROWS] = total[:, :slots]
        acc3[i * ROWS : (i + 1) * ROWS] = total[:, slots:]

    for n, c in enumerate(sorted({c for c, _ in pairs})):

        def summed(k):
            acc = acc2 if k < 9 else acc3
            return sum(acc[pl.ds(n * rows * ROWS + k + low, rows, stride=ROWS), :] for low in (0, 12))

        x, y, u, v, s = [f[row0 : row0 + rows] for f in columns[c]]
        x, y = x - x0, y - y0
        press, _ = pressure(s)
        a0, ax, ay, ap, apx, apy, au, av, aw, b0, bu, bv = [summed(k) for k in range(12)]
        sx, sy = x * a0 - ax, y * a0 - ay
        rates = [
            (6.0 * MASS) * (press * sx + x * ap - apx) - (VISCOSITY * MASS) * (u * b0 - bu),
            (6.0 * MASS) * (press * sy + y * ap - apy) - (VISCOSITY * MASS) * (v * b0 - bv),
            (-6.0 * MASS) * (u * sx + v * sy - x * au - y * av + aw),
        ]
        for f in range(3):
            out[f, n] = rates[f]
            if c in earlier:
                out[f, n, 1 : rows - 1] = rates[f][1 : rows - 1] + earlier[c][f]


def around_cell(c, r):
    return [(c + a, r + b) for a in (-1, 0, 1) for b in (-1, 0, 1)]


def inner_rates_kernel(size, own, marks, out, feat, acc2, acc3):
    cols, rows = size
    columns = [visible([own[f, c] for f in range(5)], marks[0, c], marks[1, c])[:5] for c in range(cols)]
    cells = [(c, r) for c in range(cols) for r in range(rows)]
    pairs = {cell: [j for j in around_cell(*cell) if j in cells] for cell in cells}
    pair_sums(columns, origin(*size), pairs, out, feat, acc2, acc3)


def wide_columns(cols, wide, swapped, other):
    even = lax.rem(here(), 2) == 0
    blank = [FAR, 0.0, 0.0, 0.0, 1.0, 0.0]
    columns = []
    for side in range(3):
        outside = here() == (0 if side == 0 else lax.axis_size("cut") - 1)
        for c in range(cols):
            if side == 1:
                fields = [wide[f * cols + c] for f in range(6)]
            else:
                first, second = (other, swapped) if side == 0 else (swapped, other)
                fields = [jnp.where(outside, blank[f], jnp.where(even, first[f * cols + c], second[f * cols + c])) for f in range(6)]
            columns.append(fields)
    return columns


def wide_rates_kernel(wanted, size, wide, swapped, other, inner, out, feat, acc2, acc3):
    cols, rows = size
    start, stop = wanted[0] - 1, wanted[-1] + 2
    columns = [fields[:5] for fields in wide_columns(cols, wide, swapped, other)[start:stop]]
    block = [(c + cols, r + HALO) for c in range(cols) for r in range(rows)]
    pairs = {}
    for c in wanted:
        for r in range(1, rows + 3):
            around = [j for j in around_cell(c, r) if (c, r) not in block or j not in block]
            pairs[c - start, r] = [(a - start, b) for a, b in around]
    earlier = {c + cols - start: [inner[f, c] for f in range(3)] for c in range(cols)}
    pair_sums(columns, origin(*size), pairs, out, feat, acc2, acc3, earlier)


def rates_kernel(size, ring, out, feat, acc2, acc3):
    cols, rows = size
    columns = [[ring[f, c] for f in range(5)] for c in range(cols + 2)]
    pairs = {(c, r): around_cell(c, r) for c in range(1, cols + 1) for r in range(1, rows + 1)}
    pair_sums(columns, origin(*size), pairs, out, feat, acc2, acc3)


def by_column(*found):
    return [[part[f, n] for f in range(3)] for part in found for n in range(part.shape[1])]


def moved_ring(columns, found, offset, first, ring):
    for n in range(ring.shape[1]):
        x, y, u, v, s, touch = [f[1:-1] for f in columns[n + 1]]
        live = jnp.where(x < 0.5 * FAR, 1.0, 0.0)
        pen = touch * jnp.maximum(0.0, x - (first + (n - 1)) + offset - 0.5)
        u = u + DT * live * (found[n][0] - STIFF * pen)
        v = v + DT * live * found[n][1]
        ring[0, n] = x + DT * live * u
        ring[1, n] = y + DT * live * v
        ring[2, n] = u
        ring[3, n] = v
        ring[4, n] = s + DT * live * found[n][2]


def moved_state(own, found, marks, offset, first):
    cols, rows = own.shape[1:3]
    side, rim = (len(found) - cols) // 2, (found[0][0].shape[0] - rows) // 2
    new = []
    for c in range(cols):
        live = marks[0, c]
        ax, ay, drho = [part[rim : rim + rows] for part in found[c + side]]
        pen = penalties(own[0, c], marks[1, c], live, offset, first + c)
        u = own[2, c] + DT * live * (ax - STIFF * pen)
        v = own[3, c] + DT * live * ay
        x = own[0, c] + DT * live * u
        y = own[1, c] + DT * live * v
        rho = own[4, c] + DT * live * drho
        new.append([x, y, u, v, rho])
    return new


def keep(new, own):
    for c, fields in enumerate(new):
        for f in range(5):
            own[f, c] = fields[f]


def tool_step(offset, speed, force, scale):
    speed = speed + DT * (1.0 - force * scale)
    return offset + DT * speed, speed


def first_update_kernel(size, own, found, marks, wide, swapped, other, new_own, out, feat, acc2, acc3, ring):
    first = origin(*size)[2]
    offset = marks[2, 0, 0:1]
    found = by_column(found)
    keep(moved_state(own, found, marks, offset, first), new_own)
    moved_ring(wide_columns(size[0], wide, swapped, other), found, offset, first, ring)
    rates_kernel(size, ring, out, feat, acc2, acc3)


def second_update_kernel(scale, own, found, marks, total, new_own, new_tool, sent):
    first = origin(*own.shape[1:3])[2]
    offset, speed = tool_step(marks[2, 0, 0:1], marks[2, 1, 0:1], jnp.sum(total[...], axis=0), scale)
    new_tool[0:1] = offset
    new_tool[1:2] = speed
    state = [[own[f, c] for f in range(5)] for c in range(own.shape[1])]
    new = moved_state(own, by_column(found), marks, offset, first)
    keep(new, new_own)
    fill_depth(new, marks, own_force(state, marks, offset, first), sent)


def third_update_kernel(own, first_found, last_found, marks, wide, swapped, other, tool, new_own, ring):
    first = origin(*own.shape[1:3])[2]
    found = by_column(first_found, last_found)
    keep(moved_state(own, found, marks, tool[0:1], first), new_own)
    moved_ring(wide_columns(own.shape[1], wide, swapped, other), found, tool[0:1], first, ring)


def next_force_kernel(scale, own, marks, tool, total, new_tool, force):
    offset, speed = tool_step(tool[0:1], tool[1:2], jnp.sum(total[...], axis=0), scale)
    new_tool[0:1] = offset
    new_tool[1:2] = speed
    state = [[own[f, c] for f in range(5)] for c in range(own.shape[1])]
    part = own_force(state, marks, offset, origin(*own.shape[1:3])[2])
    force[...] = jnp.broadcast_to(part[None], force.shape)


def last_kernel(near, route, own, found, marks, tool, total, sent):
    cols, rows, slots = own.shape[1:]
    size = 5 * cols * rows
    new = moved_state(own, by_column(found), marks, tool[0:1], origin(cols, rows)[2])
    sent[:, size:, :] = jnp.broadcast_to(jnp.sum(total[...], axis=0, keepdims=True), (near, sent.shape[1] - size, slots))
    target = route[0:1]
    for k in range(near):
        chosen = jnp.bitwise_and(target, near - 1) == k
        for f in range(5):
            for c in range(cols):
                at = (f * cols + c) * rows
                sent[k, at : at + rows] = jnp.where(chosen, new[c][f], 0.0)


def sort_kernel(near, size, route, got, sent):
    far, most, slots = sent.shape
    digit = lax.rem(here(), near)
    total = jnp.sum(got[:, size : size + 1, :], axis=0, keepdims=True)
    sent[:, size:, :] = jnp.broadcast_to(total, (far, most - size, slots))
    for g in range(far):
        block = jnp.zeros((size, slots), F32)
        for k in range(near):
            block = jnp.where(route[2 + k : 3 + k] == g * near + digit, got[k, 0:size], block)
        sent[g, 0:size] = block


def take_kernel(near, scale, route, got, tool, out, new_tool):
    cols, rows, slots = out.shape[1:]
    size = 5 * cols * rows
    source = route[1:2]
    for f in range(5):
        for c in range(cols):
            at = (f * cols + c) * rows
            field = got[0, at : at + rows]
            for g in range(1, got.shape[0]):
                field = jnp.where(source >= g * near, got[g, at : at + rows], field)
            out[f, c] = field
    offset, speed = tool_step(tool[0:1], tool[1:2], jnp.sum(got[:, size : size + 1, :], axis=0), scale)
    slot = lax.broadcasted_iota(jnp.int32, (1, slots), 1)
    new_tool[...] = jnp.where(slot == 0, offset, speed)[:, 0:2]


def body(positions, velocity, density, counts, contact_mask, destination, tool):
    cols, rows, slots = density.shape
    ncut, ndepth = lax.axis_size("cut"), lax.axis_size("depth")
    scale = 1.0 / (ncut * cols * ndepth * rows * slots)
    near = 8 if ncut % 8 == 0 else 1
    far = ncut // near
    size = 5 * cols * rows
    state, marking = shape(5, cols, rows, slots), shape(3, cols, rows, slots)
    message, vector = shape(ndepth, 32, slots), shape(2, slots)
    along_depth, along_plane, along_line = [shape(n, 1, slots) for n in (ndepth, 2 * ndepth, ncut // 2)]
    both = ("cut", "depth")
    pairs = range(0, ncut, 2)
    planes = [[(c + k) * ndepth + d for k in range(2) for d in range(ndepth)] for c in pairs]
    lines = [[(c + k) * ndepth + d for c in pairs] for k in range(2) for d in range(ndepth)]
    ring = shape(5, cols + 2, rows + 2, slots)
    block_rates = shape(3, cols, rows, slots)
    swap = [(i, i ^ 1) for i in range(ncut)]
    cross = [(i, i + 1 if i % 2 else i - 1) for i in range(1, ncut - 1)]

    def rates_of(kernel, out, arrays, read, summed, rest=()):
        scratch = [pltpu.VMEM((n * ROWS, slots), F32) for n in (read, summed, summed)] + list(rest)
        return call(lambda *refs: kernel((cols, rows), *refs), out, (), arrays, scratch, COST)

    def exchange(own, marks, sent):
        got = lax.all_to_all(sent, "depth", 0, 0, tiled=True)
        inner = rates_of(inner_rates_kernel, block_rates, (own, marks), cols * rows, cols * rows)
        wide = call(extend_kernel, shape(6 * cols + 1, rows + 2 * HALO, slots), (), (own, marks, got, inner))
        swapped, other = lax.ppermute(wide, "cut", swap), lax.ppermute(wide, "cut", cross)
        force = call(pair_force_kernel, along_line, (), (wide, swapped))
        total = lax.all_to_all(force, both, 0, 0, tiled=True, axis_index_groups=lines)
        return (wide, swapped, other), inner, total

    def wide_rates(around, inner, first, last):
        out = shape(3, last - first, rows + 2, slots)
        read, summed = (last - first + 2) * (rows + 4), (last - first) * (rows + 2)
        return rates_of(functools.partial(wide_rates_kernel, range(first, last)), out, (*around, inner), read, summed)

    inputs = (positions, velocity, density, counts, contact_mask, destination[None], tool[None])
    own, marks, route, sent = pl.pallas_call(
        functools.partial(start_kernel, near),
        out_shape=[state, marking, jax.ShapeDtypeStruct((16, slots), jnp.int32), message],
        in_specs=[pl.BlockSpec(memory_space=pl.ANY)] * 7,
        out_specs=[VMEM] * 4,
        scratch_shapes=[pltpu.VMEM(part.shape, part.dtype) for part in inputs[3:]] + [pltpu.SemaphoreType.DMA((7,))],
        compiler_params=pltpu.CompilerParams(vmem_limit_bytes=60 * 1024 * 1024),
    )(*inputs)
    around, inner, total = exchange(own, marks, sent)
    found = wide_rates(around, inner, 1, 3 * cols - 1)
    rest = (pltpu.VMEM(ring.shape, F32),)
    read, summed = (cols + 2) * (rows + 2), cols * rows
    own, found = rates_of(first_update_kernel, [state, block_rates], (own, found, marks, *around), read, summed, rest)

    kernel = functools.partial(second_update_kernel, scale)
    own, tool, sent = call(kernel, [state, vector, message], (), (own, found, marks, total))

    around, inner, total = exchange(own, marks, sent)
    kernel = functools.partial(next_force_kernel, scale)
    tool, force = call(kernel, [vector, along_plane], (), (own, marks, tool, total))
    got = lax.all_to_all(force, both, 0, 0, tiled=True, axis_index_groups=planes)
    middle = 3 * cols // 2
    first_found = wide_rates(around, inner, 1, middle)
    force = call(spread_kernel, along_line, (), (got, first_found))
    total = lax.all_to_all(force, both, 0, 0, tiled=True, axis_index_groups=lines)
    last_found = wide_rates(around, inner, middle, 3 * cols - 1)
    own, ringed = call(third_update_kernel, [state, ring], (), (own, first_found, last_found, marks, *around, tool))
    found = rates_of(rates_kernel, block_rates, (ringed,), (cols + 2) * (rows + 2), cols * rows)
    kernel = functools.partial(next_force_kernel, scale)
    tool, force = call(kernel, [vector, along_depth], (), (own, marks, tool, total))
    total = lax.all_to_all(force, "depth", 0, 0, tiled=True)
    kernel = functools.partial(last_kernel, near)
    sent = call(kernel, shape(near, size + 8, slots), (), (route, own, found, marks, tool, total))
    close = [[g * near + k for k in range(near)] for g in range(far)]
    apart = [[g * near + k for g in range(far)] for k in range(near)]
    got = lax.all_to_all(sent, "cut", 0, 0, tiled=True, axis_index_groups=close)
    sent = call(functools.partial(sort_kernel, near, size), shape(far, size + 8, slots), (), (route, got))
    got = lax.all_to_all(sent, "cut", 0, 0, tiled=True, axis_index_groups=apart)
    moved, tool = call(functools.partial(take_kernel, near, scale), [state, shape(1, 2)], (), (route, got, tool))
    return moved, tool[0]


def solution(mesh):
    return jax.shard_map(
        body,
        mesh=mesh,
        in_specs=(
            P(None, "cut", "depth", None),
            P(None, "cut", "depth", None),
            P("cut", "depth", None),
            P("cut", "depth"),
            P("cut", "depth"),
            P(),
            P(),
        ),
        out_specs=(P(None, "cut", "depth", None), P()),
        check_vma=False,
    )
```

```python
import functools

import jax
import jax.numpy as jnp
from jax import lax
from jax.experimental import pallas as pl
from jax.experimental.pallas import tpu as pltpu
from jax.sharding import PartitionSpec as P

HALO = 2
MASS = 0.02
SOUND = 20.0
VISCOSITY = 2.0
STIFF = 50.0
DT = 0.05

FAR = 1.0e6

ROWS = 32

COST = 20_000_000_000

F32 = jnp.float32
BF16 = jnp.bfloat16
PARAMS = pltpu.CompilerParams(vmem_limit_bytes=40 * 1024 * 1024)
VMEM = pl.BlockSpec(memory_space=pltpu.VMEM)
SMEM = pl.BlockSpec(memory_space=pltpu.SMEM)


def here():
    return lax.axis_index("cut")


def row_block():
    return lax.axis_index("depth")


def shape(*dims):
    return jax.ShapeDtypeStruct(dims, F32)


def call(kernel, outs, scalars, arrays, scratch=(), estimate=0):
    return pl.pallas_call(
        kernel,
        out_shape=outs,
        in_specs=[SMEM] * len(scalars) + [VMEM] * len(arrays),
        out_specs=[VMEM] * len(outs) if isinstance(outs, list) else VMEM,
        scratch_shapes=scratch,
        compiler_params=PARAMS,
        cost_estimate=pl.CostEstimate(flops=estimate, bytes_accessed=1 << 20, transcendentals=0) if estimate else None,
    )(*scalars, *arrays)


def pressure(s):
    inv = 1.0 / s
    return SOUND * (s - 1.0) * inv * inv, inv


def penalties(x, touch, live, offset, column):
    return touch * live * jnp.maximum(0.0, x - column + offset - 0.5)


def own_force(new, marks, offset, first):
    total = 0.0
    for c, fields in enumerate(new):
        total = total + STIFF * penalties(fields[0], marks[1, c], marks[0, c], offset, first + c)
    total = jnp.sum(total, axis=0, keepdims=True)
    return jnp.broadcast_to(jnp.sum(total, axis=1, keepdims=True), total.shape)


def visible(fields, live, touch):
    alive = live > 0
    x, y, u, v, rho = fields
    return [jnp.where(alive, x, FAR), y, u, v, jnp.where(alive, rho, 1.0), live * touch]


def fill_depth(state, marks, force, sent):
    depth, ndepth = row_block(), sent.shape[0]
    cols, rows = marks.shape[1:3]
    row = 5 * cols * HALO
    sent[...] = jnp.zeros(sent.shape, F32)
    sent[:, row : row + 1, :] = jnp.broadcast_to(force[None], (ndepth, 1, force.shape[1]))
    seen = [visible(state[c], marks[0, c], marks[1, c]) for c in range(cols)]
    slot = lax.broadcasted_iota(jnp.int32, force.shape, 1)

    def put(target, rim):
        last = force
        for c in range(cols):
            for f in range(5):
                at = (f * cols + c) * HALO
                sent[target, at : at + HALO] = seen[c][f][rim : rim + HALO]
            for k in range(HALO):
                last = jnp.where(slot == 1 + c * HALO + k, marks[1, c][rim + k : rim + k + 1], last)
        sent[target, row : row + 1] = last

    @pl.when(depth > 0)
    def _():
        put(depth - 1, 0)

    @pl.when(depth < ndepth - 1)
    def _():
        put(depth + 1, rows - HALO)


def origin(cols, rows):
    first = (here() * cols).astype(F32)
    return first + 0.5 * cols, (row_block() * rows).astype(F32) + 0.5 * rows, first


def start_kernel(near, *refs):
    inputs, (own, marks, route, sent), (counts, contact, target, first_tool, arrived) = refs[:7], refs[7:11], refs[11:]
    homes = [own.at[0:2], own.at[2:4], own.at[4], counts, contact, target, first_tool]
    copies = [pltpu.make_async_copy(part, to, arrived.at[n]) for n, (part, to) in enumerate(zip(inputs, homes))]
    for copy in copies:
        copy.start()
    for copy in copies:
        copy.wait()
    cols, rows, slots = own.shape[1:]
    row = lax.broadcasted_iota(jnp.int32, (rows, slots), 0)
    slot = lax.broadcasted_iota(jnp.int32, (rows, slots), 1)
    for c in range(cols):
        filled = jnp.zeros((rows, slots), jnp.int32)
        touch = jnp.zeros((rows, slots), jnp.int32)
        for r in range(rows):
            filled = jnp.where(row == r, counts[c : c + 1, r : r + 1], filled)
            touch = jnp.where(row == r, contact[c : c + 1, r : r + 1], touch)
        marks[0, c] = jnp.where(slot < filled, 1.0, 0.0)
        marks[1, c] = touch.astype(F32)
    new = [[own[f, c] for f in range(5)] for c in range(cols)]
    offset = jnp.broadcast_to(first_tool[0:1, 0:1], (1, slots))
    marks[2, 0] = jnp.broadcast_to(offset, (rows, slots))
    marks[2, 1] = jnp.broadcast_to(first_tool[0:1, 1:2], (rows, slots))
    fill_depth(new, marks, own_force(new, marks, offset, origin(cols, rows)[2]), sent)

    block = lax.broadcasted_iota(jnp.int32, target.shape, 1)

    def entry(at):
        return jnp.sum(jnp.where(block == at, target[...], 0), axis=1, keepdims=True)

    route[...] = jnp.zeros(route.shape, jnp.int32)
    route[0:1] = jnp.broadcast_to(entry(here()), (1, slots))
    source = jnp.sum(jnp.where(target[...] == here(), block, 0), axis=1, keepdims=True)
    route[1:2] = jnp.broadcast_to(source, (1, slots))
    group = lax.div(here(), near)
    for k in range(near):
        route[2 + k : 3 + k] = jnp.broadcast_to(entry(group * near + k), (1, slots))


def extend_kernel(own, marks, got, inner, wide):
    depth, ndepth = row_block(), got.shape[0]
    cols, rows = own.shape[1:3]
    above = got[jnp.maximum(depth - 1, 0)]
    below = got[jnp.minimum(depth + 1, ndepth - 1)]
    blank = [FAR, 0.0, 0.0, 0.0, 1.0, 0.0]
    row = 5 * cols * HALO
    for c in range(cols):
        seen = visible([own[f, c] for f in range(5)], marks[0, c], marks[1, c])
        for f in range(6):
            at = (f * cols + c) * HALO
            wide[f * cols + c, HALO : rows + HALO] = seen[f]
            if f < 5:
                wide[f * cols + c, 0:HALO] = jnp.where(depth > 0, above[at : at + HALO], blank[f])
                wide[f * cols + c, rows + HALO :] = jnp.where(depth < ndepth - 1, below[at : at + HALO], blank[f])
        for rim, start in ((above, 0), (below, rows + HALO)):
            for k in range(HALO):
                at, lane = start + k, 1 + c * HALO + k
                live = jnp.where(wide[c, at : at + 1] < 0.5 * FAR, 1.0, 0.0)
                wide[5 * cols + c, at : at + 1] = live * rim[row : row + 1, lane : lane + 1]
    total = jnp.sum(got[:, row : row + 1, :], axis=0)[:, 0:1]
    wide[6 * cols] = jnp.broadcast_to(total, wide.shape[1:])


def pair_force_kernel(wide, swapped, force):
    last = wide.shape[0] - 1
    force[...] = jnp.broadcast_to((wide[last, 0:1] + swapped[last, 0:1])[None], force.shape)


def spread_kernel(got, before, force):
    force[...] = jnp.broadcast_to(jnp.sum(got[...], axis=0, keepdims=True), force.shape)


def pair_sums(columns, center, pairs, out, feat, acc2, acc3, earlier={}):
    x0, y0, _ = center
    tall, slots = columns[0][0].shape
    row0 = min(r for _, r in pairs)
    rows = 1 + max(r for _, r in pairs) - row0
    for c, (x, y, u, v, s) in enumerate(columns):
        lx, ly = x - x0, y - y0
        press, inv = pressure(s)
        parts = [jnp.ones_like(x), lx, ly, press, press * lx, press * ly, u, v, u * lx + v * ly, inv, inv * u, inv * v]
        highs = [part.astype(BF16).astype(F32) for part in parts]
        lows = [part - high for part, high in zip(parts, highs)]
        for k, part in enumerate(highs + lows + [jnp.zeros_like(x)] * (ROWS - 24)):
            feat[pl.ds(c * tall * ROWS + k, tall, stride=ROWS), :] = part
    for i, ((c, r), around) in enumerate(pairs.items()):
        xi, yi = [jnp.broadcast_to(f[r : r + 1], (slots, slots)).T for f in columns[c][:2]]

        def weights(a, b):
            dx = xi - columns[a][0][b : b + 1]
            dy = yi - columns[a][1][b : b + 1]
            q = jnp.maximum(BF16(0.0), (1.0 - dx * dx - dy * dy).astype(BF16))
            q2 = q * q
            return jnp.concatenate([q2, q2 * q], axis=0)

        total = None
        for n in range(0, len(around), 2):
            pair = around[n : n + 2]
            w = jnp.concatenate([weights(a, b) for a, b in pair], axis=1)
            f = jnp.concatenate([feat[pl.ds((a * tall + b) * ROWS, ROWS), :] for a, b in pair], axis=1).astype(BF16)
            found = lax.dot_general(f, w, (((1,), (1,)), ((), ())), preferred_element_type=F32)
            total = found if total is None else total + found
        acc2[i * ROWS : (i + 1) * ROWS] = total[:, :slots]
        acc3[i * ROWS : (i + 1) * ROWS] = total[:, slots:]

    for n, c in enumerate(sorted({c for c, _ in pairs})):

        def summed(k):
            acc = acc2 if k < 9 else acc3
            return sum(acc[pl.ds(n * rows * ROWS + k + low, rows, stride=ROWS), :] for low in (0, 12))

        x, y, u, v, s = [f[row0 : row0 + rows] for f in columns[c]]
        x, y = x - x0, y - y0
        press, _ = pressure(s)
        a0, ax, ay, ap, apx, apy, au, av, aw, b0, bu, bv = [summed(k) for k in range(12)]
        sx, sy = x * a0 - ax, y * a0 - ay
        rates = [
            (6.0 * MASS) * (press * sx + x * ap - apx) - (VISCOSITY * MASS) * (u * b0 - bu),
            (6.0 * MASS) * (press * sy + y * ap - apy) - (VISCOSITY * MASS) * (v * b0 - bv),
            (-6.0 * MASS) * (u * sx + v * sy - x * au - y * av + aw),
        ]
        for f in range(3):
            out[f, n] = rates[f]
            if c in earlier:
                out[f, n, 1 : rows - 1] = rates[f][1 : rows - 1] + earlier[c][f]


def around_cell(c, r):
    return [(c + a, r + b) for a in (-1, 0, 1) for b in (-1, 0, 1)]


def inner_rates_kernel(size, own, marks, out, feat, acc2, acc3):
    cols, rows = size
    columns = [visible([own[f, c] for f in range(5)], marks[0, c], marks[1, c])[:5] for c in range(cols)]
    cells = [(c, r) for c in range(cols) for r in range(rows)]
    pairs = {cell: [j for j in around_cell(*cell) if j in cells] for cell in cells}
    pair_sums(columns, origin(*size), pairs, out, feat, acc2, acc3)


def wide_columns(cols, wide, swapped, other):
    even = lax.rem(here(), 2) == 0
    blank = [FAR, 0.0, 0.0, 0.0, 1.0, 0.0]
    columns = []
    for side in range(3):
        outside = here() == (0 if side == 0 else lax.axis_size("cut") - 1)
        for c in range(cols):
            if side == 1:
                fields = [wide[f * cols + c] for f in range(6)]
            else:
                first, second = (other, swapped) if side == 0 else (swapped, other)
                fields = [jnp.where(outside, blank[f], jnp.where(even, first[f * cols + c], second[f * cols + c])) for f in range(6)]
            columns.append(fields)
    return columns


def wide_rates_kernel(wanted, size, wide, swapped, other, inner, out, feat, acc2, acc3):
    cols, rows = size
    start, stop = wanted[0] - 1, wanted[-1] + 2
    columns = [fields[:5] for fields in wide_columns(cols, wide, swapped, other)[start:stop]]
    block = [(c + cols, r + HALO) for c in range(cols) for r in range(rows)]
    pairs = {}
    for c in wanted:
        for r in range(1, rows + 3):
            around = [j for j in around_cell(c, r) if (c, r) not in block or j not in block]
            pairs[c - start, r] = [(a - start, b) for a, b in around]
    earlier = {c + cols - start: [inner[f, c] for f in range(3)] for c in range(cols)}
    pair_sums(columns, origin(*size), pairs, out, feat, acc2, acc3, earlier)


def rates_kernel(size, ring, out, feat, acc2, acc3):
    cols, rows = size
    columns = [[ring[f, c] for f in range(5)] for c in range(cols + 2)]
    pairs = {(c, r): around_cell(c, r) for c in range(1, cols + 1) for r in range(1, rows + 1)}
    pair_sums(columns, origin(*size), pairs, out, feat, acc2, acc3)


def by_column(*found):
    return [[part[f, n] for f in range(3)] for part in found for n in range(part.shape[1])]


def moved_ring(columns, found, offset, first, ring):
    for n in range(ring.shape[1]):
        x, y, u, v, s, touch = [f[1:-1] for f in columns[n + 1]]
        live = jnp.where(x < 0.5 * FAR, 1.0, 0.0)
        pen = touch * jnp.maximum(0.0, x - (first + (n - 1)) + offset - 0.5)
        u = u + DT * live * (found[n][0] - STIFF * pen)
        v = v + DT * live * found[n][1]
        ring[0, n] = x + DT * live * u
        ring[1, n] = y + DT * live * v
        ring[2, n] = u
        ring[3, n] = v
        ring[4, n] = s + DT * live * found[n][2]


def moved_state(own, found, marks, offset, first):
    cols, rows = own.shape[1:3]
    side, rim = (len(found) - cols) // 2, (found[0][0].shape[0] - rows) // 2
    new = []
    for c in range(cols):
        live = marks[0, c]
        ax, ay, drho = [part[rim : rim + rows] for part in found[c + side]]
        pen = penalties(own[0, c], marks[1, c], live, offset, first + c)
        u = own[2, c] + DT * live * (ax - STIFF * pen)
        v = own[3, c] + DT * live * ay
        x = own[0, c] + DT * live * u
        y = own[1, c] + DT * live * v
        rho = own[4, c] + DT * live * drho
        new.append([x, y, u, v, rho])
    return new


def keep(new, own):
    for c, fields in enumerate(new):
        for f in range(5):
            own[f, c] = fields[f]


def tool_step(offset, speed, force, scale):
    speed = speed + DT * (1.0 - force * scale)
    return offset + DT * speed, speed


def first_update_kernel(size, own, found, marks, wide, swapped, other, new_own, out, feat, acc2, acc3, ring):
    first = origin(*size)[2]
    offset = marks[2, 0, 0:1]
    found = by_column(found)
    keep(moved_state(own, found, marks, offset, first), new_own)
    moved_ring(wide_columns(size[0], wide, swapped, other), found, offset, first, ring)
    rates_kernel(size, ring, out, feat, acc2, acc3)


def second_update_kernel(scale, own, found, marks, total, new_own, new_tool, sent):
    first = origin(*own.shape[1:3])[2]
    offset, speed = tool_step(marks[2, 0, 0:1], marks[2, 1, 0:1], jnp.sum(total[...], axis=0), scale)
    new_tool[0:1] = offset
    new_tool[1:2] = speed
    state = [[own[f, c] for f in range(5)] for c in range(own.shape[1])]
    new = moved_state(own, by_column(found), marks, offset, first)
    keep(new, new_own)
    fill_depth(new, marks, own_force(state, marks, offset, first), sent)


def third_update_kernel(own, first_found, last_found, marks, wide, swapped, other, tool, new_own, ring):
    first = origin(*own.shape[1:3])[2]
    found = by_column(first_found, last_found)
    keep(moved_state(own, found, marks, tool[0:1], first), new_own)
    moved_ring(wide_columns(own.shape[1], wide, swapped, other), found, tool[0:1], first, ring)


def next_force_kernel(scale, own, marks, tool, total, new_tool, force):
    offset, speed = tool_step(tool[0:1], tool[1:2], jnp.sum(total[...], axis=0), scale)
    new_tool[0:1] = offset
    new_tool[1:2] = speed
    state = [[own[f, c] for f in range(5)] for c in range(own.shape[1])]
    part = own_force(state, marks, offset, origin(*own.shape[1:3])[2])
    force[...] = jnp.broadcast_to(part[None], force.shape)


def last_kernel(near, route, own, found, marks, tool, total, sent):
    cols, rows, slots = own.shape[1:]
    size = 5 * cols * rows
    new = moved_state(own, by_column(found), marks, tool[0:1], origin(cols, rows)[2])
    sent[:, size:, :] = jnp.broadcast_to(jnp.sum(total[...], axis=0, keepdims=True), (near, sent.shape[1] - size, slots))
    target = route[0:1]
    for k in range(near):
        chosen = jnp.bitwise_and(target, near - 1) == k
        for f in range(5):
            for c in range(cols):
                at = (f * cols + c) * rows
                sent[k, at : at + rows] = jnp.where(chosen, new[c][f], 0.0)


def sort_kernel(near, size, route, got, sent):
    far, most, slots = sent.shape
    digit = lax.rem(here(), near)
    total = jnp.sum(got[:, size : size + 1, :], axis=0, keepdims=True)
    sent[:, size:, :] = jnp.broadcast_to(total, (far, most - size, slots))
    for g in range(far):
        block = jnp.zeros((size, slots), F32)
        for k in range(near):
            block = jnp.where(route[2 + k : 3 + k] == g * near + digit, got[k, 0:size], block)
        sent[g, 0:size] = block


def take_kernel(near, scale, route, got, tool, out, new_tool):
    cols, rows, slots = out.shape[1:]
    size = 5 * cols * rows
    source = route[1:2]
    for f in range(5):
        for c in range(cols):
            at = (f * cols + c) * rows
            field = got[0, at : at + rows]
            for g in range(1, got.shape[0]):
                field = jnp.where(source >= g * near, got[g, at : at + rows], field)
            out[f, c] = field
    offset, speed = tool_step(tool[0:1], tool[1:2], jnp.sum(got[:, size : size + 1, :], axis=0), scale)
    slot = lax.broadcasted_iota(jnp.int32, (1, slots), 1)
    new_tool[...] = jnp.where(slot == 0, offset, speed)[:, 0:2]


def body(positions, velocity, density, counts, contact_mask, destination, tool):
    cols, rows, slots = density.shape
    ncut, ndepth = lax.axis_size("cut"), lax.axis_size("depth")
    scale = 1.0 / (ncut * cols * ndepth * rows * slots)
    near = 8 if ncut % 8 == 0 else 1
    far = ncut // near
    size = 5 * cols * rows
    state, marking = shape(5, cols, rows, slots), shape(3, cols, rows, slots)
    message, vector = shape(ndepth, 24, slots), shape(2, slots)
    along_depth, along_plane, along_line = [shape(n, 1, slots) for n in (ndepth, 2 * ndepth, ncut // 2)]
    both = ("cut", "depth")
    pairs = range(0, ncut, 2)
    planes = [[(c + k) * ndepth + d for k in range(2) for d in range(ndepth)] for c in pairs]
    lines = [[(c + k) * ndepth + d for c in pairs] for k in range(2) for d in range(ndepth)]
    ring = shape(5, cols + 2, rows + 2, slots)
    block_rates = shape(3, cols, rows, slots)
    swap = [(i, i ^ 1) for i in range(ncut)]
    cross = [(i, i + 1 if i % 2 else i - 1) for i in range(1, ncut - 1)]

    def rates_of(kernel, out, arrays, read, summed, rest=()):
        scratch = [pltpu.VMEM((n * ROWS, slots), F32) for n in (read, summed, summed)] + list(rest)
        return call(lambda *refs: kernel((cols, rows), *refs), out, (), arrays, scratch, COST)

    def exchange(own, marks, sent):
        got = lax.all_to_all(sent, "depth", 0, 0, tiled=True)
        inner = rates_of(inner_rates_kernel, block_rates, (own, marks), cols * rows, cols * rows)
        wide = call(extend_kernel, shape(6 * cols + 1, rows + 2 * HALO, slots), (), (own, marks, got, inner))
        swapped, other = lax.ppermute(wide, "cut", swap), lax.ppermute(wide, "cut", cross)
        force = call(pair_force_kernel, along_line, (), (wide, swapped))
        total = lax.all_to_all(force, both, 0, 0, tiled=True, axis_index_groups=lines)
        return (wide, swapped, other), inner, total

    def wide_rates(around, inner, first, last):
        out = shape(3, last - first, rows + 2, slots)
        read, summed = (last - first + 2) * (rows + 4), (last - first) * (rows + 2)
        return rates_of(functools.partial(wide_rates_kernel, range(first, last)), out, (*around, inner), read, summed)

    inputs = (positions, velocity, density, counts, contact_mask, destination[None], tool[None])
    own, marks, route, sent = pl.pallas_call(
        functools.partial(start_kernel, near),
        out_shape=[state, marking, jax.ShapeDtypeStruct((16, slots), jnp.int32), message],
        in_specs=[pl.BlockSpec(memory_space=pl.ANY)] * 7,
        out_specs=[VMEM] * 4,
        scratch_shapes=[pltpu.VMEM(part.shape, part.dtype) for part in inputs[3:]] + [pltpu.SemaphoreType.DMA((7,))],
        compiler_params=pltpu.CompilerParams(vmem_limit_bytes=60 * 1024 * 1024),
    )(*inputs)
    around, inner, total = exchange(own, marks, sent)
    found = wide_rates(around, inner, 1, 3 * cols - 1)
    rest = (pltpu.VMEM(ring.shape, F32),)
    read, summed = (cols + 2) * (rows + 2), cols * rows
    own, found = rates_of(first_update_kernel, [state, block_rates], (own, found, marks, *around), read, summed, rest)

    kernel = functools.partial(second_update_kernel, scale)
    own, tool, sent = call(kernel, [state, vector, message], (), (own, found, marks, total))

    around, inner, total = exchange(own, marks, sent)
    kernel = functools.partial(next_force_kernel, scale)
    tool, force = call(kernel, [vector, along_plane], (), (own, marks, tool, total))
    got = lax.all_to_all(force, both, 0, 0, tiled=True, axis_index_groups=planes)
    middle = 3 * cols // 2
    first_found = wide_rates(around, inner, 1, middle)
    force = call(spread_kernel, along_line, (), (got, first_found))
    total = lax.all_to_all(force, both, 0, 0, tiled=True, axis_index_groups=lines)
    last_found = wide_rates(around, inner, middle, 3 * cols - 1)
    own, ringed = call(third_update_kernel, [state, ring], (), (own, first_found, last_found, marks, *around, tool))
    found = rates_of(rates_kernel, block_rates, (ringed,), (cols + 2) * (rows + 2), cols * rows)
    kernel = functools.partial(next_force_kernel, scale)
    tool, force = call(kernel, [vector, along_depth], (), (own, marks, tool, total))
    total = lax.all_to_all(force, "depth", 0, 0, tiled=True)
    kernel = functools.partial(last_kernel, near)
    sent = call(kernel, shape(near, size + 8, slots), (), (route, own, found, marks, tool, total))
    close = [[g * near + k for k in range(near)] for g in range(far)]
    apart = [[g * near + k for g in range(far)] for k in range(near)]
    got = lax.all_to_all(sent, "cut", 0, 0, tiled=True, axis_index_groups=close)
    sent = call(functools.partial(sort_kernel, near, size), shape(far, size + 8, slots), (), (route, got))
    got = lax.all_to_all(sent, "cut", 0, 0, tiled=True, axis_index_groups=apart)
    moved, tool = call(functools.partial(take_kernel, near, scale), [state, shape(1, 2)], (), (route, got, tool))
    return moved, tool[0]


def solution(mesh):
    return jax.shard_map(
        body,
        mesh=mesh,
        in_specs=(
            P(None, "cut", "depth", None),
            P(None, "cut", "depth", None),
            P("cut", "depth", None),
            P("cut", "depth"),
            P("cut", "depth"),
            P(),
            P(),
        ),
        out_specs=(P(None, "cut", "depth", None), P()),
        check_vma=False,
    )
```
